128 devices in a mesh: row: 8 (over x, core), col: 16 (over y, z).
Axes of the slice: x: 4, y: 4, z: 4, core: 2. Of those that a mesh axis runs over, the one named last changes fastest.
Arguments:
- points: bfloat16 [131072, 256], P(('row', 'col')), may hold values from -6 to 6
- feature_scale: float32 [256], replicated, may hold values from 0.02 to 0.25
- tile_tasks: int32 [8, 16, 8], P('row', 'col'), may hold values from 0 to 127, as said below
- task_count: int32 [8, 16], P('row', 'col'), may hold values from 1 to 8, as said below
- seed_ids: int32 [64], replicated, may hold values from 0 to 131071, as said below
Outputs:
- embedding: float32 [131072, 64], P(('row', 'col'))
The draws below stay inside these ranges and needn't reach their ends.
Inputs may be any that keep to these rules, and one draw needn't show every extreme that they name: `tile_tasks`: entries at slots below task_count of a device name devices other than itself (row-major over row, col); entries from task_count on are ignored. Over all devices, each device is named by at most 8 listed entries, and some device by exactly 8. Entries may repeat. `task_count`: some device lists exactly 8 tasks. `seed_ids`: the 64 seeds are distinct.
All inputs are finite; a program needn't handle non-finite values.
Results may differ from the reference program's by a relative error of at most 0.035.
Values may be sent and summed in bfloat16 or wider, within the bound.
No kernel may reach another device: no remote copies, remote signals or barrier semaphores. Data moves between devices by JAX's collectives and lax.ppermute only.
A program may use at most 128 MiB of HBM per device.

```python
import math
import jax
import jax.numpy as jnp
from jax import lax

DIM = 256
NVEC = 64
BLOCK = 1024
ITERS = 2
MOST = 8
NPTS = 131072
N_ROW = 8
N_COL = 16


def task_table(key):
    key_low, key_crowd, key_maps, key_target = jax.random.split(key, 4)
    blocks_all = N_ROW * N_COL
    lower = jax.random.randint(key_low, (blocks_all,), 1, max(MOST // 3, 1) + 1)
    crowded = jax.random.randint(key_crowd, (blocks_all,), 0, 8) == 0
    counts = jnp.where(crowded, MOST, lower)
    target = jax.random.randint(key_target, (), 0, blocks_all)

    def one_map(subkey):
        key_order, key_shift = jax.random.split(subkey)
        order = jax.random.permutation(key_order, blocks_all)
        inverse = jnp.argsort(order)
        offset = jax.random.randint(key_shift, (), 1, blocks_all)
        mapped = order[(inverse + offset) % blocks_all]
        source = order[(inverse[target] - offset) % blocks_all]
        return (mapped, source)
    maps, sources = jax.vmap(one_map)(jax.random.split(key_maps, MOST))
    counts = counts.at[sources].set(MOST)
    return (counts.astype(jnp.int32), maps.T.astype(jnp.int32))


def draw_tile_tasks(key, part):
    counts, maps = task_table(key)
    return maps.reshape(N_ROW, N_COL, MOST)


def draw_task_count(key, part):
    counts, maps = task_table(key)
    return counts.reshape(N_ROW, N_COL)


def draw_seed_ids(key, part):
    key = jax.random.fold_in(key, 7)
    return jax.random.permutation(key, NPTS)[:NVEC].astype(jnp.int32)


def block_scale(key, extent, shards, low, high):
    def one(axis_at, shards_of):
        steps = jax.random.uniform(jax.random.fold_in(jax.random.fold_in(key, 6), axis_at), (shards_of,), jnp.float32, low / len(shards), high / len(shards))
        return jnp.repeat(jnp.exp(steps), extent[axis_at] // shards_of).reshape((-1,) + (1,) * (len(extent) - axis_at - 1))

    factor_of = one(*shards[0])
    for cut in shards[1:]:
        factor_of = factor_of * one(*cut)
    return factor_of


def normal_values(stream_key, shape, scale, bound, cuts=(), kind=jnp.bfloat16):
    array = scale * jax.random.normal(stream_key, shape, jnp.float32)
    if cuts:
        array = array * block_scale(stream_key, shape, cuts, -0.22, 0.18)
    return jnp.clip(array, -bound, bound).astype(kind)


def setup_inputs(seed: int = 0) -> dict:
    splits = jax.random.split(jax.random.key(seed), 6)
    points = normal_values(splits[0], (NPTS, DIM), 1.0, 6.0, ((0, 128),))
    feature_scale = jnp.clip(jnp.exp(jax.random.uniform(splits[1], (DIM,), jnp.float32, math.log(0.02), math.log(0.25))), 0.02, 0.25)
    tile_tasks = draw_tile_tasks(jax.random.fold_in(splits[5], 71), 0)
    task_count = draw_task_count(jax.random.fold_in(splits[5], 71), 0)
    seed_ids = draw_seed_ids(jax.random.fold_in(splits[5], 71), 0)
    return dict(points=points, feature_scale=feature_scale, tile_tasks=tile_tasks, task_count=task_count, seed_ids=seed_ids)


def squares(rows):
    widened = rows.astype(jnp.float32)
    return lax.optimization_barrier(jnp.sum(widened * widened, axis=1))

def kernel_block(left_rows, right_rows):
    dot_terms = lax.dot_general(left_rows.astype(jnp.float32), right_rows.astype(jnp.float32), (((1,), (1,)), ((), ())), preferred_element_type=jnp.float32)
    return jnp.exp(-0.5 * (squares(left_rows)[:, None] + squares(right_rows)[None, :] - 2.0 * dot_terms))

def orthonormal(subspace):
    gram_total = lax.dot_general(subspace, subspace, (((0,), (0,)), ((), ())), precision=lax.Precision.HIGHEST)
    factor = jnp.linalg.cholesky(gram_total)
    return lax.linalg.triangular_solve(factor, subspace, left_side=False, lower=True, transpose_a=True)

def reference(points, feature_scale, tile_tasks, task_count, seed_ids):
    blocks_all = N_ROW * N_COL
    weighted = (points.astype(jnp.float32) * feature_scale[None, :]).astype(jnp.bfloat16)
    blocks = weighted.reshape(blocks_all, BLOCK, DIM)
    owners = jnp.arange(blocks_all, dtype=jnp.int32)
    partners = tile_tasks.reshape(blocks_all, MOST).astype(jnp.int32)
    in_list = (jnp.arange(MOST, dtype=jnp.int32)[None, :] < task_count.reshape(blocks_all, 1)).reshape(-1)
    first_block = ((owners // N_COL)[:, None] * N_COL + partners % N_COL).reshape(-1).astype(jnp.int32)
    second_block = (partners // N_COL * N_COL + (owners % N_COL)[:, None]).reshape(-1).astype(jnp.int32)

    def degree_task(degree, item):
        first_index, second_index, is_live = item

        def add_tile(current):
            tile_value = kernel_block(blocks[first_index], blocks[second_index])
            current = current.at[first_index].add(lax.optimization_barrier(jnp.sum(tile_value, axis=1)))
            return current.at[second_index].add(lax.optimization_barrier(jnp.sum(tile_value, axis=0)))
        return (lax.cond(is_live, add_tile, lambda current: current, degree), None)
    degree = lax.map(lambda rows: lax.optimization_barrier(jnp.sum(kernel_block(rows, rows), axis=1)), blocks)
    degree, unused = lax.scan(degree_task, degree, (first_block, second_block, in_list))
    inv_root = lax.rsqrt(degree)
    seed_rows = jnp.take(weighted, seed_ids.astype(jnp.int32), axis=0)
    subspace = orthonormal(kernel_block(weighted, seed_rows))
    for iteration in range(ITERS):
        spread = (subspace.reshape(blocks_all, BLOCK, NVEC) * inv_root[:, :, None]).astype(jnp.bfloat16)
        applied = lax.map(lambda pair: jnp.dot(kernel_block(pair[0], pair[0]).astype(jnp.bfloat16).astype(jnp.float32), pair[1].astype(jnp.float32), preferred_element_type=jnp.float32), (blocks, spread))

        def apply_task(current, item):
            first_index, second_index, is_live = item

            def add_tile(state):
                tile_value = kernel_block(blocks[first_index], blocks[second_index]).astype(jnp.bfloat16)
                state = state.at[first_index].add(jnp.dot(tile_value.astype(jnp.float32), spread[second_index].astype(jnp.float32), preferred_element_type=jnp.float32))
                mirrored = lax.dot_general(tile_value.astype(jnp.float32), spread[first_index].astype(jnp.float32), (((0,), (0,)), ((), ())), preferred_element_type=jnp.float32)
                return state.at[second_index].add(mirrored)
            return (lax.cond(is_live, add_tile, lambda state: state, current), None)
        applied, unused = lax.scan(apply_task, applied, (first_block, second_block, in_list))
        subspace = orthonormal((applied * inv_root[:, :, None]).reshape(NPTS, NVEC))
    scaled = subspace * jnp.sqrt(jnp.float32(NPTS))
    return scaled * lax.rsqrt(lax.optimization_barrier(jnp.mean(scaled * scaled, axis=1, keepdims=True)) + 1e-06)
```

```python
import functools
import math

import jax
import jax.numpy as jnp
from jax import lax
from jax.experimental import pallas as pl
from jax.experimental.pallas import tpu as pltpu
from jax.sharding import PartitionSpec as P

ITERS = 2
LOG2E = math.log2(math.e)
VMEM = 48 * 1024 * 1024
HIGH = lax.Precision.HIGHEST


def lane_sums(values):
    part = values[:, :128]
    for start in range(128, values.shape[1], 128):
        part = part + values[:, start : start + 128]
    return jnp.sum(part.T, axis=0, keepdims=True)


def half_squares(rows):
    wide = rows.astype(jnp.float32)
    return wide * wide * (0.5 * LOG2E)


def tile_chunk(left, right, right_half):
    dots = lax.dot_general(
        left, right, (((1,), (1,)), ((), ())), preferred_element_type=jnp.float32
    )
    left_half = jnp.sum(half_squares(left), axis=1, keepdims=True)
    return jnp.exp2(dots * LOG2E - left_half - right_half)


def form_kernel(chunk, first, second, live, left, right, tile, row_deg, col_deg):
    step = pl.program_id(0)

    @pl.when(step == 0)
    def clear():
        row_deg[...] = jnp.zeros_like(row_deg)
        col_deg[...] = jnp.zeros_like(col_deg)

    @pl.when(step < live[0])
    def work():
        rows = left.shape[1]
        right_rows = right[0]
        right_half = lane_sums(half_squares(right_rows))
        col_total = jnp.zeros((1, rows), jnp.float32)
        row_totals = []
        for start in range(0, rows, chunk):
            value = tile_chunk(left[0, start : start + chunk, :], right_rows, right_half)
            tile[0, start : start + chunk, :] = value.astype(jnp.bfloat16)
            col_total = col_total + jnp.sum(value, axis=0, keepdims=True)
            row_totals.append(lane_sums(value))
        row_slot = first[step]
        col_slot = second[step]
        row_deg[row_slot] = row_deg[row_slot] + jnp.concatenate(row_totals, axis=1)
        col_deg[col_slot] = col_deg[col_slot] + col_total


def form_tiles(first, second, live, row_band, col_band):
    col_devices, rows, depth = row_band.shape
    row_devices = col_band.shape[0]
    slots = first.shape[0]

    def last(step, live_ref):
        return jnp.minimum(step, live_ref[0] - 1)

    return pl.pallas_call(
        functools.partial(form_kernel, min(256, rows)),
        grid_spec=pltpu.PrefetchScalarGridSpec(
            num_scalar_prefetch=3,
            grid=(slots,),
            in_specs=[
                pl.BlockSpec((1, rows, depth), lambda s, f, g, n: (f[last(s, n)], 0, 0)),
                pl.BlockSpec((1, rows, depth), lambda s, f, g, n: (g[last(s, n)], 0, 0)),
            ],
            out_specs=[
                pl.BlockSpec((1, rows, rows), lambda s, f, g, n: (last(s, n), 0, 0)),
                pl.BlockSpec((col_devices, 1, rows), lambda s, f, g, n: (0, 0, 0)),
                pl.BlockSpec((row_devices, 1, rows), lambda s, f, g, n: (0, 0, 0)),
            ],
        ),
        out_shape=[
            jax.ShapeDtypeStruct((slots, rows, rows), jnp.bfloat16),
            jax.ShapeDtypeStruct((col_devices, 1, rows), jnp.float32),
            jax.ShapeDtypeStruct((row_devices, 1, rows), jnp.float32),
        ],
        compiler_params=pltpu.CompilerParams(vmem_limit_bytes=VMEM),
        name="form_tiles",
    )(first, second, live, row_band, col_band)


def diagonal_kernel(chunk, own, tile, degree):
    rows = own.shape[0]
    right_rows = own[...]
    right_half = lane_sums(half_squares(right_rows))
    total = jnp.zeros((1, rows), jnp.float32)
    for start in range(0, rows, chunk):
        value = tile_chunk(own[start : start + chunk, :], right_rows, right_half)
        tile[start : start + chunk, :] = value.astype(jnp.bfloat16)
        total = total + jnp.sum(value, axis=0, keepdims=True)
    degree[...] = total


def form_diagonal(own):
    rows = own.shape[0]
    return pl.pallas_call(
        functools.partial(diagonal_kernel, min(256, rows)),
        out_shape=[
            jax.ShapeDtypeStruct((rows, rows), jnp.bfloat16),
            jax.ShapeDtypeStruct((1, rows), jnp.float32),
        ],
        compiler_params=pltpu.CompilerParams(vmem_limit_bytes=VMEM),
        name="form_diagonal",
    )(own)


def apply_kernel(contract, source, target, live, tile, vectors, out, total):
    step = pl.program_id(0)

    @pl.when(step == 0)
    def clear():
        total[...] = jnp.zeros_like(total)

    @pl.when(step < live[0])
    def work():
        slot = target[step]
        total[slot] = total[slot] + lax.dot_general(
            vectors[0],
            tile[0],
            (((1,), (contract,)), ((), ())),
            preferred_element_type=jnp.float32,
        )

    @pl.when(step == pl.num_programs(0) - 1)
    def store():
        out[...] = total[...].astype(jnp.bfloat16)


def apply_tiles(contract, source, target, live, tiles, vectors, targets):
    slots, rows, unused = tiles.shape
    vecs = vectors.shape[1]

    def last(step, live_ref):
        return jnp.minimum(step, live_ref[0] - 1)

    return pl.pallas_call(
        functools.partial(apply_kernel, contract),
        grid_spec=pltpu.PrefetchScalarGridSpec(
            num_scalar_prefetch=3,
            grid=(slots,),
            in_specs=[
                pl.BlockSpec((1, rows, rows), lambda s, f, g, n: (last(s, n), 0, 0)),
                pl.BlockSpec((1, vecs, rows), lambda s, f, g, n: (f[last(s, n)], 0, 0)),
            ],
            out_specs=pl.BlockSpec((targets, vecs, rows), lambda s, f, g, n: (0, 0, 0)),
            scratch_shapes=[pltpu.VMEM((targets, vecs, rows), jnp.float32)],
        ),
        out_shape=jax.ShapeDtypeStruct((targets, vecs, rows), jnp.bfloat16),
        compiler_params=pltpu.CompilerParams(vmem_limit_bytes=VMEM),
        name="apply_tiles",
    )(source, target, live, tiles, vectors)


def spread_to(array, axis):
    devices = lax.axis_size(axis)
    copies = jnp.broadcast_to(array[None], (devices,) + array.shape)
    return lax.all_to_all(copies, axis, 0, 0, tiled=True)


def sum_over_mesh(array):
    return jnp.sum(spread_to(jnp.sum(spread_to(array, "row"), axis=0), "col"), axis=0)


def orthonormal(subspace):
    local_gram = lax.dot_general(subspace, subspace, (((1,), (1,)), ((), ())), precision=HIGH)
    factor = jnp.linalg.cholesky(sum_over_mesh(local_gram))
    return lax.linalg.triangular_solve(factor, subspace, left_side=True, lower=True)


def gather_row(own):
    devices = lax.axis_size("row")
    half = own.shape[0] // 2

    def shift(array, by):
        return lax.ppermute(array, "row", [(i, (i + by) % devices) for i in range(devices)])

    before = shift(own, 2)
    after = shift(own, -2)
    across = jnp.concatenate([shift(before[:half], 2), shift(after[half:], -2)], axis=0)
    mine = jnp.stack([own, before, after, across])
    other = lax.ppermute(mine, "row", [(i, i ^ 1) for i in range(devices)])
    return jnp.concatenate([mine, other], axis=0)


def place_in_row(index):
    here = lax.axis_index("row")
    apart = (index // 2 - here // 2) % 4
    order = jnp.where(apart == 0, 0, jnp.where(apart == 3, 1, jnp.where(apart == 1, 2, 3)))
    return order + 4 * ((index - here) % 2)


def shards(points, feature_scale, tile_tasks, task_count, seed_ids):
    rows = points.shape[0]
    row_devices = lax.axis_size("row")
    col_devices = lax.axis_size("col")
    all_devices = row_devices * col_devices
    self_index = lax.axis_index("row") * col_devices + lax.axis_index("col")
    weighted = (points.astype(jnp.float32) * feature_scale[None, :]).astype(jnp.bfloat16)
    row_band = lax.all_gather(weighted, "col", axis=0)
    col_band = gather_row(weighted)
    listed = tile_tasks.reshape(-1)
    live = task_count.reshape(1)
    used = jnp.where(jnp.arange(listed.shape[0]) < live, listed, 0)
    first = used % col_devices
    second = used // col_devices

    local_seed = seed_ids - self_index * rows
    inside = (local_seed >= 0) & (local_seed < rows)
    picked = jnp.where(
        inside[:, None], jnp.take(weighted, jnp.clip(local_seed, 0, rows - 1), axis=0), 0
    ).astype(jnp.bfloat16)
    seed_rows = sum_over_mesh(picked)

    diagonal, own_degree = form_diagonal(weighted)
    own_half = jnp.sum(half_squares(weighted), axis=1)
    seed_half = jnp.sum(half_squares(seed_rows), axis=1)
    seed_dots = lax.dot_general(
        seed_rows, weighted, (((1,), (1,)), ((), ())), preferred_element_type=jnp.float32
    )
    start = jnp.exp2(seed_dots * LOG2E - seed_half[:, None] - own_half[None, :])
    subspace = orthonormal(start)

    tiles, row_deg, col_deg = form_tiles(
        first, place_in_row(second), live, row_band, col_band
    )
    row_places = place_in_row(jnp.arange(row_devices))
    col_deg = jnp.take(col_deg, row_places, axis=0)
    degree = (
        own_degree
        + jnp.sum(lax.all_to_all(row_deg, "col", 0, 0, tiled=True), axis=0)
        + jnp.sum(lax.all_to_all(col_deg, "row", 0, 0, tiled=True), axis=0)
    )
    inv_root = lax.rsqrt(degree)
    for iteration in range(ITERS):
        spread = (subspace * inv_root).astype(jnp.bfloat16)
        col_vec = lax.all_gather(spread, "row", axis=0)
        row_vec = spread_to(spread, "col")
        own_part = lax.dot_general(
            spread, diagonal, (((1,), (0,)), ((), ())), preferred_element_type=jnp.float32
        )
        to_second = apply_tiles(0, first, second, live, tiles, row_vec, row_devices)
        second_part = lax.psum_scatter(to_second, "row", scatter_dimension=0, tiled=False)
        to_first = apply_tiles(1, second, first, live, tiles, col_vec, col_devices)
        first_parts = lax.all_to_all(to_first, "col", 0, 0, tiled=True)
        applied = (
            own_part
            + jnp.sum(first_parts.astype(jnp.float32), axis=0)
            + second_part.astype(jnp.float32)
        )
        subspace = orthonormal(applied * inv_root)
    scaled = subspace * jnp.sqrt(jnp.float32(all_devices * rows))
    result = scaled * lax.rsqrt(jnp.mean(scaled * scaled, axis=0, keepdims=True) + 1e-06)
    return result.T


def solution(mesh):
    return jax.shard_map(
        shards,
        mesh=mesh,
        in_specs=(P(("row", "col"), None), P(), P("row", "col", None), P("row", "col"), P()),
        out_specs=P(("row", "col"), None),
        check_vma=False,
    )
```

```python
import functools
import math

import jax
import jax.numpy as jnp
from jax import lax
from jax.experimental import pallas as pl
from jax.experimental.pallas import tpu as pltpu
from jax.sharding import PartitionSpec as P

ITERS = 2
LOG2E = math.log2(math.e)
VMEM = 48 * 1024 * 1024
HIGH = lax.Precision.HIGHEST
RIDGE = 1e-6


def lane_sums(values):
    part = values[:, :128]
    for start in range(128, values.shape[1], 128):
        part = part + values[:, start : start + 128]
    return jnp.sum(part.T, axis=0, keepdims=True)


def half_squares(rows):
    wide = rows.astype(jnp.float32)
    return wide * wide * (0.5 * LOG2E)


def tile_chunk(left, right, right_half):
    dots = lax.dot_general(
        left, right, (((1,), (1,)), ((), ())), preferred_element_type=jnp.float32
    )
    left_half = jnp.sum(half_squares(left), axis=1, keepdims=True)
    return jnp.exp2(dots * LOG2E - left_half - right_half)


def pack_row(row):
    return jnp.concatenate([row[:, i : i + 128] for i in range(0, row.shape[1], 128)], axis=0)


def unpack_row(block):
    return jnp.concatenate([block[i : i + 1, :] for i in range(block.shape[0])], axis=1)


def packed_gram(vectors):
    gram = lax.dot_general(
        vectors,
        vectors,
        (((1,), (1,)), ((), ())),
        precision=HIGH,
        preferred_element_type=jnp.float32,
    )
    half = gram.shape[0] // 2
    return jnp.concatenate([gram[:half], gram[half:]], axis=1)


def inverse_factor(packed, ridge):
    half, width = packed.shape
    size = 2 * half
    state = jnp.concatenate([packed, pltpu.roll(packed, size, 1)], axis=0)
    row_id = lax.broadcasted_iota(jnp.int32, state.shape, 0)
    lane_id = lax.broadcasted_iota(jnp.int32, state.shape, 1)
    state = jnp.where(lane_id < size, state, jnp.where(lane_id - size == row_id, 1.0, 0.0))
    if ridge:
        on_diagonal = lane_id == row_id
        trace = jnp.sum(jnp.where(on_diagonal, state, 0.0))
        state = jnp.where(on_diagonal, state + trace * (RIDGE / size), state)
    done = []
    for start in range(0, size, 8):
        columns = [
            jnp.broadcast_to(state[:, start + j : start + j + 1], state.shape) for j in range(8)
        ]
        row_id = lax.broadcasted_iota(jnp.int32, state.shape, 0)
        scale = jnp.zeros((8, width), jnp.float32)
        for j in range(8):
            column = columns[j]
            pivot = column[j : j + 1, :]
            scale = jnp.where(row_id[:8] == j, lax.rsqrt(pivot), scale)
            factor = jnp.where(row_id > j, column * (1.0 / pivot), 0.0)
            state = state - factor * state[j : j + 1, :]
            for m in range(j + 1, 8):
                columns[m] = columns[m] - factor * column[m : m + 1, :]
        done.append(state[:8] * scale)
        state = state[8:]
    full = jnp.concatenate(done, axis=0)
    return pltpu.roll(full, size, 1)[:, :size]


def transform(matrix, vectors):
    return jnp.dot(matrix, vectors, precision=HIGH, preferred_element_type=jnp.float32)


def call(kernel, name, out_shape):
    return pl.pallas_call(
        kernel,
        out_shape=out_shape,
        compiler_params=pltpu.CompilerParams(vmem_limit_bytes=VMEM),
        name=name,
    )


def f32(*shape):
    return jax.ShapeDtypeStruct(shape, jnp.float32)


def bf16(*shape):
    return jax.ShapeDtypeStruct(shape, jnp.bfloat16)


def seed_kernel_rows(seeds, block):
    dots = lax.dot_general(
        seeds, block, (((1,), (1,)), ((), ())), preferred_element_type=jnp.float32
    )
    seed_half = jnp.sum(half_squares(seeds), axis=1, keepdims=True)
    return jnp.exp2(dots * LOG2E - seed_half - lane_sums(half_squares(block)))


def start_kernel(seeds, own, start, grams):
    value = seed_kernel_rows(seeds[...], own[...])
    start[...] = value
    grams[...] = jnp.broadcast_to(packed_gram(value)[None], grams.shape)


def first_factor_kernel(grams, start, diagonal, own_degree, factor, subspace, later_gram):
    inverse = inverse_factor(jnp.sum(grams[...], axis=0), False)
    factor[...] = inverse
    value = transform(inverse, start[...])
    subspace[...] = value
    root = lax.rsqrt(own_degree[...])
    product = jnp.dot(
        (value * root).astype(jnp.bfloat16), diagonal[...], preferred_element_type=jnp.float32
    )
    later_gram[...] = packed_gram(product * root)


def later_factor_kernel(grams, factor):
    factor[...] = inverse_factor(jnp.sum(grams[...], axis=0), True)


def degree_kernel(own_degree, row_parts, col_parts, roots, root):
    total = jnp.sum(row_parts[...], axis=0) + jnp.sum(col_parts[...], axis=0)
    value = lax.rsqrt(total + pack_row(own_degree[...]))
    roots[...] = jnp.broadcast_to(value[None], roots.shape)
    root[...] = unpack_row(value)


def gathered(own_part, first_parts, second_part, root):
    total = own_part[...] + second_part[...].astype(jnp.float32)
    for index in range(first_parts.shape[0]):
        total = total + first_parts[index].astype(jnp.float32)
    return total * root[...]


def between_kernel(own_part, first_parts, second_part, root, factor, copies, spread):
    value = transform(factor[...], gathered(own_part, first_parts, second_part, root))
    value = (value * root[...]).astype(jnp.bfloat16)
    spread[...] = value
    copies[...] = jnp.broadcast_to(value[None], copies.shape)


def last_kernel(own_part, first_parts, second_part, root, subspace, grams):
    value = gathered(own_part, first_parts, second_part, root)
    subspace[...] = value
    grams[...] = jnp.broadcast_to(packed_gram(value)[None], grams.shape)


def final_kernel(points_all, grams, subspace, embedding):
    inverse = inverse_factor(jnp.sum(grams[...], axis=0), False)
    scaled = transform(inverse, subspace[...]) * math.sqrt(points_all)
    mean = jnp.mean(scaled * scaled, axis=0, keepdims=True)
    embedding[...] = (scaled * lax.rsqrt(mean + 1e-06)).T


def relay_kernel(grams, copies):
    copies[...] = jnp.broadcast_to(jnp.sum(grams[...], axis=0)[None], copies.shape)


def vectors_kernel(first, second, live, left, right, seeds, factor, from_first, from_second):
    @pl.when(pl.program_id(0) < live[0])
    def work():
        for block, out in ((left, from_first), (right, from_second)):
            out[0] = transform(factor[...], seed_kernel_rows(seeds[...], block[0]))


def start_vectors(first, second, live, row_band, col_band, seeds, factor):
    unused, rows, depth = row_band.shape
    slots = first.shape[0]
    vecs = seeds.shape[0]

    def last(step, live_ref):
        return jnp.minimum(step, live_ref[0] - 1)

    return pl.pallas_call(
        vectors_kernel,
        grid_spec=pltpu.PrefetchScalarGridSpec(
            num_scalar_prefetch=3,
            grid=(slots,),
            in_specs=[
                pl.BlockSpec((1, rows, depth), lambda s, f, g, n: (f[last(s, n)], 0, 0)),
                pl.BlockSpec((1, rows, depth), lambda s, f, g, n: (g[last(s, n)], 0, 0)),
                pl.BlockSpec((vecs, depth), lambda s, f, g, n: (0, 0)),
                pl.BlockSpec((vecs, vecs), lambda s, f, g, n: (0, 0)),
            ],
            out_specs=[
                pl.BlockSpec((1, vecs, rows), lambda s, f, g, n: (last(s, n), 0, 0))
            ] * 2,
        ),
        out_shape=[f32(slots, vecs, rows)] * 2,
        compiler_params=pltpu.CompilerParams(vmem_limit_bytes=VMEM),
        name="start_vectors",
    )(first, second, live, row_band, col_band, seeds, factor)


def form_kernel(chunk, first, second, live, left, right, tile, row_deg, col_deg):
    step = pl.program_id(0)

    @pl.when(step == 0)
    def clear():
        row_deg[...] = jnp.zeros_like(row_deg)
        col_deg[...] = jnp.zeros_like(col_deg)

    @pl.when(step < live[0])
    def work():
        rows = left.shape[1]
        right_rows = right[0]
        right_half = lane_sums(half_squares(right_rows))
        col_total = jnp.zeros((1, rows), jnp.float32)
        row_totals = []
        for start in range(0, rows, chunk):
            value = tile_chunk(left[0, start : start + chunk, :], right_rows, right_half)
            tile[0, start : start + chunk, :] = value.astype(jnp.bfloat16)
            col_total = col_total + jnp.sum(value, axis=0, keepdims=True)
            row_totals.append(lane_sums(value))
        row_slot = first[step]
        col_slot = second[step]
        row_total = jnp.concatenate(row_totals, axis=1)
        row_deg[row_slot] = row_deg[row_slot] + pack_row(row_total)
        col_deg[col_slot] = col_deg[col_slot] + pack_row(col_total)


def form_tiles(first, second, live, row_band, col_band):
    col_devices, rows, depth = row_band.shape
    row_devices = col_band.shape[0]
    slots = first.shape[0]

    def last(step, live_ref):
        return jnp.minimum(step, live_ref[0] - 1)

    return pl.pallas_call(
        functools.partial(form_kernel, min(256, rows)),
        grid_spec=pltpu.PrefetchScalarGridSpec(
            num_scalar_prefetch=3,
            grid=(slots,),
            in_specs=[
                pl.BlockSpec((1, rows, depth), lambda s, f, g, n: (f[last(s, n)], 0, 0)),
                pl.BlockSpec((1, rows, depth), lambda s, f, g, n: (g[last(s, n)], 0, 0)),
            ],
            out_specs=[
                pl.BlockSpec((1, rows, rows), lambda s, f, g, n: (last(s, n), 0, 0)),
                pl.BlockSpec((col_devices, rows // 128, 128), lambda s, f, g, n: (0, 0, 0)),
                pl.BlockSpec((row_devices, rows // 128, 128), lambda s, f, g, n: (0, 0, 0)),
            ],
        ),
        out_shape=[
            bf16(slots, rows, rows),
            f32(col_devices, rows // 128, 128),
            f32(row_devices, rows // 128, 128),
        ],
        compiler_params=pltpu.CompilerParams(vmem_limit_bytes=VMEM),
        name="form_tiles",
    )(first, second, live, row_band, col_band)


def diagonal_kernel(chunk, own, tile, degree):
    rows = own.shape[0]
    right_rows = own[...]
    right_half = lane_sums(half_squares(right_rows))
    total = jnp.zeros((1, rows), jnp.float32)
    for start in range(0, rows, chunk):
        value = tile_chunk(own[start : start + chunk, :], right_rows, right_half)
        tile[start : start + chunk, :] = value.astype(jnp.bfloat16)
        total = total + jnp.sum(value, axis=0, keepdims=True)
    degree[...] = total


def form_diagonal(own):
    rows = own.shape[0]
    return pl.pallas_call(
        functools.partial(diagonal_kernel, min(256, rows)),
        out_shape=[
            jax.ShapeDtypeStruct((rows, rows), jnp.bfloat16),
            jax.ShapeDtypeStruct((1, rows), jnp.float32),
        ],
        compiler_params=pltpu.CompilerParams(vmem_limit_bytes=VMEM),
        name="form_diagonal",
    )(own)


def apply_kernel(contract, source, target, live, tile, vectors, *rest):
    step = pl.program_id(0)
    roots, out, total = rest if len(rest) == 3 else (None,) + rest

    @pl.when(step == 0)
    def clear():
        total[...] = jnp.zeros_like(total)

    @pl.when(step < live[0])
    def work():
        slot = target[step]
        block = vectors[0]
        if roots is not None:
            block = (block * unpack_row(roots[0])).astype(jnp.bfloat16)
        total[slot] = total[slot] + lax.dot_general(
            block, tile[0], (((1,), (contract,)), ((), ())), preferred_element_type=jnp.float32
        )

    @pl.when(step == pl.num_programs(0) - 1)
    def store():
        out[...] = total[...].astype(jnp.bfloat16)


def apply_tiles(contract, source, target, live, tiles, vectors, roots, targets):
    slots, rows, unused = tiles.shape
    vecs = vectors.shape[1]

    def last(step, live_ref):
        return jnp.minimum(step, live_ref[0] - 1)

    def by_task(s, f, g, n):
        return (last(s, n), 0, 0)

    def by_block(s, f, g, n):
        return (f[last(s, n)], 0, 0)

    in_specs = [
        pl.BlockSpec((1, rows, rows), by_task),
        pl.BlockSpec((1, vecs, rows), by_block if roots is None else by_task),
    ]
    operands = [tiles, vectors]
    if roots is not None:
        in_specs.append(pl.BlockSpec((1, rows // 128, 128), by_block))
        operands.append(roots)
    return pl.pallas_call(
        functools.partial(apply_kernel, contract),
        grid_spec=pltpu.PrefetchScalarGridSpec(
            num_scalar_prefetch=3,
            grid=(slots,),
            in_specs=in_specs,
            out_specs=pl.BlockSpec((targets, vecs, rows), lambda s, f, g, n: (0, 0, 0)),
            scratch_shapes=[pltpu.VMEM((targets, vecs, rows), jnp.float32)],
        ),
        out_shape=bf16(targets, vecs, rows),
        compiler_params=pltpu.CompilerParams(vmem_limit_bytes=VMEM),
        name="apply_tiles",
    )(source, target, live, *operands)


def spread_to(array, axis):
    devices = lax.axis_size(axis)
    copies = jnp.broadcast_to(array[None], (devices,) + array.shape)
    return lax.all_to_all(copies, axis, 0, 0, tiled=True)


def exchange(copies, axis):
    return lax.all_to_all(copies, axis, 0, 0, tiled=True)


def together(*arrays):
    return lax.optimization_barrier(arrays)


def place_in_row(index):
    here = lax.axis_index("row")
    apart = (index // 2 - here // 2) % 4
    order = jnp.where(apart == 0, 0, jnp.where(apart == 3, 1, jnp.where(apart == 1, 2, 3)))
    return order + 4 * ((index - here) % 2)


def shards(points, feature_scale, tile_tasks, task_count, seed_ids):
    rows = points.shape[0]
    vecs = seed_ids.shape[0]
    row_devices = lax.axis_size("row")
    col_devices = lax.axis_size("col")
    all_devices = row_devices * col_devices
    self_index = lax.axis_index("row") * col_devices + lax.axis_index("col")
    weighted = (points.astype(jnp.float32) * feature_scale[None, :]).astype(jnp.bfloat16)
    row_band = lax.all_gather(weighted, "col", axis=0)
    listed = tile_tasks.reshape(-1)
    live = task_count.reshape(1)
    used = jnp.where(jnp.arange(listed.shape[0]) < live, listed, 0)
    first = used % col_devices
    second_device = used // col_devices
    second = place_in_row(second_device)

    def shift(array, by):
        return lax.ppermute(
            array, "row", [(i, (i + by) % row_devices) for i in range(row_devices)]
        )

    local_seed = seed_ids - self_index * rows
    inside = (local_seed >= 0) & (local_seed < rows)
    picked = jnp.where(
        inside[:, None], jnp.take(weighted, jnp.clip(local_seed, 0, rows - 1), axis=0), 0
    ).astype(jnp.bfloat16)
    seed_parts = spread_to(picked, "row")
    before = shift(weighted, 2)
    after = shift(weighted, -2)
    before, after, seed_parts = together(before, after, seed_parts)
    half = rows // 2
    across_low = shift(before[:half], 2)
    across_high = shift(after[half:], -2)
    seed_parts = spread_to(jnp.sum(seed_parts, axis=0), "col")
    across_low, across_high, seed_parts = together(across_low, across_high, seed_parts)
    seeds = jnp.sum(seed_parts, axis=0)
    across = jnp.concatenate([across_low, across_high], axis=0)
    mine = jnp.stack([weighted, before, after, across])
    other = lax.ppermute(mine, "row", [(i, i ^ 1) for i in range(row_devices)])

    start, grams = call(
        start_kernel, "start", [f32(vecs, rows), f32(row_devices, vecs // 2, 2 * vecs)]
    )(seeds, weighted)
    grams = exchange(grams, "row")
    col_band, grams = together(jnp.concatenate([mine, other], axis=0), grams)
    grams = call(relay_kernel, "relay", f32(col_devices, vecs // 2, 2 * vecs))(grams)
    grams = exchange(grams, "col")
    diagonal, own_degree = form_diagonal(weighted)
    factor, subspace, later_gram = call(
        first_factor_kernel,
        "first_factor",
        [f32(vecs, vecs), f32(vecs, rows), f32(vecs // 2, 2 * vecs)],
    )(grams, start, diagonal, own_degree)
    later_grams = lax.all_gather(later_gram, ("row", "col"), axis=0)

    tiles, row_deg, col_deg = form_tiles(first, second, live, row_band, col_band)
    row_places = place_in_row(jnp.arange(row_devices))
    col_deg = jnp.take(col_deg, row_places, axis=0)
    row_parts = exchange(row_deg, "col")
    col_parts = exchange(col_deg, "row")
    roots, inv_root = call(
        degree_kernel, "degree", [f32(col_devices, rows // 128, 128), f32(1, rows)]
    )(own_degree, row_parts, col_parts)
    from_first, from_second = start_vectors(
        first, second, live, row_band, col_band, seeds, factor
    )
    col_roots = exchange(roots[:row_devices], "row")
    row_roots = exchange(roots, "col")
    spread = (subspace * inv_root).astype(jnp.bfloat16)
    for iteration in range(ITERS):
        own_part = lax.dot_general(
            spread, diagonal, (((1,), (0,)), ((), ())), preferred_element_type=jnp.float32
        )
        to_second = apply_tiles(
            0, first, second_device, live, tiles, from_first, row_roots, row_devices
        )
        to_second, from_second = together(to_second, from_second)
        second_part = lax.psum_scatter(to_second, "row", scatter_dimension=0, tiled=False)
        to_first = apply_tiles(
            1, second_device, first, live, tiles, from_second, col_roots, col_devices
        )
        first_parts = exchange(to_first, "col")
        if iteration + 1 < ITERS:
            later_factor = call(later_factor_kernel, "later_factor", f32(vecs, vecs))(later_grams)
            copies, spread = call(
                between_kernel, "between", [bf16(col_devices, vecs, rows), bf16(vecs, rows)]
            )(own_part, first_parts, second_part, inv_root, later_factor)
            from_second = lax.all_gather(spread, "row", axis=0)
            from_first = exchange(copies, "col")
            row_roots = col_roots = None
    subspace, grams = call(
        last_kernel, "last", [f32(vecs, rows), f32(row_devices, vecs // 2, 2 * vecs)]
    )(own_part, first_parts, second_part, inv_root)
    grams = exchange(grams, "row")
    grams = call(relay_kernel, "relay", f32(col_devices, vecs // 2, 2 * vecs))(grams)
    grams = exchange(grams, "col")
    return call(
        functools.partial(final_kernel, all_devices * rows), "final", f32(rows, vecs)
    )(grams, subspace)


def solution(mesh):
    return jax.shard_map(
        shards,
        mesh=mesh,
        in_specs=(P(("row", "col"), None), P(), P("row", "col", None), P("row", "col"), P()),
        out_specs=P(("row", "col"), None),
        check_vma=False,
    )
```

```python
import functools
import math

import jax
import jax.numpy as jnp
from jax import lax
from jax.experimental import pallas as pl
from jax.experimental.pallas import tpu as pltpu
from jax.sharding import PartitionSpec as P

ITERS = 2
LOG2E = math.log2(math.e)
VMEM = 60 * 1024 * 1024
HIGH = lax.Precision.HIGHEST
RIDGE = 1e-6


def lane_sums(values):
    part = values[:, :128]
    for start in range(128, values.shape[1], 128):
        part = part + values[:, start : start + 128]
    return jnp.sum(part.T, axis=0, keepdims=True)


def half_squares(rows):
    wide = rows.astype(jnp.float32)
    return wide * wide * (0.5 * LOG2E)


def tile_chunk(left, right, right_half):
    dots = lax.dot_general(
        left, right, (((1,), (1,)), ((), ())), preferred_element_type=jnp.float32
    )
    left_half = jnp.sum(half_squares(left), axis=1, keepdims=True)
    return jnp.exp2(dots * LOG2E - left_half - right_half)


def pack_row(row):
    return jnp.concatenate([row[:, i : i + 128] for i in range(0, row.shape[1], 128)], axis=0)


def unpack_row(block):
    return jnp.concatenate([block[i : i + 1, :] for i in range(block.shape[0])], axis=1)


def packed_gram(vectors):
    gram = lax.dot_general(
        vectors,
        vectors,
        (((1,), (1,)), ((), ())),
        precision=HIGH,
        preferred_element_type=jnp.float32,
    )
    half = gram.shape[0] // 2
    return jnp.concatenate([gram[:half], gram[half:]], axis=1)


def inverse_factor(packed, ridge):
    half, width = packed.shape
    size = 2 * half
    state = jnp.concatenate([packed, pltpu.roll(packed, size, 1)], axis=0)
    row_id = lax.broadcasted_iota(jnp.int32, state.shape, 0)
    lane_id = lax.broadcasted_iota(jnp.int32, state.shape, 1)
    state = jnp.where(lane_id < size, state, jnp.where(lane_id - size == row_id, 1.0, 0.0))
    if ridge:
        on_diagonal = lane_id == row_id
        trace = jnp.sum(jnp.where(on_diagonal, state, 0.0))
        state = jnp.where(on_diagonal, state + trace * (RIDGE / size), state)
    done = []
    for start in range(0, size, 8):
        columns = [
            jnp.broadcast_to(state[:, start + j : start + j + 1], state.shape) for j in range(8)
        ]
        row_id = lax.broadcasted_iota(jnp.int32, state.shape, 0)
        scale = jnp.zeros((8, width), jnp.float32)
        for j in range(8):
            column = columns[j]
            pivot = column[j : j + 1, :]
            scale = jnp.where(row_id[:8] == j, lax.rsqrt(pivot), scale)
            factor = jnp.where(row_id > j, column * (1.0 / pivot), 0.0)
            state = state - factor * state[j : j + 1, :]
            for m in range(j + 1, 8):
                columns[m] = columns[m] - factor * column[m : m + 1, :]
        done.append(state[:8] * scale)
        state = state[8:]
    full = jnp.concatenate(done, axis=0)
    return pltpu.roll(full, size, 1)[:, :size]


def transform(matrix, vectors):
    return jnp.dot(matrix, vectors, precision=HIGH, preferred_element_type=jnp.float32)


def call(kernel, name, out_shape):
    return pl.pallas_call(
        kernel,
        out_shape=out_shape,
        compiler_params=pltpu.CompilerParams(vmem_limit_bytes=VMEM),
        name=name,
    )


def f32(*shape):
    return jax.ShapeDtypeStruct(shape, jnp.float32)


def bf16(*shape):
    return jax.ShapeDtypeStruct(shape, jnp.bfloat16)


def seed_kernel_rows(seeds, block):
    dots = lax.dot_general(
        seeds, block, (((1,), (1,)), ((), ())), preferred_element_type=jnp.float32
    )
    seed_half = jnp.sum(half_squares(seeds), axis=1, keepdims=True)
    return jnp.exp2(dots * LOG2E - seed_half - lane_sums(half_squares(block)))


def start_kernel(seeds, own, start, grams):
    value = seed_kernel_rows(seeds[...], own[...])
    start[...] = value
    grams[...] = jnp.broadcast_to(packed_gram(value)[None], grams.shape)


def first_factor_kernel(grams, start, diagonal, own_degree, factor, subspace, later_gram):
    inverse = inverse_factor(jnp.sum(grams[...], axis=0), False)
    factor[...] = inverse
    value = transform(inverse, start[...])
    subspace[...] = value
    root = lax.rsqrt(own_degree[...])
    product = jnp.dot(
        (value * root).astype(jnp.bfloat16), diagonal[...], preferred_element_type=jnp.float32
    )
    later_gram[...] = packed_gram(product * root)


def later_factor_kernel(grams, factor):
    factor[...] = inverse_factor(jnp.sum(grams[...], axis=0), True)


def degree_kernel(own_degree, row_parts, col_parts, roots, root):
    total = jnp.sum(row_parts[...], axis=0) + jnp.sum(col_parts[...], axis=0)
    value = lax.rsqrt(total + pack_row(own_degree[...]))
    roots[...] = jnp.broadcast_to(value[None], roots.shape)
    root[...] = unpack_row(value)


def gathered(own_part, first_parts, second_part, root):
    total = own_part[...] + second_part[...].astype(jnp.float32)
    for index in range(first_parts.shape[0]):
        total = total + first_parts[index].astype(jnp.float32)
    return total * root[...]


def between_kernel(own_part, first_parts, second_part, root, factor, copies, spread):
    value = transform(factor[...], gathered(own_part, first_parts, second_part, root))
    value = (value * root[...]).astype(jnp.bfloat16)
    spread[...] = value
    copies[...] = jnp.broadcast_to(value[None], copies.shape)


def last_kernel(own_part, first_parts, second_part, root, subspace, grams):
    value = gathered(own_part, first_parts, second_part, root)
    subspace[...] = value
    grams[...] = jnp.broadcast_to(packed_gram(value)[None], grams.shape)


def final_kernel(points_all, grams, subspace, embedding):
    inverse = inverse_factor(jnp.sum(grams[...], axis=0), False)
    scaled = transform(inverse, subspace[...]) * math.sqrt(points_all)
    mean = jnp.mean(scaled * scaled, axis=0, keepdims=True)
    embedding[...] = (scaled * lax.rsqrt(mean + 1e-06)).T


def relay_kernel(grams, copies):
    copies[...] = jnp.broadcast_to(jnp.sum(grams[...], axis=0)[None], copies.shape)


def vectors_kernel(first, second, live, left, right, seeds, factor, from_first, from_second):
    @pl.when(pl.program_id(0) < live[0])
    def work():
        for block, out in ((left, from_first), (right, from_second)):
            out[0] = transform(factor[...], seed_kernel_rows(seeds[...], block[0]))


def start_vectors(first, second, live, row_band, col_band, seeds, factor):
    unused, rows, depth = row_band.shape
    slots = first.shape[0]
    vecs = seeds.shape[0]

    def last(step, live_ref):
        return jnp.maximum(jnp.minimum(step, live_ref[0] - 1), 0)

    return pl.pallas_call(
        vectors_kernel,
        grid_spec=pltpu.PrefetchScalarGridSpec(
            num_scalar_prefetch=3,
            grid=(slots,),
            in_specs=[
                pl.BlockSpec((1, rows, depth), lambda s, f, g, n: (f[last(s, n)], 0, 0)),
                pl.BlockSpec((1, rows, depth), lambda s, f, g, n: (g[last(s, n)], 0, 0)),
                pl.BlockSpec((vecs, depth), lambda s, f, g, n: (0, 0)),
                pl.BlockSpec((vecs, vecs), lambda s, f, g, n: (0, 0)),
            ],
            out_specs=[
                pl.BlockSpec((1, vecs, rows), lambda s, f, g, n: (last(s, n), 0, 0))
            ] * 2,
        ),
        out_shape=[f32(slots, vecs, rows)] * 2,
        compiler_params=pltpu.CompilerParams(vmem_limit_bytes=VMEM),
        name="start_vectors",
    )(first, second, live, row_band, col_band, seeds, factor)


def form_kernel(chunk, first, second, live, left, right, tile, row_deg, col_deg):
    step = pl.program_id(0)

    @pl.when(step == 0)
    def clear():
        row_deg[...] = jnp.zeros_like(row_deg)
        col_deg[...] = jnp.zeros_like(col_deg)

    @pl.when(step < live[0])
    def work():
        rows = left.shape[1]
        right_rows = right[0]
        right_half = lane_sums(half_squares(right_rows))
        col_total = jnp.zeros((1, rows), jnp.float32)
        row_totals = []
        for start in range(0, rows, chunk):
            value = tile_chunk(left[0, start : start + chunk, :], right_rows, right_half)
            tile[0, start : start + chunk, :] = value.astype(jnp.bfloat16)
            col_total = col_total + jnp.sum(value, axis=0, keepdims=True)
            row_totals.append(lane_sums(value))
        row_slot = first[step]
        col_slot = second[step]
        row_total = jnp.concatenate(row_totals, axis=1)
        row_deg[row_slot] = row_deg[row_slot] + pack_row(row_total)
        col_deg[col_slot] = col_deg[col_slot] + pack_row(col_total)


def form_tiles(first, second, live, row_band, col_band):
    col_devices, rows, depth = row_band.shape
    row_devices = col_band.shape[0]
    slots = first.shape[0]

    def last(step, live_ref):
        return jnp.maximum(jnp.minimum(step, live_ref[0] - 1), 0)

    return pl.pallas_call(
        functools.partial(form_kernel, min(256, rows)),
        grid_spec=pltpu.PrefetchScalarGridSpec(
            num_scalar_prefetch=3,
            grid=(slots,),
            in_specs=[
                pl.BlockSpec((1, rows, depth), lambda s, f, g, n: (f[last(s, n)], 0, 0)),
                pl.BlockSpec((1, rows, depth), lambda s, f, g, n: (g[last(s, n)], 0, 0)),
            ],
            out_specs=[
                pl.BlockSpec((1, rows, rows), lambda s, f, g, n: (last(s, n), 0, 0)),
                pl.BlockSpec((col_devices, rows // 128, 128), lambda s, f, g, n: (0, 0, 0)),
                pl.BlockSpec((row_devices, rows // 128, 128), lambda s, f, g, n: (0, 0, 0)),
            ],
        ),
        out_shape=[
            bf16(slots, rows, rows),
            f32(col_devices, rows // 128, 128),
            f32(row_devices, rows // 128, 128),
        ],
        compiler_params=pltpu.CompilerParams(vmem_limit_bytes=VMEM),
        name="form_tiles",
    )(first, second, live, row_band, col_band)


def diagonal_kernel(chunk, own, tile, degree):
    rows = own.shape[0]
    right_rows = own[...]
    right_half = lane_sums(half_squares(right_rows))
    total = jnp.zeros((1, rows), jnp.float32)
    for start in range(0, rows, chunk):
        value = tile_chunk(own[start : start + chunk, :], right_rows, right_half)
        tile[start : start + chunk, :] = value.astype(jnp.bfloat16)
        total = total + jnp.sum(value, axis=0, keepdims=True)
    degree[...] = total


def form_diagonal(own):
    rows = own.shape[0]
    return pl.pallas_call(
        functools.partial(diagonal_kernel, min(256, rows)),
        out_shape=[
            jax.ShapeDtypeStruct((rows, rows), jnp.bfloat16),
            jax.ShapeDtypeStruct((1, rows), jnp.float32),
        ],
        compiler_params=pltpu.CompilerParams(vmem_limit_bytes=VMEM),
        name="form_diagonal",
    )(own)


def apply_kernel(contract, source, target, live, tile, vectors, *rest):
    step = pl.program_id(0)
    roots, out, total = rest if len(rest) == 3 else (None,) + rest

    @pl.when(step == 0)
    def clear():
        total[...] = jnp.zeros_like(total)

    @pl.when(step < live[0])
    def work():
        slot = target[step]
        block = vectors[0]
        if roots is not None:
            block = (block * unpack_row(roots[0])).astype(jnp.bfloat16)
        total[slot] = total[slot] + lax.dot_general(
            block, tile[0], (((1,), (contract,)), ((), ())), preferred_element_type=jnp.float32
        )

    @pl.when(step == pl.num_programs(0) - 1)
    def store():
        out[...] = total[...].astype(jnp.bfloat16)


def apply_tiles(contract, source, target, live, tiles, vectors, roots, targets):
    slots, rows, unused = tiles.shape
    vecs = vectors.shape[1]

    def last(step, live_ref):
        return jnp.maximum(jnp.minimum(step, live_ref[0] - 1), 0)

    def by_task(s, f, g, n):
        return (last(s, n), 0, 0)

    def by_block(s, f, g, n):
        return (f[last(s, n)], 0, 0)

    in_specs = [
        pl.BlockSpec((1, rows, rows), by_task),
        pl.BlockSpec((1, vecs, rows), by_block if roots is None else by_task),
    ]
    operands = [tiles, vectors]
    if roots is not None:
        in_specs.append(pl.BlockSpec((1, rows // 128, 128), by_block))
        operands.append(roots)
    return pl.pallas_call(
        functools.partial(apply_kernel, contract),
        grid_spec=pltpu.PrefetchScalarGridSpec(
            num_scalar_prefetch=3,
            grid=(slots,),
            in_specs=in_specs,
            out_specs=pl.BlockSpec((targets, vecs, rows), lambda s, f, g, n: (0, 0, 0)),
            scratch_shapes=[pltpu.VMEM((targets, vecs, rows), jnp.float32)],
        ),
        out_shape=bf16(targets, vecs, rows),
        compiler_params=pltpu.CompilerParams(vmem_limit_bytes=VMEM),
        name="apply_tiles",
    )(source, target, live, *operands)


def spread_to(array, axis):
    devices = lax.axis_size(axis)
    copies = jnp.broadcast_to(array[None], (devices,) + array.shape)
    return lax.all_to_all(copies, axis, 0, 0, tiled=True)


def exchange(copies, axis):
    return lax.all_to_all(copies, axis, 0, 0, tiled=True)


def together(*arrays):
    return lax.optimization_barrier(arrays)


def place_in_row(index, here):
    apart = (index // 2 - here // 2 + 4) % 4
    order = jnp.where(apart == 0, 0, jnp.where(apart == 3, 1, jnp.where(apart == 1, 2, 3)))
    return order + 4 * ((index + here) % 2)


def assign_kernel(shape, here, table, first, second, place, live, load, ends, chosen):
    devices, width, slots, cols = shape
    me = here[0]

    def each_task(body, init):
        def of_device(device, state):
            def of_slot(slot, inner):
                return body(device, slot, table[device * width + slot], inner)

            return lax.fori_loop(0, table[device * width + slots], of_slot, state)

        return lax.fori_loop(0, devices, of_device, init)

    def clear(device, state):
        load[device] = 0
        return state

    lax.fori_loop(0, devices, clear, 0)

    def place_first(device, slot, partner, state):
        end = jnp.where(load[partner] <= load[device], partner, device)
        load[end] = load[end] + 1
        ends[device * slots + slot] = end
        return state

    each_task(place_first, 0)

    def place_last(device, slot, partner, count):
        end = ends[device * slots + slot]
        other = device + partner - end
        move = load[end] > load[other] + 1
        load[end] = load[end] - jnp.where(move, 1, 0)
        load[other] = load[other] + jnp.where(move, 1, 0)
        final = jnp.where(move, other, end)
        chosen[count] = device + partner - final
        return count + jnp.where(final == me, 1, 0)

    count = each_task(place_last, 0)
    most = lax.fori_loop(0, devices, lambda i, top: jnp.maximum(top, load[i]), 0)
    shared = most <= slots
    live[0] = jnp.where(shared, count, table[me * width + slots])
    for slot in range(slots):
        listed = jnp.where(shared, chosen[slot], table[me * width + slot])
        partner = jnp.where(slot < live[0], listed, 0)
        first[slot] = lax.rem(partner, cols)
        second[slot] = lax.div(partner, cols)
        place[slot] = place_in_row(second[slot], lax.div(me, cols))


def assign_tasks(self_index, table, devices, slots, cols):
    width = table.shape[0] // devices
    smem = pl.BlockSpec(memory_space=pltpu.SMEM)
    lists = jax.ShapeDtypeStruct((slots,), jnp.int32)
    return pl.pallas_call(
        functools.partial(assign_kernel, (devices, width, slots, cols)),
        in_specs=[smem, smem],
        out_specs=[smem] * 4,
        out_shape=[lists, lists, lists, jax.ShapeDtypeStruct((1,), jnp.int32)],
        scratch_shapes=[
            pltpu.SMEM((devices,), jnp.int32),
            pltpu.SMEM((devices * slots,), jnp.int32),
            pltpu.SMEM((4 * slots,), jnp.int32),
        ],
        name="assign_tasks",
    )(self_index.reshape(1), table)


def shards(points, feature_scale, tile_tasks, task_count, seed_ids):
    rows = points.shape[0]
    vecs = seed_ids.shape[0]
    row_devices = lax.axis_size("row")
    col_devices = lax.axis_size("col")
    all_devices = row_devices * col_devices
    self_index = lax.axis_index("row") * col_devices + lax.axis_index("col")
    weighted = (points.astype(jnp.float32) * feature_scale[None, :]).astype(jnp.bfloat16)
    row_band = lax.all_gather(weighted, "col", axis=0)
    listed = tile_tasks.reshape(-1)
    slots = listed.shape[0]

    def shift(array, by):
        return lax.ppermute(
            array, "row", [(i, (i + by) % row_devices) for i in range(row_devices)]
        )

    local_seed = seed_ids - self_index * rows
    inside = (local_seed >= 0) & (local_seed < rows)
    picked = jnp.where(
        inside[:, None], jnp.take(weighted, jnp.clip(local_seed, 0, rows - 1), axis=0), 0
    ).astype(jnp.bfloat16)
    own_line = jnp.concatenate(
        [listed, task_count.reshape(-1), jnp.zeros((slots - 1,), jnp.int32)]
    )
    lines = jnp.where(
        (jnp.arange(all_devices) == self_index)[:, None], own_line[None, :], 0
    ).astype(jnp.bfloat16)
    lines = lines.reshape(-1, weighted.shape[1])
    padding = jnp.zeros((-lines.shape[0] % 16, weighted.shape[1]), jnp.bfloat16)
    picked = jnp.concatenate([picked, lines, padding], axis=0)
    seed_parts = spread_to(picked, "row")
    before = shift(weighted, 2)
    after = shift(weighted, -2)
    before, after, seed_parts = together(before, after, seed_parts)
    half = rows // 2
    across_low = shift(before[:half], 2)
    across_high = shift(after[half:], -2)
    seed_parts = spread_to(jnp.sum(seed_parts, axis=0), "col")
    across_low, across_high, seed_parts = together(across_low, across_high, seed_parts)
    seed_sum = jnp.sum(seed_parts, axis=0)
    seeds = seed_sum[:vecs]
    table = seed_sum[vecs : vecs + lines.shape[0]].astype(jnp.int32).reshape(-1)
    first, second_device, second, live = assign_tasks(
        self_index, table, all_devices, slots, col_devices
    )
    across = jnp.concatenate([across_low, across_high], axis=0)
    mine = jnp.stack([weighted, before, after, across])
    other = lax.ppermute(mine, "row", [(i, i ^ 1) for i in range(row_devices)])

    start, grams = call(
        start_kernel, "start", [f32(vecs, rows), f32(row_devices, vecs // 2, 2 * vecs)]
    )(seeds, weighted)
    grams = exchange(grams, "row")
    col_band, grams = together(jnp.concatenate([mine, other], axis=0), grams)
    grams = call(relay_kernel, "relay", f32(col_devices, vecs // 2, 2 * vecs))(grams)
    grams = exchange(grams, "col")
    diagonal, own_degree = form_diagonal(weighted)
    factor, subspace, later_gram = call(
        first_factor_kernel,
        "first_factor",
        [f32(vecs, vecs), f32(vecs, rows), f32(vecs // 2, 2 * vecs)],
    )(grams, start, diagonal, own_degree)
    later_grams = lax.all_gather(later_gram, ("row", "col"), axis=0)

    tiles, row_deg, col_deg = form_tiles(first, second, live, row_band, col_band)
    row_places = place_in_row(jnp.arange(row_devices), lax.axis_index("row"))
    col_deg = jnp.take(col_deg, row_places, axis=0)
    row_parts = exchange(row_deg, "col")
    col_parts = exchange(col_deg, "row")
    roots, inv_root = call(
        degree_kernel, "degree", [f32(col_devices, rows // 128, 128), f32(1, rows)]
    )(own_degree, row_parts, col_parts)
    from_first, from_second = start_vectors(
        first, second, live, row_band, col_band, seeds, factor
    )
    col_roots = exchange(roots[:row_devices], "row")
    row_roots = exchange(roots, "col")
    spread = (subspace * inv_root).astype(jnp.bfloat16)
    for iteration in range(ITERS):
        own_part = lax.dot_general(
            spread, diagonal, (((1,), (0,)), ((), ())), preferred_element_type=jnp.float32
        )
        to_second = apply_tiles(
            0, first, second_device, live, tiles, from_first, row_roots, row_devices
        )
        to_second, from_second = together(to_second, from_second)
        second_part = lax.psum_scatter(to_second, "row", scatter_dimension=0, tiled=False)
        to_first = apply_tiles(
            1, second_device, first, live, tiles, from_second, col_roots, col_devices
        )
        first_parts = exchange(to_first, "col")
        if iteration + 1 < ITERS:
            later_factor = call(later_factor_kernel, "later_factor", f32(vecs, vecs))(later_grams)
            copies, spread = call(
                between_kernel, "between", [bf16(col_devices, vecs, rows), bf16(vecs, rows)]
            )(own_part, first_parts, second_part, inv_root, later_factor)
            from_second = lax.all_gather(spread, "row", axis=0)
            from_first = exchange(copies, "col")
            row_roots = col_roots = None
    subspace, grams = call(
        last_kernel, "last", [f32(vecs, rows), f32(row_devices, vecs // 2, 2 * vecs)]
    )(own_part, first_parts, second_part, inv_root)
    grams = exchange(grams, "row")
    grams = call(relay_kernel, "relay", f32(col_devices, vecs // 2, 2 * vecs))(grams)
    grams = exchange(grams, "col")
    return call(
        functools.partial(final_kernel, all_devices * rows), "final", f32(rows, vecs)
    )(grams, subspace)


def solution(mesh):
    return jax.shard_map(
        shards,
        mesh=mesh,
        in_specs=(P(("row", "col"), None), P(), P("row", "col", None), P("row", "col"), P()),
        out_specs=P(("row", "col"), None),
        check_vma=False,
    )
```

```python
import functools
import math

import jax
import jax.numpy as jnp
from jax import lax
from jax.experimental import pallas as pl
from jax.experimental.pallas import tpu as pltpu
from jax.sharding import PartitionSpec as P

ITERS = 2
LOG2E = math.log2(math.e)
VMEM = 60 * 1024 * 1024
SMALL = 24 * 1024 * 1024
HIGH = lax.Precision.HIGHEST
RIDGE = 1e-6


def lane_sums(values):
    part = values[:, :128]
    for start in range(128, values.shape[1], 128):
        part = part + values[:, start : start + 128]
    return jnp.sum(part.T, axis=0, keepdims=True)


def half_squares(rows):
    wide = rows.astype(jnp.float32)
    return wide * wide * (0.5 * LOG2E)


def tile_chunk(left, right, right_half):
    dots = lax.dot_general(
        left, right, (((1,), (1,)), ((), ())), preferred_element_type=jnp.float32
    )
    left_half = jnp.sum(half_squares(left), axis=1, keepdims=True)
    return jnp.exp2(dots * LOG2E - left_half - right_half)


def pack_row(row):
    return jnp.concatenate([row[:, i : i + 128] for i in range(0, row.shape[1], 128)], axis=0)


def unpack_row(block):
    return jnp.concatenate([block[i : i + 1, :] for i in range(block.shape[0])], axis=1)


def packed_gram(vectors):
    gram = lax.dot_general(
        vectors,
        vectors,
        (((1,), (1,)), ((), ())),
        precision=HIGH,
        preferred_element_type=jnp.float32,
    )
    half = gram.shape[0] // 2
    return jnp.concatenate([gram[:half], gram[half:]], axis=1)


def inverse_factor(packed, ridge):
    half, width = packed.shape
    size = 2 * half
    state = jnp.concatenate([packed, pltpu.roll(packed, size, 1)], axis=0)
    row_id = lax.broadcasted_iota(jnp.int32, state.shape, 0)
    lane_id = lax.broadcasted_iota(jnp.int32, state.shape, 1)
    state = jnp.where(lane_id < size, state, jnp.where(lane_id - size == row_id, 1.0, 0.0))
    if ridge:
        on_diagonal = lane_id == row_id
        trace = jnp.sum(jnp.where(on_diagonal, state, 0.0))
        state = jnp.where(on_diagonal, state + trace * (RIDGE / size), state)
    done = []
    for start in range(0, size, 8):
        columns = [
            jnp.broadcast_to(state[:, start + j : start + j + 1], state.shape) for j in range(8)
        ]
        row_id = lax.broadcasted_iota(jnp.int32, state.shape, 0)
        scale = jnp.zeros((8, width), jnp.float32)
        for j in range(8):
            column = columns[j]
            pivot = column[j : j + 1, :]
            scale = jnp.where(row_id[:8] == j, lax.rsqrt(pivot), scale)
            factor = jnp.where(row_id > j, column * (1.0 / pivot), 0.0)
            state = state - factor * state[j : j + 1, :]
            for m in range(j + 1, 8):
                columns[m] = columns[m] - factor * column[m : m + 1, :]
        done.append(state[:8] * scale)
        state = state[8:]
    full = jnp.concatenate(done, axis=0)
    return pltpu.roll(full, size, 1)[:, :size]


def transform(matrix, vectors):
    return jnp.dot(matrix, vectors, precision=HIGH, preferred_element_type=jnp.float32)


def call(kernel, name, out_shape, grant=SMALL):
    return pl.pallas_call(
        kernel,
        out_shape=out_shape,
        compiler_params=pltpu.CompilerParams(vmem_limit_bytes=grant),
        name=name,
    )


def f32(*shape):
    return jax.ShapeDtypeStruct(shape, jnp.float32)


def bf16(*shape):
    return jax.ShapeDtypeStruct(shape, jnp.bfloat16)


def seed_kernel_rows(seeds, block):
    dots = lax.dot_general(
        seeds, block, (((1,), (1,)), ((), ())), preferred_element_type=jnp.float32
    )
    seed_half = jnp.sum(half_squares(seeds), axis=1, keepdims=True)
    return jnp.exp2(dots * LOG2E - seed_half - lane_sums(half_squares(block)))


def start_kernel(seeds, own, start, grams):
    value = seed_kernel_rows(seeds[...], own[...])
    start[...] = value
    grams[...] = jnp.broadcast_to(packed_gram(value)[None], grams.shape)


def first_factor_kernel(grams, start, diagonal, own_degree, factor, subspace, later_gram):
    inverse = inverse_factor(jnp.sum(grams[...], axis=0), False)
    factor[...] = inverse
    value = transform(inverse, start[...])
    subspace[...] = value
    root = lax.rsqrt(own_degree[...])
    product = jnp.dot(
        (value * root).astype(jnp.bfloat16), diagonal[...], preferred_element_type=jnp.float32
    )
    later_gram[...] = packed_gram(product * root)


def later_factor_kernel(grams, factor):
    factor[...] = inverse_factor(jnp.sum(grams[...], axis=0), True)


def degree_kernel(own_degree, parts, roots, root):
    value = lax.rsqrt(jnp.sum(parts[...], axis=0) + pack_row(own_degree[...]))
    roots[...] = jnp.broadcast_to(value[None], roots.shape)
    root[...] = unpack_row(value)


def gathered(own_part, first_parts, second_part, root):
    total = own_part[...] + second_part[...].astype(jnp.float32)
    for index in range(first_parts.shape[0]):
        total = total + first_parts[index].astype(jnp.float32)
    return total * root[...]


def between_kernel(own_part, first_parts, second_part, root, factor, copies, spread):
    value = transform(factor[...], gathered(own_part, first_parts, second_part, root))
    value = (value * root[...]).astype(jnp.bfloat16)
    spread[...] = value
    copies[...] = jnp.broadcast_to(value[None], copies.shape)


def last_kernel(own_part, first_parts, second_part, root, subspace, grams):
    value = gathered(own_part, first_parts, second_part, root)
    subspace[...] = value
    grams[...] = jnp.broadcast_to(packed_gram(value)[None], grams.shape)


def final_kernel(points_all, grams, subspace, embedding):
    inverse = inverse_factor(jnp.sum(grams[...], axis=0), False)
    scaled = transform(inverse, subspace[...]) * math.sqrt(points_all)
    mean = jnp.mean(scaled * scaled, axis=0, keepdims=True)
    embedding[...] = scaled * lax.rsqrt(mean + 1e-06)


def relay_kernel(grams, copies):
    copies[...] = jnp.broadcast_to(jnp.sum(grams[...], axis=0)[None], copies.shape)


def vectors_kernel(first, second, live, left, right, seeds, factor, from_first, from_second):
    @pl.when(pl.program_id(0) < live[0])
    def work():
        for block, out in ((left, from_first), (right, from_second)):
            out[0] = transform(factor[...], seed_kernel_rows(seeds[...], block[0]))


def start_vectors(first, second, live, row_band, col_band, seeds, factor):
    unused, rows, depth = row_band.shape
    slots = first.shape[0]
    vecs = seeds.shape[0]

    def last(step, live_ref):
        return jnp.maximum(jnp.minimum(step, live_ref[0] - 1), 0)

    return pl.pallas_call(
        vectors_kernel,
        grid_spec=pltpu.PrefetchScalarGridSpec(
            num_scalar_prefetch=3,
            grid=(slots,),
            in_specs=[
                pl.BlockSpec((1, rows, depth), lambda s, f, g, n: (f[last(s, n)], 0, 0)),
                pl.BlockSpec((1, rows, depth), lambda s, f, g, n: (g[last(s, n)], 0, 0)),
                pl.BlockSpec((vecs, depth), lambda s, f, g, n: (0, 0)),
                pl.BlockSpec((vecs, vecs), lambda s, f, g, n: (0, 0)),
            ],
            out_specs=[
                pl.BlockSpec((1, vecs, rows), lambda s, f, g, n: (last(s, n), 0, 0))
            ] * 2,
        ),
        out_shape=[f32(slots, vecs, rows)] * 2,
        compiler_params=pltpu.CompilerParams(vmem_limit_bytes=VMEM),
        name="start_vectors",
    )(first, second, live, row_band, col_band, seeds, factor)


def form_kernel(chunk, first, second, owners, live, left, right, tile, degrees):
    step = pl.program_id(0)

    @pl.when(step == 0)
    def clear():
        degrees[...] = jnp.zeros_like(degrees)

    @pl.when(step < live[0])
    def work():
        rows = left.shape[1]
        right_rows = right[0]
        right_half = lane_sums(half_squares(right_rows))
        col_total = jnp.zeros((1, rows), jnp.float32)
        row_totals = []
        for start in range(0, rows, chunk):
            value = tile_chunk(left[0, start : start + chunk, :], right_rows, right_half)
            tile[0, start : start + chunk, :] = value.astype(jnp.bfloat16)
            col_total = col_total + jnp.sum(value, axis=0, keepdims=True)
            row_totals.append(lane_sums(value))
        left_owner = owners[2 * step]
        right_owner = owners[2 * step + 1]
        row_total = jnp.concatenate(row_totals, axis=1)
        degrees[left_owner] = degrees[left_owner] + pack_row(row_total)
        degrees[right_owner] = degrees[right_owner] + pack_row(col_total)


def form_tiles(first, second, owners, live, row_band, col_band):
    col_devices, rows, depth = row_band.shape
    all_devices = col_devices * col_band.shape[0]
    slots = first.shape[0]

    def last(step, live_ref):
        return jnp.maximum(jnp.minimum(step, live_ref[0] - 1), 0)

    return pl.pallas_call(
        functools.partial(form_kernel, min(256, rows)),
        grid_spec=pltpu.PrefetchScalarGridSpec(
            num_scalar_prefetch=4,
            grid=(slots,),
            in_specs=[
                pl.BlockSpec((1, rows, depth), lambda s, f, g, o, n: (f[last(s, n)], 0, 0)),
                pl.BlockSpec((1, rows, depth), lambda s, f, g, o, n: (g[last(s, n)], 0, 0)),
            ],
            out_specs=[
                pl.BlockSpec((1, rows, rows), lambda s, f, g, o, n: (last(s, n), 0, 0)),
                pl.BlockSpec(
                    (all_devices, rows // 128, 128), lambda s, f, g, o, n: (0, 0, 0)
                ),
            ],
        ),
        out_shape=[bf16(slots, rows, rows), f32(all_devices, rows // 128, 128)],
        compiler_params=pltpu.CompilerParams(vmem_limit_bytes=VMEM),
        name="form_tiles",
    )(first, second, owners, live, row_band, col_band)


def diagonal_kernel(chunk, own, tile, degree):
    rows = own.shape[0]
    right_rows = own[...]
    right_half = lane_sums(half_squares(right_rows))
    total = jnp.zeros((1, rows), jnp.float32)
    for start in range(0, rows, chunk):
        value = tile_chunk(own[start : start + chunk, :], right_rows, right_half)
        tile[start : start + chunk, :] = value.astype(jnp.bfloat16)
        total = total + jnp.sum(value, axis=0, keepdims=True)
    degree[...] = total


def form_diagonal(own):
    rows = own.shape[0]
    return pl.pallas_call(
        functools.partial(diagonal_kernel, min(256, rows)),
        out_shape=[
            jax.ShapeDtypeStruct((rows, rows), jnp.bfloat16),
            jax.ShapeDtypeStruct((1, rows), jnp.float32),
        ],
        compiler_params=pltpu.CompilerParams(vmem_limit_bytes=SMALL),
        name="form_diagonal",
    )(own)


def apply_kernel(contract, source, target, live, tile, vectors, *rest):
    step = pl.program_id(0)
    roots, out, total = rest if len(rest) == 3 else (None,) + rest

    @pl.when(step == 0)
    def clear():
        total[...] = jnp.zeros_like(total)

    @pl.when(step < live[0])
    def work():
        slot = target[step]
        block = vectors[0]
        if roots is not None:
            block = (block * unpack_row(roots[0])).astype(jnp.bfloat16)
        total[slot] = total[slot] + lax.dot_general(
            block, tile[0], (((1,), (contract,)), ((), ())), preferred_element_type=jnp.float32
        )

    @pl.when(step == pl.num_programs(0) - 1)
    def store():
        out[...] = total[...].astype(jnp.bfloat16)


def apply_tiles(contract, source, target, live, tiles, vectors, roots, targets):
    slots, rows, unused = tiles.shape
    vecs = vectors.shape[1]

    def last(step, live_ref):
        return jnp.maximum(jnp.minimum(step, live_ref[0] - 1), 0)

    def by_task(s, f, g, n):
        return (last(s, n), 0, 0)

    def by_block(s, f, g, n):
        return (f[last(s, n)], 0, 0)

    in_specs = [
        pl.BlockSpec((1, rows, rows), by_task),
        pl.BlockSpec((1, vecs, rows), by_block if roots is None else by_task),
    ]
    operands = [tiles, vectors]
    if roots is not None:
        in_specs.append(pl.BlockSpec((1, rows // 128, 128), by_block))
        operands.append(roots)
    return pl.pallas_call(
        functools.partial(apply_kernel, contract),
        grid_spec=pltpu.PrefetchScalarGridSpec(
            num_scalar_prefetch=3,
            grid=(slots,),
            in_specs=in_specs,
            out_specs=pl.BlockSpec((targets, vecs, rows), lambda s, f, g, n: (0, 0, 0)),
            scratch_shapes=[pltpu.VMEM((targets, vecs, rows), jnp.float32)],
        ),
        out_shape=bf16(targets, vecs, rows),
        compiler_params=pltpu.CompilerParams(vmem_limit_bytes=VMEM),
        name="apply_tiles",
    )(source, target, live, *operands)


def spread_to(array, axis):
    devices = lax.axis_size(axis)
    copies = jnp.broadcast_to(array[None], (devices,) + array.shape)
    return lax.all_to_all(copies, axis, 0, 0, tiled=True)


def exchange(copies, axis):
    return lax.all_to_all(copies, axis, 0, 0, tiled=True)


def together(*arrays):
    return lax.optimization_barrier(arrays)


def place_in_row(index, here):
    apart = (index // 2 - here // 2 + 4) % 4
    order = jnp.where(apart == 0, 0, jnp.where(apart == 3, 1, jnp.where(apart == 1, 2, 3)))
    return order + 4 * ((index + here) % 2)


def assign_kernel(slots, cols, here, table, first, second, place, owners, live):
    devices = table.shape[1]
    me = here[0]
    filler = jnp.zeros((devices - table.shape[0], devices), jnp.float32)
    by_device = jnp.concatenate([table[...], filler], axis=0).T
    device = lax.broadcasted_iota(jnp.int32, (devices, devices), 0)
    lane = lax.broadcasted_iota(jnp.int32, (devices, devices), 1)
    same = jnp.where(device == lane, 1.0, 0.0)
    count = by_device[:, slots : slots + 1]
    load = jnp.zeros((1, devices), jnp.float32)
    moves = []
    taken = []
    listed = []
    for slot in range(slots):
        partner = by_device[:, slot : slot + 1]
        is_listed = jnp.where(count > slot, 1.0, 0.0)
        picks = jnp.where(lane.astype(jnp.float32) == partner, 1.0, 0.0)
        move = (picks - same) * is_listed
        apart = jnp.sum(move * load, axis=1, keepdims=True)
        take = jnp.where(apart <= 0, is_listed, 0.0)
        load = load + jnp.sum(same * is_listed + move * take, axis=0, keepdims=True)
        moves.append(move)
        taken.append(take)
        listed.append(is_listed)
    for slot in range(slots):
        apart = jnp.sum(moves[slot] * load, axis=1, keepdims=True)
        give = jnp.where(apart < -1, listed[slot] * (1.0 - taken[slot]), 0.0)
        back = jnp.where(apart > 1, taken[slot], 0.0)
        load = load + jnp.sum(moves[slot] * (give - back), axis=0, keepdims=True)
        taken[slot] = taken[slot] + give - back
    shared = jnp.where(jnp.max(load) <= slots, 1.0, 0.0)
    code = jnp.zeros((devices, devices), jnp.float32)
    number = device.astype(jnp.float32)
    for slot in range(slots):
        partner = by_device[:, slot : slot + 1]
        take = taken[slot] * shared
        kept = jnp.where(device == me, listed[slot] - take, 0.0)
        come = jnp.where(partner == me.astype(jnp.float32), take, 0.0)
        other = kept * partner + come * number
        cell = (kept + come) * (number * slots + (slot + 1)) * devices + other
        code = jnp.where(lane == slot, cell, code)
    live[0] = jnp.sum(jnp.where(code > 0, 1.0, 0.0)).astype(jnp.int32)
    for slot in range(slots):
        top = jnp.max(code)
        partner = lax.rem(top.astype(jnp.int32), devices)
        code = jnp.where(code == top, 0.0, code)
        first_slot = lax.rem(partner, cols)
        second_slot = lax.div(partner, cols)
        first[slot] = first_slot
        second[slot] = second_slot
        place[slot] = place_in_row(second_slot, lax.div(me, cols))
        owners[2 * slot] = lax.div(me, cols) * cols + first_slot
        owners[2 * slot + 1] = second_slot * cols + lax.rem(me, cols)


def assign_tasks(self_index, table, slots, cols):
    smem = pl.BlockSpec(memory_space=pltpu.SMEM)
    sizes = (slots, slots, slots, 2 * slots, 1)
    return pl.pallas_call(
        functools.partial(assign_kernel, slots, cols),
        in_specs=[smem, pl.BlockSpec(memory_space=pltpu.VMEM)],
        out_specs=[smem] * len(sizes),
        out_shape=[jax.ShapeDtypeStruct((size,), jnp.int32) for size in sizes],
        compiler_params=pltpu.CompilerParams(vmem_limit_bytes=SMALL),
        name="assign_tasks",
    )(self_index.reshape(1), table)


def shards(points, feature_scale, tile_tasks, task_count, seed_ids):
    rows = points.shape[0]
    vecs = seed_ids.shape[0]
    row_devices = lax.axis_size("row")
    col_devices = lax.axis_size("col")
    all_devices = row_devices * col_devices
    self_index = lax.axis_index("row") * col_devices + lax.axis_index("col")
    weighted = (points.astype(jnp.float32) * feature_scale[None, :]).astype(jnp.bfloat16)
    row_band = lax.all_gather(weighted, "col", axis=0)
    listed = tile_tasks.reshape(-1)
    slots = listed.shape[0]

    def shift(array, by):
        return lax.ppermute(
            array, "row", [(i, (i + by) % row_devices) for i in range(row_devices)]
        )

    local_seed = seed_ids - self_index * rows
    inside = (local_seed >= 0) & (local_seed < rows)
    picked = jnp.where(
        inside[:, None], jnp.take(weighted, jnp.clip(local_seed, 0, rows - 1), axis=0), 0
    ).astype(jnp.bfloat16)
    own_line = jnp.concatenate(
        [listed, task_count.reshape(-1), jnp.zeros((slots - 1,), jnp.int32)]
    )
    lines = jnp.where(
        (jnp.arange(weighted.shape[1]) == self_index)[None, :], own_line[:, None], 0
    ).astype(jnp.bfloat16)
    picked = jnp.concatenate([picked, lines], axis=0)
    seed_parts = spread_to(picked, "row")
    sent, seed_parts = together(weighted, seed_parts)
    before = shift(sent, 2)
    after = shift(sent, -2)
    half = rows // 2
    across_low = shift(before[:half], 2)
    across_high = shift(after[half:], -2)
    seed_parts = spread_to(jnp.sum(seed_parts, axis=0), "col")
    seed_sum = jnp.sum(seed_parts, axis=0)
    seeds = seed_sum[:vecs]
    table = seed_sum[vecs:, :all_devices].astype(jnp.float32)
    assigned = assign_tasks(self_index, table, slots, col_devices)
    across = jnp.concatenate([across_low, across_high], axis=0)
    mine = jnp.stack([weighted, before, after, across])
    other = lax.ppermute(mine, "row", [(i, i ^ 1) for i in range(row_devices)])

    start, grams = call(
        start_kernel, "start", [f32(vecs, rows), f32(row_devices, vecs // 2, 2 * vecs)]
    )(seeds, weighted)
    grams = exchange(grams, "row")
    grams, first, second_device, second, owners, live = together(grams, *assigned)
    grams = call(relay_kernel, "relay", f32(col_devices, vecs // 2, 2 * vecs))(grams)
    grams = exchange(grams, "col")
    col_band, grams = together(jnp.concatenate([mine, other], axis=0), grams)
    diagonal, own_degree = form_diagonal(weighted)
    factor, subspace, later_gram = call(
        first_factor_kernel,
        "first_factor",
        [f32(vecs, vecs), f32(vecs, rows), f32(vecs // 2, 2 * vecs)],
    )(grams, start, diagonal, own_degree)
    later_grams = lax.all_gather(later_gram, ("row", "col"), axis=0)

    tiles, degrees = form_tiles(first, second, owners, live, row_band, col_band)
    roots, inv_root = call(
        degree_kernel, "degree", [f32(col_devices, rows // 128, 128), f32(1, rows)]
    )(own_degree, exchange(degrees, ("row", "col")))
    from_first, from_second = start_vectors(
        first, second, live, row_band, col_band, seeds, factor
    )
    col_roots = exchange(roots[:row_devices], "row")
    row_roots = exchange(roots, "col")
    spread = (subspace * inv_root).astype(jnp.bfloat16)
    for iteration in range(ITERS):
        own_part = lax.dot_general(
            spread, diagonal, (((1,), (0,)), ((), ())), preferred_element_type=jnp.float32
        )
        to_second = apply_tiles(
            0, first, second_device, live, tiles, from_first, row_roots, row_devices
        )
        to_second, from_second = together(to_second, from_second)
        second_part = lax.psum_scatter(to_second, "row", scatter_dimension=0, tiled=False)
        to_first = apply_tiles(
            1, second_device, first, live, tiles, from_second, col_roots, col_devices
        )
        first_parts = exchange(to_first, "col")
        if iteration + 1 < ITERS:
            later_factor = call(later_factor_kernel, "later_factor", f32(vecs, vecs))(later_grams)
            copies, spread = call(
                between_kernel, "between", [bf16(col_devices, vecs, rows), bf16(vecs, rows)], VMEM
            )(own_part, first_parts, second_part, inv_root, later_factor)
            from_second = lax.all_gather(spread, "row", axis=0)
            from_first = exchange(copies, "col")
            row_roots = col_roots = None
    subspace, grams = call(
        last_kernel, "last", [f32(vecs, rows), f32(row_devices, vecs // 2, 2 * vecs)]
    )(own_part, first_parts, second_part, inv_root)
    grams = exchange(grams, "row")
    grams = call(relay_kernel, "relay", f32(col_devices, vecs // 2, 2 * vecs))(grams)
    grams = exchange(grams, "col")
    return call(
        functools.partial(final_kernel, all_devices * rows), "final", f32(vecs, rows)
    )(grams, subspace).T


def solution(mesh):
    return jax.shard_map(
        shards,
        mesh=mesh,
        in_specs=(P(("row", "col"), None), P(), P("row", "col", None), P("row", "col"), P()),
        out_specs=P(("row", "col"), None),
        check_vma=False,
    )
```

```python
import functools
import math

import jax
import jax.numpy as jnp
from jax import lax
from jax.experimental import pallas as pl
from jax.experimental.pallas import tpu as pltpu
from jax.sharding import PartitionSpec as P

ITERS = 2
LOG2E = math.log2(math.e)
VMEM = 60 * 1024 * 1024
SMALL = 24 * 1024 * 1024
HIGH = lax.Precision.HIGHEST
RIDGE = 1e-6


def lane_sums(values):
    part = values[:, :128]
    for start in range(128, values.shape[1], 128):
        part = part + values[:, start : start + 128]
    return jnp.sum(part.T, axis=0, keepdims=True)


def task_lists(slots):
    return 0, slots, 2 * slots, 3 * slots, 5 * slots


def live_step(step, lists, slots):
    return jnp.maximum(jnp.minimum(step, lists[5 * slots] - 1), 0)


def half_squares(rows):
    wide = rows.astype(jnp.float32)
    return wide * wide * (0.5 * LOG2E)


def tile_chunk(left, right, right_half):
    dots = lax.dot_general(
        left, right, (((1,), (1,)), ((), ())), preferred_element_type=jnp.float32
    )
    left_half = jnp.sum(half_squares(left), axis=1, keepdims=True)
    return jnp.exp2(dots * LOG2E - left_half - right_half)


def pack_row(row):
    return jnp.concatenate([row[:, i : i + 128] for i in range(0, row.shape[1], 128)], axis=0)


def unpack_row(block):
    return jnp.concatenate([block[i : i + 1, :] for i in range(block.shape[0])], axis=1)


def packed_gram(vectors):
    gram = lax.dot_general(
        vectors,
        vectors,
        (((1,), (1,)), ((), ())),
        precision=HIGH,
        preferred_element_type=jnp.float32,
    )
    half = gram.shape[0] // 2
    return jnp.concatenate([gram[:half], gram[half:]], axis=1)


def inverse_factor(packed, ridge):
    half, width = packed.shape
    size = 2 * half
    state = jnp.concatenate([packed, pltpu.roll(packed, size, 1)], axis=0)
    row_id = lax.broadcasted_iota(jnp.int32, state.shape, 0)
    lane_id = lax.broadcasted_iota(jnp.int32, state.shape, 1)
    state = jnp.where(lane_id < size, state, jnp.where(lane_id - size == row_id, 1.0, 0.0))
    if ridge:
        on_diagonal = lane_id == row_id
        trace = jnp.sum(jnp.where(on_diagonal, state, 0.0))
        state = jnp.where(on_diagonal, state + trace * (RIDGE / size), state)
    done = []
    for start in range(0, size, 8):
        columns = [
            jnp.broadcast_to(state[:, start + j : start + j + 1], state.shape) for j in range(8)
        ]
        row_id = lax.broadcasted_iota(jnp.int32, state.shape, 0)
        scale = jnp.zeros((8, width), jnp.float32)
        for j in range(8):
            column = columns[j]
            pivot = column[j : j + 1, :]
            scale = jnp.where(row_id[:8] == j, lax.rsqrt(pivot), scale)
            factor = jnp.where(row_id > j, column * (1.0 / pivot), 0.0)
            state = state - factor * state[j : j + 1, :]
            for m in range(j + 1, 8):
                columns[m] = columns[m] - factor * column[m : m + 1, :]
        done.append(state[:8] * scale)
        state = state[8:]
    full = jnp.concatenate(done, axis=0)
    return pltpu.roll(full, size, 1)[:, :size]


def transform(matrix, vectors):
    return jnp.dot(matrix, vectors, precision=HIGH, preferred_element_type=jnp.float32)


def call(kernel, name, out_shape, grant=SMALL):
    return pl.pallas_call(
        kernel,
        out_shape=out_shape,
        compiler_params=pltpu.CompilerParams(vmem_limit_bytes=grant),
        name=name,
    )


def f32(*shape):
    return jax.ShapeDtypeStruct(shape, jnp.float32)


def bf16(*shape):
    return jax.ShapeDtypeStruct(shape, jnp.bfloat16)


def seed_kernel_rows(seeds, block):
    dots = lax.dot_general(
        seeds, block, (((1,), (1,)), ((), ())), preferred_element_type=jnp.float32
    )
    seed_half = jnp.sum(half_squares(seeds), axis=1, keepdims=True)
    return jnp.exp2(dots * LOG2E - seed_half - lane_sums(half_squares(block)))


def start_kernel(seeds, own, start, grams):
    value = seed_kernel_rows(seeds[...], own[...])
    start[...] = value
    grams[...] = jnp.broadcast_to(packed_gram(value)[None], grams.shape)


def first_factor_kernel(grams, start, diagonal, own_degree, factor, subspace, later_gram):
    inverse = inverse_factor(jnp.sum(grams[...], axis=0), False)
    factor[...] = inverse
    value = transform(inverse, start[...])
    subspace[...] = value
    root = lax.rsqrt(own_degree[...])
    product = jnp.dot(
        (value * root).astype(jnp.bfloat16), diagonal[...], preferred_element_type=jnp.float32
    )
    later_gram[...] = packed_gram(product * root)


def later_factor_kernel(grams, factor):
    factor[...] = inverse_factor(jnp.sum(grams[...], axis=0), True)


def degree_kernel(own_degree, parts, roots, root):
    value = lax.rsqrt(jnp.sum(parts[...], axis=0) + pack_row(own_degree[...]))
    roots[...] = jnp.broadcast_to(value[None], roots.shape)
    root[...] = unpack_row(value)


def gathered(own_part, first_parts, second_part, root):
    total = own_part[...] + second_part[...].astype(jnp.float32)
    for index in range(first_parts.shape[0]):
        total = total + first_parts[index].astype(jnp.float32)
    return total * root[...]


def between_kernel(own_part, first_parts, second_part, root, factor, copies, spread):
    value = transform(factor[...], gathered(own_part, first_parts, second_part, root))
    value = (value * root[...]).astype(jnp.bfloat16)
    spread[...] = value
    copies[...] = jnp.broadcast_to(value[None], copies.shape)


def last_kernel(own_part, first_parts, second_part, root, subspace, grams):
    value = gathered(own_part, first_parts, second_part, root)
    subspace[...] = value
    grams[...] = jnp.broadcast_to(packed_gram(value)[None], grams.shape)


def final_kernel(points_all, grams, subspace, embedding):
    inverse = inverse_factor(jnp.sum(grams[...], axis=0), False)
    scaled = transform(inverse, subspace[...]) * math.sqrt(points_all)
    mean = jnp.mean(scaled * scaled, axis=0, keepdims=True)
    embedding[...] = scaled * lax.rsqrt(mean + 1e-06)


def relay_kernel(grams, copies):
    copies[...] = jnp.broadcast_to(jnp.sum(grams[...], axis=0)[None], copies.shape)


def vectors_kernel(slots, lists, block, seeds, factor, out):
    @pl.when(pl.program_id(0) < lists[5 * slots])
    def work():
        out[0] = transform(factor[...], seed_kernel_rows(seeds[...], block[0]))


def start_vectors(lists, slots, source, band, seeds, factor):
    unused, rows, depth = band.shape
    vecs = seeds.shape[0]
    return pl.pallas_call(
        functools.partial(vectors_kernel, slots),
        grid_spec=pltpu.PrefetchScalarGridSpec(
            num_scalar_prefetch=1,
            grid=(slots,),
            in_specs=[
                pl.BlockSpec(
                    (1, rows, depth), lambda s, t: (t[source + live_step(s, t, slots)], 0, 0)
                ),
                pl.BlockSpec((vecs, depth), lambda s, t: (0, 0)),
                pl.BlockSpec((vecs, vecs), lambda s, t: (0, 0)),
            ],
            out_specs=pl.BlockSpec(
                (1, vecs, rows), lambda s, t: (live_step(s, t, slots), 0, 0)
            ),
        ),
        out_shape=f32(slots, vecs, rows),
        compiler_params=pltpu.CompilerParams(vmem_limit_bytes=VMEM),
        name="start_vectors",
    )(lists, band, seeds, factor)


def form_kernel(chunk, slots, lists, left, right, tile, degrees):
    step = pl.program_id(0)

    @pl.when(step == 0)
    def clear():
        degrees[...] = jnp.zeros_like(degrees)

    @pl.when(step < lists[5 * slots])
    def work():
        rows = left.shape[1]
        right_rows = right[0]
        right_half = lane_sums(half_squares(right_rows))
        col_total = jnp.zeros((1, rows), jnp.float32)
        row_totals = []
        for start in range(0, rows, chunk):
            value = tile_chunk(left[0, start : start + chunk, :], right_rows, right_half)
            tile[0, start : start + chunk, :] = value.astype(jnp.bfloat16)
            col_total = col_total + jnp.sum(value, axis=0, keepdims=True)
            row_totals.append(lane_sums(value))
        left_owner = lists[3 * slots + 2 * step]
        right_owner = lists[3 * slots + 2 * step + 1]
        row_total = jnp.concatenate(row_totals, axis=1)
        degrees[left_owner] = degrees[left_owner] + pack_row(row_total)
        degrees[right_owner] = degrees[right_owner] + pack_row(col_total)


def form_tiles(lists, slots, row_band, col_band):
    col_devices, rows, depth = row_band.shape
    all_devices = col_devices * col_band.shape[0]
    firsts, unused, places, owners, live = task_lists(slots)

    return pl.pallas_call(
        functools.partial(form_kernel, min(256, rows), slots),
        grid_spec=pltpu.PrefetchScalarGridSpec(
            num_scalar_prefetch=1,
            grid=(slots,),
            in_specs=[
                pl.BlockSpec(
                    (1, rows, depth), lambda s, t: (t[firsts + live_step(s, t, slots)], 0, 0)
                ),
                pl.BlockSpec(
                    (1, rows, depth), lambda s, t: (t[places + live_step(s, t, slots)], 0, 0)
                ),
            ],
            out_specs=[
                pl.BlockSpec((1, rows, rows), lambda s, t: (live_step(s, t, slots), 0, 0)),
                pl.BlockSpec((all_devices, rows // 128, 128), lambda s, t: (0, 0, 0)),
            ],
        ),
        out_shape=[bf16(slots, rows, rows), f32(all_devices, rows // 128, 128)],
        compiler_params=pltpu.CompilerParams(vmem_limit_bytes=VMEM),
        name="form_tiles",
    )(lists, row_band, col_band)


def diagonal_kernel(chunk, own, tile, degree):
    rows = own.shape[0]
    right_rows = own[...]
    right_half = lane_sums(half_squares(right_rows))
    total = jnp.zeros((1, rows), jnp.float32)
    for start in range(0, rows, chunk):
        value = tile_chunk(own[start : start + chunk, :], right_rows, right_half)
        tile[start : start + chunk, :] = value.astype(jnp.bfloat16)
        total = total + jnp.sum(value, axis=0, keepdims=True)
    degree[...] = total


def form_diagonal(own):
    rows = own.shape[0]
    return pl.pallas_call(
        functools.partial(diagonal_kernel, min(256, rows)),
        out_shape=[
            jax.ShapeDtypeStruct((rows, rows), jnp.bfloat16),
            jax.ShapeDtypeStruct((1, rows), jnp.float32),
        ],
        compiler_params=pltpu.CompilerParams(vmem_limit_bytes=SMALL),
        name="form_diagonal",
    )(own)


def apply_kernel(contract, slots, target, lists, tile, vectors, *rest):
    step = pl.program_id(0)
    roots, out = rest if len(rest) == 2 else (None,) + rest

    @pl.when(step == 0)
    def clear():
        out[...] = jnp.zeros_like(out)

    @pl.when(step < lists[5 * slots])
    def work():
        slot = lists[target + step]
        block = vectors[0]
        if roots is not None:
            block = (block * unpack_row(roots[0])).astype(jnp.bfloat16)
        product = lax.dot_general(
            block, tile[0], (((1,), (contract,)), ((), ())), preferred_element_type=jnp.float32
        )
        out[slot] = (out[slot].astype(jnp.float32) + product).astype(jnp.bfloat16)


def apply_tiles(contract, lists, source, target, tiles, vectors, roots, targets):
    slots, rows, unused = tiles.shape
    vecs = vectors.shape[1]

    def by_task(s, t):
        return (live_step(s, t, slots), 0, 0)

    def by_block(s, t):
        return (t[source + live_step(s, t, slots)], 0, 0)

    in_specs = [
        pl.BlockSpec((1, rows, rows), by_task),
        pl.BlockSpec((1, vecs, rows), by_block if roots is None else by_task),
    ]
    operands = [tiles, vectors]
    if roots is not None:
        in_specs.append(pl.BlockSpec((1, rows // 128, 128), by_block))
        operands.append(roots)
    return pl.pallas_call(
        functools.partial(apply_kernel, contract, slots, target),
        grid_spec=pltpu.PrefetchScalarGridSpec(
            num_scalar_prefetch=1,
            grid=(slots,),
            in_specs=in_specs,
            out_specs=pl.BlockSpec((targets, vecs, rows), lambda s, t: (0, 0, 0)),
        ),
        out_shape=bf16(targets, vecs, rows),
        compiler_params=pltpu.CompilerParams(vmem_limit_bytes=VMEM),
        name="apply_tiles",
    )(lists, *operands)


def spread_to(array, axis):
    devices = lax.axis_size(axis)
    copies = jnp.broadcast_to(array[None], (devices,) + array.shape)
    return lax.all_to_all(copies, axis, 0, 0, tiled=True)


def exchange(copies, axis):
    return lax.all_to_all(copies, axis, 0, 0, tiled=True)


def together(*arrays):
    return lax.optimization_barrier(arrays)


def place_in_row(index, here):
    apart = (index // 2 - here // 2 + 4) % 4
    order = jnp.where(apart == 0, 0, jnp.where(apart == 3, 1, jnp.where(apart == 1, 2, 3)))
    return order + 4 * ((index + here) % 2)


def assign_kernel(slots, cols, here, table, lists):
    devices = table.shape[1]
    me = here[0]
    filler = jnp.zeros((devices - table.shape[0], devices), jnp.float32)
    by_device = jnp.concatenate([table[...], filler], axis=0).T
    device = lax.broadcasted_iota(jnp.int32, (devices, devices), 0)
    lane = lax.broadcasted_iota(jnp.int32, (devices, devices), 1)
    same = jnp.where(device == lane, 1.0, 0.0)
    count = by_device[:, slots : slots + 1]
    load = jnp.zeros((1, devices), jnp.float32)
    moves = []
    taken = []
    listed = []
    for slot in range(slots):
        partner = by_device[:, slot : slot + 1]
        is_listed = jnp.where(count > slot, 1.0, 0.0)
        picks = jnp.where(lane.astype(jnp.float32) == partner, 1.0, 0.0)
        move = (picks - same) * is_listed
        apart = jnp.sum(move * load, axis=1, keepdims=True)
        take = jnp.where(apart <= 0, is_listed, 0.0)
        load = load + jnp.sum(same * is_listed + move * take, axis=0, keepdims=True)
        moves.append(move)
        taken.append(take)
        listed.append(is_listed)
    for slot in range(slots):
        apart = jnp.sum(moves[slot] * load, axis=1, keepdims=True)
        give = jnp.where(apart < -1, listed[slot] * (1.0 - taken[slot]), 0.0)
        back = jnp.where(apart > 1, taken[slot], 0.0)
        load = load + jnp.sum(moves[slot] * (give - back), axis=0, keepdims=True)
        taken[slot] = taken[slot] + give - back
    shared = jnp.where(jnp.max(load) <= slots, 1.0, 0.0)
    code = jnp.zeros((devices, devices), jnp.float32)
    number = device.astype(jnp.float32)
    for slot in range(slots):
        partner = by_device[:, slot : slot + 1]
        take = taken[slot] * shared
        kept = jnp.where(device == me, listed[slot] - take, 0.0)
        come = jnp.where(partner == me.astype(jnp.float32), take, 0.0)
        other = kept * partner + come * number
        cell = (kept + come) * (number * slots + (slot + 1)) * devices + other
        code = jnp.where(lane == slot, cell, code)
    lists[5 * slots] = jnp.sum(jnp.where(code > 0, 1.0, 0.0)).astype(jnp.int32)
    for slot in range(slots):
        top = jnp.max(code)
        partner = lax.rem(top.astype(jnp.int32), devices)
        code = jnp.where(code == top, 0.0, code)
        first_slot = lax.rem(partner, cols)
        second_slot = lax.div(partner, cols)
        lists[slot] = first_slot
        lists[slots + slot] = second_slot
        lists[2 * slots + slot] = place_in_row(second_slot, lax.div(me, cols))
        lists[3 * slots + 2 * slot] = lax.div(me, cols) * cols + first_slot
        lists[3 * slots + 2 * slot + 1] = second_slot * cols + lax.rem(me, cols)


def assign_tasks(self_index, table, slots, cols):
    smem = pl.BlockSpec(memory_space=pltpu.SMEM)
    return pl.pallas_call(
        functools.partial(assign_kernel, slots, cols),
        in_specs=[smem, pl.BlockSpec(memory_space=pltpu.VMEM)],
        out_specs=smem,
        out_shape=jax.ShapeDtypeStruct((6 * slots,), jnp.int32),
        compiler_params=pltpu.CompilerParams(vmem_limit_bytes=SMALL),
        name="assign_tasks",
    )(self_index.reshape(1), table)


def shards(points, feature_scale, tile_tasks, task_count, seed_ids):
    rows = points.shape[0]
    vecs = seed_ids.shape[0]
    row_devices = lax.axis_size("row")
    col_devices = lax.axis_size("col")
    all_devices = row_devices * col_devices
    self_index = lax.axis_index("row") * col_devices + lax.axis_index("col")
    weighted = (points.astype(jnp.float32) * feature_scale[None, :]).astype(jnp.bfloat16)
    row_band = lax.all_gather(weighted, "col", axis=0)
    listed = tile_tasks.reshape(-1)
    slots = listed.shape[0]

    def shift(array, by):
        return lax.ppermute(
            array, "row", [(i, (i + by) % row_devices) for i in range(row_devices)]
        )

    local_seed = seed_ids - self_index * rows
    inside = (local_seed >= 0) & (local_seed < rows)
    picked = jnp.where(
        inside[:, None], jnp.take(weighted, jnp.clip(local_seed, 0, rows - 1), axis=0), 0
    ).astype(jnp.bfloat16)
    own_line = jnp.concatenate(
        [listed, task_count.reshape(-1), jnp.zeros((slots - 1,), jnp.int32)]
    )
    lines = jnp.where(
        (jnp.arange(weighted.shape[1]) == self_index)[None, :], own_line[:, None], 0
    ).astype(jnp.bfloat16)
    picked = jnp.concatenate([picked, lines], axis=0)
    seed_parts = spread_to(picked, "row")
    before = shift(weighted, 2)
    after = shift(weighted, -2)
    before, after, seed_parts = together(before, after, seed_parts)
    half = rows // 2
    across_low = shift(before[:half], 2)
    across_high = shift(after[half:], -2)
    seed_parts = spread_to(jnp.sum(seed_parts, axis=0), "col")
    diagonal, own_degree = form_diagonal(weighted)
    seed_sum = jnp.sum(seed_parts, axis=0)
    seeds = seed_sum[:vecs]
    table = seed_sum[vecs:, :all_devices].astype(jnp.float32)
    start, grams = call(
        start_kernel, "start", [f32(vecs, rows), f32(row_devices, vecs // 2, 2 * vecs)]
    )(seeds, weighted)
    across_low, across_high, grams = together(across_low, across_high, grams)
    grams = exchange(grams, "row")
    across = jnp.concatenate([across_low, across_high], axis=0)
    mine = jnp.stack([weighted, before, after, across])
    mine, grams = together(mine, grams)
    other = lax.ppermute(mine, "row", [(i, i ^ 1) for i in range(row_devices)])
    grams = call(relay_kernel, "relay", f32(col_devices, vecs // 2, 2 * vecs))(grams)
    grams = exchange(grams, "col")
    lists = assign_tasks(self_index, table, slots, col_devices)
    firsts, seconds, places, unused, unused = task_lists(slots)
    col_band, grams = together(jnp.concatenate([mine, other], axis=0), grams)
    factor, subspace, later_gram = call(
        first_factor_kernel,
        "first_factor",
        [f32(vecs, vecs), f32(vecs, rows), f32(vecs // 2, 2 * vecs)],
    )(grams, start, diagonal, own_degree)
    later_grams = lax.all_gather(later_gram, ("row", "col"), axis=0)

    tiles, degrees = form_tiles(lists, slots, row_band, col_band)
    roots, inv_root = call(
        degree_kernel, "degree", [f32(col_devices, rows // 128, 128), f32(1, rows)]
    )(own_degree, exchange(degrees, ("row", "col")))
    row_roots = exchange(roots, "col")
    from_first = start_vectors(lists, slots, firsts, row_band, seeds, factor)
    row_roots, from_first, roots = together(row_roots, from_first, roots)
    col_roots = exchange(roots[:row_devices], "row")
    from_second = start_vectors(lists, slots, places, col_band, seeds, factor)
    row_roots, col_roots, from_second = together(row_roots, col_roots, from_second)
    spread = (subspace * inv_root).astype(jnp.bfloat16)
    for iteration in range(ITERS):
        own_part = lax.dot_general(
            spread, diagonal, (((1,), (0,)), ((), ())), preferred_element_type=jnp.float32
        )
        to_second = apply_tiles(
            0, lists, firsts, seconds, tiles, from_first, row_roots, row_devices
        )
        to_second, from_second = together(to_second, from_second)
        second_part = lax.psum_scatter(to_second, "row", scatter_dimension=0, tiled=False)
        to_first = apply_tiles(
            1, lists, seconds, firsts, tiles, from_second, col_roots, col_devices
        )
        first_parts = exchange(to_first, "col")
        if iteration + 1 < ITERS:
            later_factor = call(later_factor_kernel, "later_factor", f32(vecs, vecs))(later_grams)
            copies, spread = call(
                between_kernel, "between", [bf16(col_devices, vecs, rows), bf16(vecs, rows)], VMEM
            )(own_part, first_parts, second_part, inv_root, later_factor)
            from_second = lax.all_gather(spread, "row", axis=0)
            from_first = exchange(copies, "col")
            row_roots = col_roots = None
    subspace, grams = call(
        last_kernel, "last", [f32(vecs, rows), f32(row_devices, vecs // 2, 2 * vecs)]
    )(own_part, first_parts, second_part, inv_root)
    grams = exchange(grams, "row")
    grams = call(relay_kernel, "relay", f32(col_devices, vecs // 2, 2 * vecs))(grams)
    grams = exchange(grams, "col")
    return call(
        functools.partial(final_kernel, all_devices * rows), "final", f32(vecs, rows)
    )(grams, subspace).T


def solution(mesh):
    return jax.shard_map(
        shards,
        mesh=mesh,
        in_specs=(P(("row", "col"), None), P(), P("row", "col", None), P("row", "col"), P()),
        out_specs=P(("row", "col"), None),
        check_vma=False,
    )
```

```python
import functools
import math

import jax
import jax.numpy as jnp
from jax import lax
from jax.experimental import pallas as pl
from jax.experimental.pallas import tpu as pltpu
from jax.sharding import PartitionSpec as P

ITERS = 2
LOG2E = math.log2(math.e)
VMEM = 60 * 1024 * 1024
SMALL = 24 * 1024 * 1024
HIGH = lax.Precision.HIGHEST
RIDGE = 1e-6


def lane_sums(values):
    part = values[:, :128]
    for start in range(128, values.shape[1], 128):
        part = part + values[:, start : start + 128]
    return jnp.sum(part.T, axis=0, keepdims=True)


def task_lists(slots):
    return 0, slots, 2 * slots, 3 * slots, 5 * slots


def live_step(step, lists, slots):
    return jnp.maximum(jnp.minimum(step, lists[5 * slots] - 1), 0)


def half_squares(rows):
    wide = rows.astype(jnp.float32)
    return wide * wide * (0.5 * LOG2E)


def tile_chunk(left, right, right_half):
    dots = lax.dot_general(
        left, right, (((1,), (1,)), ((), ())), preferred_element_type=jnp.float32
    )
    left_half = jnp.sum(half_squares(left), axis=1, keepdims=True)
    return jnp.exp2(dots * LOG2E - left_half - right_half)


def packed_gram(vectors):
    gram = lax.dot_general(
        vectors,
        vectors,
        (((1,), (1,)), ((), ())),
        precision=HIGH,
        preferred_element_type=jnp.float32,
    )
    half = gram.shape[0] // 2
    return jnp.concatenate([gram[:half], gram[half:]], axis=1)


def inverse_factor(packed, ridge):
    half, width = packed.shape
    size = 2 * half
    state = jnp.concatenate([packed, pltpu.roll(packed, size, 1)], axis=0)
    row_id = lax.broadcasted_iota(jnp.int32, state.shape, 0)
    lane_id = lax.broadcasted_iota(jnp.int32, state.shape, 1)
    state = jnp.where(lane_id < size, state, jnp.where(lane_id - size == row_id, 1.0, 0.0))
    if ridge:
        on_diagonal = lane_id == row_id
        trace = jnp.sum(jnp.where(on_diagonal, state, 0.0))
        state = jnp.where(on_diagonal, state + trace * (RIDGE / size), state)
    done = []
    for start in range(0, size, 8):
        columns = [
            jnp.broadcast_to(state[:, start + j : start + j + 1], state.shape) for j in range(8)
        ]
        row_id = lax.broadcasted_iota(jnp.int32, state.shape, 0)
        scale = jnp.zeros((8, width), jnp.float32)
        for j in range(8):
            column = columns[j]
            pivot = column[j : j + 1, :]
            scale = jnp.where(row_id[:8] == j, lax.rsqrt(pivot), scale)
            factor = jnp.where(row_id > j, column * (1.0 / pivot), 0.0)
            state = state - factor * state[j : j + 1, :]
            for m in range(j + 1, 8):
                columns[m] = columns[m] - factor * column[m : m + 1, :]
        done.append(state[:8] * scale)
        state = state[8:]
    full = jnp.concatenate(done, axis=0)
    return pltpu.roll(full, size, 1)[:, :size]


def transform(matrix, vectors):
    return jnp.dot(matrix, vectors, precision=HIGH, preferred_element_type=jnp.float32)


def call(kernel, name, out_shape, grant=SMALL):
    return pl.pallas_call(
        kernel,
        out_shape=out_shape,
        compiler_params=pltpu.CompilerParams(vmem_limit_bytes=grant),
        name=name,
    )


def f32(*shape):
    return jax.ShapeDtypeStruct(shape, jnp.float32)


def bf16(*shape):
    return jax.ShapeDtypeStruct(shape, jnp.bfloat16)


def seed_kernel_rows(seeds, block):
    dots = lax.dot_general(
        seeds, block, (((1,), (1,)), ((), ())), preferred_element_type=jnp.float32
    )
    seed_half = jnp.sum(half_squares(seeds), axis=1, keepdims=True)
    return jnp.exp2(dots * LOG2E - seed_half - lane_sums(half_squares(block)))


def start_kernel(seeds, own, start, grams):
    value = seed_kernel_rows(seeds[...], own[...])
    start[...] = value
    grams[...] = jnp.broadcast_to(packed_gram(value)[None], grams.shape)


def first_factor_kernel(grams, start, diagonal, own_degree, factor, subspace, later_gram):
    inverse = inverse_factor(jnp.sum(grams[...], axis=0), False)
    factor[...] = inverse
    value = transform(inverse, start[...])
    subspace[...] = value
    root = lax.rsqrt(own_degree[...])
    product = jnp.dot(
        (value * root).astype(jnp.bfloat16), diagonal[...], preferred_element_type=jnp.float32
    )
    later_gram[...] = packed_gram(product * root)


def later_factor_kernel(gram_rows, factor):
    factor[...] = inverse_factor(gram_rows[:, 0, :], True)


def later_factor(lines, vecs):
    half, width = vecs // 2, 2 * vecs
    place = lines.shape[2] // width - 1
    return pl.pallas_call(
        later_factor_kernel,
        grid=(1,),
        in_specs=[pl.BlockSpec((half, 1, width), lambda s: (0, 0, place))],
        out_specs=pl.BlockSpec((vecs, vecs), lambda s: (0, 0)),
        out_shape=f32(vecs, vecs),
        compiler_params=pltpu.CompilerParams(vmem_limit_bytes=SMALL),
        name="later_factor",
    )(lines)


def degree_kernel(own_degree, parts, copies, root):
    points = root.shape[1]
    total = jnp.sum(parts[...], axis=0)
    value = lax.rsqrt(total[:, :points] + own_degree[...])
    root[...] = value
    copies[...] = jnp.broadcast_to(
        jnp.concatenate([value, total[:, points:]], axis=1)[None], copies.shape
    )


def gathered(own_part, first_parts, second_part, root):
    total = own_part[...] + second_part[...].astype(jnp.float32)
    for index in range(first_parts.shape[0]):
        total = total + first_parts[index].astype(jnp.float32)
    return total * root[...]


def between_kernel(own_part, first_parts, second_part, root, factor, copies, spread):
    value = transform(factor[...], gathered(own_part, first_parts, second_part, root))
    value = (value * root[...]).astype(jnp.bfloat16)
    spread[...] = value
    copies[...] = jnp.broadcast_to(value[None], copies.shape)


def between(own_part, first_parts, second_part, root, factor):
    copies, vecs, rows = first_parts.shape
    return call(
        between_kernel, "between", [bf16(copies, vecs, rows), bf16(vecs, rows)], VMEM
    )(own_part, first_parts, second_part, root, factor)


def last_kernel(own_part, first_parts, second_part, root, subspace, grams):
    value = gathered(own_part, first_parts, second_part, root)
    subspace[...] = value
    grams[...] = jnp.broadcast_to(packed_gram(value)[None], grams.shape)


def final_kernel(points_all, grams, subspace, embedding):
    inverse = inverse_factor(jnp.sum(grams[...], axis=0), False)
    scaled = transform(inverse, subspace[...]) * math.sqrt(points_all)
    mean = jnp.mean(scaled * scaled, axis=0, keepdims=True)
    embedding[...] = scaled * lax.rsqrt(mean + 1e-06)


def relay_kernel(grams, copies):
    copies[...] = jnp.broadcast_to(jnp.sum(grams[...], axis=0)[None], copies.shape)


def vectors_kernel(slots, lists, block, seeds, factor, out):
    @pl.when(pl.program_id(0) < lists[5 * slots])
    def work():
        out[0] = transform(factor[...], seed_kernel_rows(seeds[...], block[0]))


def start_vectors(lists, slots, source, band, seeds, factor):
    unused, rows, depth = band.shape
    vecs = seeds.shape[0]
    return pl.pallas_call(
        functools.partial(vectors_kernel, slots),
        grid_spec=pltpu.PrefetchScalarGridSpec(
            num_scalar_prefetch=1,
            grid=(slots,),
            in_specs=[
                pl.BlockSpec(
                    (1, rows, depth), lambda s, t: (t[source + live_step(s, t, slots)], 0, 0)
                ),
                pl.BlockSpec((vecs, depth), lambda s, t: (0, 0)),
                pl.BlockSpec((vecs, vecs), lambda s, t: (0, 0)),
            ],
            out_specs=pl.BlockSpec(
                (1, vecs, rows), lambda s, t: (live_step(s, t, slots), 0, 0)
            ),
        ),
        out_shape=f32(slots, vecs, rows),
        compiler_params=pltpu.CompilerParams(vmem_limit_bytes=VMEM),
        cost_estimate=pl.CostEstimate(
            flops=4_000_000_000, bytes_accessed=10_000_000, transcendentals=0
        ),
        name="start_vectors",
    )(lists, band, seeds, factor)


def form_kernel(chunk, slots, lists, left, right, gram, tile, lines):
    step = pl.program_id(0)
    points = left.shape[1]

    @pl.when(step == 0)
    def clear():
        lines[...] = jnp.zeros_like(lines)
        for index in range(gram.shape[0]):
            lines[index, :, points:] = gram[index : index + 1, :]

    @pl.when(step < lists[5 * slots])
    def work():
        rows = left.shape[1]
        right_rows = right[0]
        right_half = lane_sums(half_squares(right_rows))
        col_total = jnp.zeros((1, rows), jnp.float32)
        row_totals = []
        for start in range(0, rows, chunk):
            value = tile_chunk(left[0, start : start + chunk, :], right_rows, right_half)
            tile[0, start : start + chunk, :] = value.astype(jnp.bfloat16)
            col_total = col_total + jnp.sum(value, axis=0, keepdims=True)
            row_totals.append(lane_sums(value))
        left_owner = lists[3 * slots + 2 * step]
        right_owner = lists[3 * slots + 2 * step + 1]
        row_total = jnp.concatenate(row_totals, axis=1)
        lines[left_owner, :, :points] = lines[left_owner, :, :points] + row_total
        lines[right_owner, :, :points] = lines[right_owner, :, :points] + col_total


def form_tiles(lists, slots, row_band, col_band, gram):
    col_devices, rows, depth = row_band.shape
    line = (col_devices * col_band.shape[0], 1, rows + gram.shape[1])
    firsts, unused, places, owners, live = task_lists(slots)

    return pl.pallas_call(
        functools.partial(form_kernel, min(256, rows), slots),
        grid_spec=pltpu.PrefetchScalarGridSpec(
            num_scalar_prefetch=1,
            grid=(slots,),
            in_specs=[
                pl.BlockSpec(
                    (1, rows, depth), lambda s, t: (t[firsts + live_step(s, t, slots)], 0, 0)
                ),
                pl.BlockSpec(
                    (1, rows, depth), lambda s, t: (t[places + live_step(s, t, slots)], 0, 0)
                ),
                pl.BlockSpec(gram.shape, lambda s, t: (0, 0)),
            ],
            out_specs=[
                pl.BlockSpec((1, rows, rows), lambda s, t: (live_step(s, t, slots), 0, 0)),
                pl.BlockSpec(line, lambda s, t: (0, 0, 0)),
            ],
        ),
        out_shape=[bf16(slots, rows, rows), f32(*line)],
        compiler_params=pltpu.CompilerParams(vmem_limit_bytes=VMEM),
        name="form_tiles",
    )(lists, row_band, col_band, gram)


def diagonal_kernel(chunk, own, tile, degree):
    rows = own.shape[0]
    right_rows = own[...]
    right_half = lane_sums(half_squares(right_rows))
    total = jnp.zeros((1, rows), jnp.float32)
    for start in range(0, rows, chunk):
        value = tile_chunk(own[start : start + chunk, :], right_rows, right_half)
        tile[start : start + chunk, :] = value.astype(jnp.bfloat16)
        total = total + jnp.sum(value, axis=0, keepdims=True)
    degree[...] = total


def form_diagonal(own):
    rows = own.shape[0]
    return pl.pallas_call(
        functools.partial(diagonal_kernel, min(256, rows)),
        out_shape=[
            jax.ShapeDtypeStruct((rows, rows), jnp.bfloat16),
            jax.ShapeDtypeStruct((1, rows), jnp.float32),
        ],
        compiler_params=pltpu.CompilerParams(vmem_limit_bytes=SMALL),
        name="form_diagonal",
    )(own)


def apply_kernel(slots, lists, tile, left, right, *rest):
    step = pl.program_id(0)
    left_roots, right_roots, to_first, to_second = rest if len(rest) == 4 else (None, None) + rest

    def scaled(vectors, roots):
        if roots is None:
            return vectors[0]
        return (vectors[0] * roots[0, :, : vectors.shape[2]]).astype(jnp.bfloat16)

    def add(out, slot, vectors, contract):
        product = lax.dot_general(
            vectors, tile[0], (((1,), (contract,)), ((), ())), preferred_element_type=jnp.float32
        )
        out[slot] = (out[slot].astype(jnp.float32) + product).astype(jnp.bfloat16)

    @pl.when(step == 0)
    def clear():
        to_first[...] = jnp.zeros_like(to_first)
        to_second[...] = jnp.zeros_like(to_second)

    @pl.when(step < lists[5 * slots])
    def work():
        add(to_second, lists[slots + step], scaled(left, left_roots), 0)
        add(to_first, lists[step], scaled(right, right_roots), 1)


def apply_tiles(lists, tiles, from_first, from_second, roots, col_devices, row_devices):
    slots, rows, unused = tiles.shape
    vecs = from_first.shape[1]

    def by_task(s, t):
        return (live_step(s, t, slots), 0, 0)

    def by_first(s, t):
        return (t[live_step(s, t, slots)], 0, 0)

    def by_second(s, t):
        return (t[slots + live_step(s, t, slots)], 0, 0)

    def by_owner(side):
        return lambda s, t: (t[3 * slots + 2 * live_step(s, t, slots) + side], 0, 0)

    block = (1, vecs, rows)
    by_slot = roots is not None
    in_specs = [
        pl.BlockSpec((1, rows, rows), by_task),
        pl.BlockSpec(block, by_task if by_slot else by_first),
        pl.BlockSpec(block, by_task if by_slot else by_second),
    ]
    operands = [lists, tiles, from_first, from_second]
    if by_slot:
        for side in range(2):
            in_specs.append(pl.BlockSpec((1,) + roots.shape[1:], by_owner(side)))
            operands.append(roots)
    return pl.pallas_call(
        functools.partial(apply_kernel, slots),
        grid_spec=pltpu.PrefetchScalarGridSpec(
            num_scalar_prefetch=1,
            grid=(slots,),
            in_specs=in_specs,
            out_specs=[
                pl.BlockSpec((col_devices, vecs, rows), lambda s, t: (0, 0, 0)),
                pl.BlockSpec((row_devices, vecs, rows), lambda s, t: (0, 0, 0)),
            ],
        ),
        out_shape=[bf16(col_devices, vecs, rows), bf16(row_devices, vecs, rows)],
        compiler_params=pltpu.CompilerParams(vmem_limit_bytes=VMEM),
        name="apply_tiles",
    )(*operands)


def spread_to(array, axis):
    devices = lax.axis_size(axis)
    copies = jnp.broadcast_to(array[None], (devices,) + array.shape)
    return lax.all_to_all(copies, axis, 0, 0, tiled=True)


def exchange(copies, axis):
    return lax.all_to_all(copies, axis, 0, 0, tiled=True)


def together(*arrays):
    return lax.optimization_barrier(arrays)


def place_in_row(index, here):
    apart = (index // 2 - here // 2 + 4) % 4
    order = jnp.where(apart == 0, 0, jnp.where(apart == 3, 1, jnp.where(apart == 1, 2, 3)))
    return order + 4 * ((index + here) % 2)


def assign_kernel(slots, cols, here, table, lists):
    devices = table.shape[1]
    me = here[0]
    filler = jnp.zeros((devices - table.shape[0], devices), jnp.float32)
    by_device = jnp.concatenate([table[...], filler], axis=0).T
    device = lax.broadcasted_iota(jnp.int32, (devices, devices), 0)
    lane = lax.broadcasted_iota(jnp.int32, (devices, devices), 1)
    same = jnp.where(device == lane, 1.0, 0.0)
    count = by_device[:, slots : slots + 1]
    load = jnp.zeros((1, devices), jnp.float32)
    moves = []
    taken = []
    listed = []
    for slot in range(slots):
        partner = by_device[:, slot : slot + 1]
        is_listed = jnp.where(count > slot, 1.0, 0.0)
        picks = jnp.where(lane.astype(jnp.float32) == partner, 1.0, 0.0)
        move = (picks - same) * is_listed
        apart = jnp.sum(move * load, axis=1, keepdims=True)
        take = jnp.where(apart <= 0, is_listed, 0.0)
        load = load + jnp.sum(same * is_listed + move * take, axis=0, keepdims=True)
        moves.append(move)
        taken.append(take)
        listed.append(is_listed)
    for slot in range(slots):
        apart = jnp.sum(moves[slot] * load, axis=1, keepdims=True)
        give = jnp.where(apart < -1, listed[slot] * (1.0 - taken[slot]), 0.0)
        back = jnp.where(apart > 1, taken[slot], 0.0)
        load = load + jnp.sum(moves[slot] * (give - back), axis=0, keepdims=True)
        taken[slot] = taken[slot] + give - back
    shared = jnp.where(jnp.max(load) <= slots, 1.0, 0.0)
    code = jnp.zeros((devices, devices), jnp.float32)
    number = device.astype(jnp.float32)
    for slot in range(slots):
        partner = by_device[:, slot : slot + 1]
        take = taken[slot] * shared
        kept = jnp.where(device == me, listed[slot] - take, 0.0)
        come = jnp.where(partner == me.astype(jnp.float32), take, 0.0)
        other = kept * partner + come * number
        cell = (kept + come) * (number * slots + (slot + 1)) * devices + other
        code = jnp.where(lane == slot, cell, code)
    lists[5 * slots] = jnp.sum(jnp.where(code > 0, 1.0, 0.0)).astype(jnp.int32)
    for slot in range(slots):
        top = jnp.max(code)
        partner = lax.rem(top.astype(jnp.int32), devices)
        code = jnp.where(code == top, 0.0, code)
        first_slot = lax.rem(partner, cols)
        second_slot = lax.div(partner, cols)
        lists[slot] = first_slot
        lists[slots + slot] = second_slot
        lists[2 * slots + slot] = place_in_row(second_slot, lax.div(me, cols))
        lists[3 * slots + 2 * slot] = lax.div(me, cols) * cols + first_slot
        lists[3 * slots + 2 * slot + 1] = second_slot * cols + lax.rem(me, cols)


def assign_tasks(self_index, table, slots, cols):
    smem = pl.BlockSpec(memory_space=pltpu.SMEM)
    return pl.pallas_call(
        functools.partial(assign_kernel, slots, cols),
        in_specs=[smem, pl.BlockSpec(memory_space=pltpu.VMEM)],
        out_specs=smem,
        out_shape=jax.ShapeDtypeStruct((6 * slots,), jnp.int32),
        compiler_params=pltpu.CompilerParams(vmem_limit_bytes=SMALL),
        name="assign_tasks",
    )(self_index.reshape(1), table)


def shards(points, feature_scale, tile_tasks, task_count, seed_ids):
    rows = points.shape[0]
    vecs = seed_ids.shape[0]
    row_devices = lax.axis_size("row")
    col_devices = lax.axis_size("col")
    all_devices = row_devices * col_devices
    self_index = lax.axis_index("row") * col_devices + lax.axis_index("col")
    weighted = (points.astype(jnp.float32) * feature_scale[None, :]).astype(jnp.bfloat16)
    row_band = lax.all_gather(weighted, "col", axis=0)
    listed = tile_tasks.reshape(-1)
    slots = listed.shape[0]

    def shift(array, by):
        return lax.ppermute(
            array, "row", [(i, (i + by) % row_devices) for i in range(row_devices)]
        )

    local_seed = seed_ids - self_index * rows
    inside = (local_seed >= 0) & (local_seed < rows)
    picked = jnp.where(
        inside[:, None], jnp.take(weighted, jnp.clip(local_seed, 0, rows - 1), axis=0), 0
    ).astype(jnp.bfloat16)
    own_line = jnp.concatenate(
        [listed, task_count.reshape(-1), jnp.zeros((slots - 1,), jnp.int32)]
    )
    lines = jnp.where(
        (jnp.arange(weighted.shape[1]) == self_index)[None, :], own_line[:, None], 0
    ).astype(jnp.bfloat16)
    picked = jnp.concatenate([picked, lines], axis=0)
    seed_parts = spread_to(picked, "row")
    before = shift(weighted, 2)
    after = shift(weighted, -2)
    before, after, seed_parts = together(before, after, seed_parts)
    half = rows // 2
    across_low = shift(before[:half], 2)
    across_high = shift(after[half:], -2)
    seed_parts = spread_to(jnp.sum(seed_parts, axis=0), "col")
    diagonal, own_degree = form_diagonal(weighted)
    seed_sum = jnp.sum(seed_parts, axis=0)
    seeds = seed_sum[:vecs]
    table = seed_sum[vecs:, :all_devices].astype(jnp.float32)
    start, grams = call(
        start_kernel, "start", [f32(vecs, rows), f32(row_devices, vecs // 2, 2 * vecs)]
    )(seeds, weighted)
    across_low, across_high, grams = together(across_low, across_high, grams)
    grams = exchange(grams, "row")
    across = jnp.concatenate([across_low, across_high], axis=0)
    mine = jnp.stack([weighted, before, after, across])
    mine, grams = together(mine, grams)
    other = lax.ppermute(mine, "row", [(i, i ^ 1) for i in range(row_devices)])
    grams = call(relay_kernel, "relay", f32(col_devices, vecs // 2, 2 * vecs))(grams)
    grams = exchange(grams, "col")
    lists = assign_tasks(self_index, table, slots, col_devices)
    firsts, seconds, places, unused, unused = task_lists(slots)
    col_band, grams = together(jnp.concatenate([mine, other], axis=0), grams)
    factor, subspace, later_gram = call(
        first_factor_kernel,
        "first_factor",
        [f32(vecs, vecs), f32(vecs, rows), f32(vecs // 2, 2 * vecs)],
    )(grams, start, diagonal, own_degree)

    tiles, lines = form_tiles(lists, slots, row_band, col_band, later_gram)
    copies, inv_root = call(degree_kernel, "degree", [f32(*lines.shape), f32(1, rows)])(
        own_degree, exchange(lines, ("row", "col"))
    )
    lines = exchange(copies, ("row", "col"))
    roots = lines
    from_first = start_vectors(lists, slots, firsts, row_band, seeds, factor)
    from_second = start_vectors(lists, slots, places, col_band, seeds, factor)
    spread = (subspace * inv_root).astype(jnp.bfloat16)
    for iteration in range(ITERS):
        own_part = lax.dot_general(
            spread, diagonal, (((1,), (0,)), ((), ())), preferred_element_type=jnp.float32
        )
        to_first, to_second = apply_tiles(
            lists, tiles, from_first, from_second, roots, col_devices, row_devices
        )
        second_part = lax.psum_scatter(to_second, "row", scatter_dimension=0, tiled=False)
        first_parts = exchange(to_first, "col")
        if iteration + 1 < ITERS:
            copies, spread = between(
                own_part, first_parts, second_part, inv_root, later_factor(lines, vecs)
            )
            from_second = lax.all_gather(spread, "row", axis=0)
            from_first = exchange(copies, "col")
            roots = None
    subspace, grams = call(
        last_kernel, "last", [f32(vecs, rows), f32(row_devices, vecs // 2, 2 * vecs)]
    )(own_part, first_parts, second_part, inv_root)
    grams = exchange(grams, "row")
    grams = call(relay_kernel, "relay", f32(col_devices, vecs // 2, 2 * vecs))(grams)
    grams = exchange(grams, "col")
    return call(
        functools.partial(final_kernel, all_devices * rows), "final", f32(vecs, rows)
    )(grams, subspace).T


def solution(mesh):
    return jax.shard_map(
        shards,
        mesh=mesh,
        in_specs=(P(("row", "col"), None), P(), P("row", "col", None), P("row", "col"), P()),
        out_specs=P(("row", "col"), None),
        check_vma=False,
    )
```

```python
import functools
import math

import jax
import jax.numpy as jnp
from jax import lax
from jax.experimental import pallas as pl
from jax.experimental.pallas import tpu as pltpu
from jax.sharding import PartitionSpec as P

ITERS = 2
LOG2E = math.log2(math.e)
VMEM = 60 * 1024 * 1024
SMALL = 24 * 1024 * 1024
HIGH = lax.Precision.HIGHEST
RIDGE = 1e-6


def weigh(block, scale):
    return (block.astype(jnp.float32) * scale[...]).astype(jnp.bfloat16)


def lane_sums(values):
    part = values[:, :128]
    for start in range(128, values.shape[1], 128):
        part = part + values[:, start : start + 128]
    return jnp.sum(part.T, axis=0, keepdims=True)


def task_lists(slots):
    return 0, slots, 2 * slots, 3 * slots, 5 * slots


def live_step(step, lists, slots):
    return jnp.maximum(jnp.minimum(step, lists[5 * slots] - 1), 0)


def half_squares(rows):
    wide = rows.astype(jnp.float32)
    return wide * wide * (0.5 * LOG2E)


def tile_chunk(left, right, right_half):
    dots = lax.dot_general(
        left, right, (((1,), (1,)), ((), ())), preferred_element_type=jnp.float32
    )
    left_half = jnp.sum(half_squares(left), axis=1, keepdims=True)
    return jnp.exp2(dots * LOG2E - left_half - right_half)


def fold(block):
    return jnp.concatenate([block[i : i + 8, :] for i in range(0, block.shape[0], 8)], axis=1)


def unfold(lines):
    return jnp.concatenate([lines[:, i : i + 32] for i in range(0, lines.shape[1], 32)], axis=0)


def packed_gram(vectors):
    gram = lax.dot_general(
        vectors,
        vectors,
        (((1,), (1,)), ((), ())),
        precision=HIGH,
        preferred_element_type=jnp.float32,
    )
    half = gram.shape[0] // 2
    quarters = (gram[:half, :half], gram[half:, :half], gram[half:, half:])
    return jnp.concatenate([fold(quarter) for quarter in quarters], axis=0)


def inverse_factor(packed, ridge):
    width = packed.shape[1]
    size = width // 2
    upper, lower_left, lower = (unfold(packed[i : i + 8, :]) for i in (0, 8, 16))
    filler = jnp.zeros((size // 2, size), jnp.float32)
    state = jnp.concatenate(
        [
            jnp.concatenate([upper, lower_left.T, filler], axis=1),
            jnp.concatenate([lower_left, lower, filler], axis=1),
        ],
        axis=0,
    )
    row_id = lax.broadcasted_iota(jnp.int32, state.shape, 0)
    lane_id = lax.broadcasted_iota(jnp.int32, state.shape, 1)
    state = jnp.where(lane_id < size, state, jnp.where(lane_id - size == row_id, 1.0, 0.0))
    if ridge:
        on_diagonal = lane_id == row_id
        trace = jnp.sum(jnp.where(on_diagonal, state, 0.0))
        state = jnp.where(on_diagonal, state + trace * (RIDGE / size), state)
    done = []
    for start in range(0, size, 8):
        columns = [
            jnp.broadcast_to(state[:, start + j : start + j + 1], state.shape) for j in range(8)
        ]
        row_id = lax.broadcasted_iota(jnp.int32, state.shape, 0)
        scale = jnp.zeros((8, width), jnp.float32)
        for j in range(8):
            column = columns[j]
            pivot = column[j : j + 1, :]
            scale = jnp.where(row_id[:8] == j, lax.rsqrt(pivot), scale)
            factor = jnp.where(row_id > j, column * (1.0 / pivot), 0.0)
            state = state - factor * state[j : j + 1, :]
            for m in range(j + 1, 8):
                columns[m] = columns[m] - factor * column[m : m + 1, :]
        done.append(state[:8] * scale)
        state = state[8:]
    full = jnp.concatenate(done, axis=0)
    return pltpu.roll(full, size, 1)[:, :size]


def transform(matrix, vectors):
    return jnp.dot(matrix, vectors, precision=HIGH, preferred_element_type=jnp.float32)


def call(kernel, name, out_shape, grant=SMALL):
    return pl.pallas_call(
        kernel,
        out_shape=out_shape,
        compiler_params=pltpu.CompilerParams(vmem_limit_bytes=grant),
        name=name,
    )


def f32(*shape):
    return jax.ShapeDtypeStruct(shape, jnp.float32)


def bf16(*shape):
    return jax.ShapeDtypeStruct(shape, jnp.bfloat16)


def seed_kernel_rows(seeds, block):
    dots = lax.dot_general(
        seeds, block, (((1,), (1,)), ((), ())), preferred_element_type=jnp.float32
    )
    seed_half = jnp.sum(half_squares(seeds), axis=1, keepdims=True)
    return jnp.exp2(dots * LOG2E - seed_half - lane_sums(half_squares(block)))


def start_kernel(seeds, own, start, grams):
    value = seed_kernel_rows(seeds[...], own[...])
    start[...] = value
    grams[...] = jnp.broadcast_to(packed_gram(value)[None], grams.shape)


def first_factor_kernel(grams, start, diagonal, own_degree, factor, subspace, later_gram):
    inverse = inverse_factor(jnp.sum(grams[...], axis=0), False)
    factor[...] = inverse
    value = transform(inverse, start[...])
    subspace[...] = value
    root = lax.rsqrt(own_degree[...])
    product = jnp.dot(
        (value * root).astype(jnp.bfloat16), diagonal[...], preferred_element_type=jnp.float32
    )
    later_gram[...] = packed_gram(product * root)


def later_factor_kernel(gram_rows, factor):
    factor[...] = inverse_factor(gram_rows[:, 0, :], True)


def later_factor(lines, vecs):
    height, width = 3 * vecs // 8, 2 * vecs
    place = lines.shape[2] // width - 1
    return pl.pallas_call(
        later_factor_kernel,
        grid=(1,),
        in_specs=[pl.BlockSpec((height, 1, width), lambda s: (0, 0, place))],
        out_specs=pl.BlockSpec((vecs, vecs), lambda s: (0, 0)),
        out_shape=f32(vecs, vecs),
        compiler_params=pltpu.CompilerParams(vmem_limit_bytes=SMALL),
        name="later_factor",
    )(lines)


def degree_kernel(own_degree, parts, copies, root):
    points = root.shape[1]
    total = jnp.sum(parts[...], axis=0)
    value = lax.rsqrt(total[:, :points] + own_degree[...])
    root[...] = value
    copies[...] = jnp.broadcast_to(
        jnp.concatenate([value, total[:, points:]], axis=1)[None], copies.shape
    )


def gathered(own_part, first_parts, second_part, root):
    total = own_part[...] + second_part[...].astype(jnp.float32)
    for index in range(first_parts.shape[0]):
        total = total + first_parts[index].astype(jnp.float32)
    return total * root[...]


def between_kernel(own_part, first_parts, second_part, root, factor, copies, spread):
    value = transform(factor[...], gathered(own_part, first_parts, second_part, root))
    value = (value * root[...]).astype(jnp.bfloat16)
    spread[...] = value
    copies[...] = jnp.broadcast_to(value[None], copies.shape)


def between(own_part, first_parts, second_part, root, factor):
    copies, vecs, rows = first_parts.shape
    return call(
        between_kernel, "between", [bf16(copies, vecs, rows), bf16(vecs, rows)], VMEM
    )(own_part, first_parts, second_part, root, factor)


def last_kernel(own_part, first_parts, second_part, root, subspace, grams):
    value = gathered(own_part, first_parts, second_part, root)
    subspace[...] = value
    grams[...] = jnp.broadcast_to(packed_gram(value)[None], grams.shape)


def final_kernel(points_all, grams, subspace, embedding):
    inverse = inverse_factor(jnp.sum(grams[...], axis=0), False)
    scaled = transform(inverse, subspace[...]) * math.sqrt(points_all)
    mean = jnp.mean(scaled * scaled, axis=0, keepdims=True)
    embedding[...] = scaled * lax.rsqrt(mean + 1e-06)


def relay_kernel(grams, copies):
    copies[...] = jnp.broadcast_to(jnp.sum(grams[...], axis=0)[None], copies.shape)


def vectors_kernel(slots, lists, block, seeds, factor, *rest):
    out = rest[-1]

    @pl.when(pl.program_id(0) < lists[5 * slots])
    def work():
        rows = block[0] if len(rest) == 1 else weigh(block[0], rest[0])
        out[0] = transform(factor[...], seed_kernel_rows(seeds[...], rows))


def start_vectors(lists, slots, source, band, seeds, factor, *scale):
    unused, rows, depth = band.shape
    vecs = seeds.shape[0]
    return pl.pallas_call(
        functools.partial(vectors_kernel, slots),
        grid_spec=pltpu.PrefetchScalarGridSpec(
            num_scalar_prefetch=1,
            grid=(slots,),
            in_specs=[
                pl.BlockSpec(
                    (1, rows, depth), lambda s, t: (t[source + live_step(s, t, slots)], 0, 0)
                ),
                pl.BlockSpec((vecs, depth), lambda s, t: (0, 0)),
                pl.BlockSpec((vecs, vecs), lambda s, t: (0, 0)),
            ]
            + [pl.BlockSpec(one.shape, lambda s, t: (0, 0)) for one in scale],
            out_specs=pl.BlockSpec(
                (1, vecs, rows), lambda s, t: (live_step(s, t, slots), 0, 0)
            ),
        ),
        out_shape=f32(slots, vecs, rows),
        compiler_params=pltpu.CompilerParams(vmem_limit_bytes=VMEM),
        cost_estimate=pl.CostEstimate(
            flops=4_000_000_000, bytes_accessed=10_000_000, transcendentals=0
        ),
        name="start_vectors",
    )(lists, band, seeds, factor, *scale)


def form_kernel(chunk, slots, lists, left, right, scale, gram, tile, lines):
    step = pl.program_id(0)
    points = left.shape[1]

    @pl.when(step == 0)
    def clear():
        lines[...] = jnp.zeros_like(lines)
        for index in range(gram.shape[0]):
            lines[index, :, points:] = gram[index : index + 1, :]

    @pl.when(step < lists[5 * slots])
    def work():
        rows = left.shape[1]
        right_rows = right[0]
        right_half = lane_sums(half_squares(right_rows))
        col_total = jnp.zeros((1, rows), jnp.float32)
        row_totals = []
        for start in range(0, rows, chunk):
            left_rows = weigh(left[0, start : start + chunk, :], scale)
            value = tile_chunk(left_rows, right_rows, right_half)
            tile[0, start : start + chunk, :] = value.astype(jnp.bfloat16)
            col_total = col_total + jnp.sum(value, axis=0, keepdims=True)
            row_totals.append(lane_sums(value))
        left_owner = lists[3 * slots + 2 * step]
        right_owner = lists[3 * slots + 2 * step + 1]
        row_total = jnp.concatenate(row_totals, axis=1)
        lines[left_owner, :, :points] = lines[left_owner, :, :points] + row_total
        lines[right_owner, :, :points] = lines[right_owner, :, :points] + col_total


def form_tiles(lists, slots, row_band, col_band, scale, gram):
    col_devices, rows, depth = row_band.shape
    line = (col_devices * col_band.shape[0], 1, rows + gram.shape[1])
    firsts, unused, places, owners, live = task_lists(slots)

    return pl.pallas_call(
        functools.partial(form_kernel, min(256, rows), slots),
        grid_spec=pltpu.PrefetchScalarGridSpec(
            num_scalar_prefetch=1,
            grid=(slots,),
            in_specs=[
                pl.BlockSpec(
                    (1, rows, depth), lambda s, t: (t[firsts + live_step(s, t, slots)], 0, 0)
                ),
                pl.BlockSpec(
                    (1, rows, depth), lambda s, t: (t[places + live_step(s, t, slots)], 0, 0)
                ),
                pl.BlockSpec(scale.shape, lambda s, t: (0, 0)),
                pl.BlockSpec(gram.shape, lambda s, t: (0, 0)),
            ],
            out_specs=[
                pl.BlockSpec((1, rows, rows), lambda s, t: (live_step(s, t, slots), 0, 0)),
                pl.BlockSpec(line, lambda s, t: (0, 0, 0)),
            ],
        ),
        out_shape=[bf16(slots, rows, rows), f32(*line)],
        compiler_params=pltpu.CompilerParams(vmem_limit_bytes=VMEM),
        name="form_tiles",
    )(lists, row_band, col_band, scale, gram)


def diagonal_kernel(chunk, own, tile, degree):
    rows = own.shape[0]
    right_rows = own[...]
    right_half = lane_sums(half_squares(right_rows))
    total = jnp.zeros((1, rows), jnp.float32)
    for start in range(0, rows, chunk):
        value = tile_chunk(own[start : start + chunk, :], right_rows, right_half)
        tile[start : start + chunk, :] = value.astype(jnp.bfloat16)
        total = total + jnp.sum(value, axis=0, keepdims=True)
    degree[...] = total


def form_diagonal(own):
    rows = own.shape[0]
    return pl.pallas_call(
        functools.partial(diagonal_kernel, min(256, rows)),
        out_shape=[
            jax.ShapeDtypeStruct((rows, rows), jnp.bfloat16),
            jax.ShapeDtypeStruct((1, rows), jnp.float32),
        ],
        compiler_params=pltpu.CompilerParams(vmem_limit_bytes=SMALL),
        name="form_diagonal",
    )(own)


def apply_kernel(slots, lists, tile, left, right, *rest):
    step = pl.program_id(0)
    left_roots, right_roots, to_first, to_second = rest if len(rest) == 4 else (None, None) + rest

    def scaled(vectors, roots):
        if roots is None:
            return vectors[0]
        return (vectors[0] * roots[0, :, : vectors.shape[2]]).astype(jnp.bfloat16)

    def add(out, slot, vectors, contract):
        product = lax.dot_general(
            vectors, tile[0], (((1,), (contract,)), ((), ())), preferred_element_type=jnp.float32
        )
        out[slot] = (out[slot].astype(jnp.float32) + product).astype(jnp.bfloat16)

    @pl.when(step == 0)
    def clear():
        to_first[...] = jnp.zeros_like(to_first)
        to_second[...] = jnp.zeros_like(to_second)

    @pl.when(step < lists[5 * slots])
    def work():
        add(to_second, lists[slots + step], scaled(left, left_roots), 0)
        add(to_first, lists[step], scaled(right, right_roots), 1)


def apply_tiles(lists, tiles, from_first, from_second, roots, col_devices, row_devices):
    slots, rows, unused = tiles.shape
    vecs = from_first.shape[1]

    def by_task(s, t):
        return (live_step(s, t, slots), 0, 0)

    def by_first(s, t):
        return (t[live_step(s, t, slots)], 0, 0)

    def by_second(s, t):
        return (t[slots + live_step(s, t, slots)], 0, 0)

    def by_owner(side):
        return lambda s, t: (t[3 * slots + 2 * live_step(s, t, slots) + side], 0, 0)

    block = (1, vecs, rows)
    by_slot = roots is not None
    in_specs = [
        pl.BlockSpec((1, rows, rows), by_task),
        pl.BlockSpec(block, by_task if by_slot else by_first),
        pl.BlockSpec(block, by_task if by_slot else by_second),
    ]
    operands = [lists, tiles, from_first, from_second]
    if by_slot:
        for side in range(2):
            in_specs.append(pl.BlockSpec((1,) + roots.shape[1:], by_owner(side)))
            operands.append(roots)
    return pl.pallas_call(
        functools.partial(apply_kernel, slots),
        grid_spec=pltpu.PrefetchScalarGridSpec(
            num_scalar_prefetch=1,
            grid=(slots,),
            in_specs=in_specs,
            out_specs=[
                pl.BlockSpec((col_devices, vecs, rows), lambda s, t: (0, 0, 0)),
                pl.BlockSpec((row_devices, vecs, rows), lambda s, t: (0, 0, 0)),
            ],
        ),
        out_shape=[bf16(col_devices, vecs, rows), bf16(row_devices, vecs, rows)],
        compiler_params=pltpu.CompilerParams(vmem_limit_bytes=VMEM),
        name="apply_tiles",
    )(*operands)


def spread_to(array, axis):
    devices = lax.axis_size(axis)
    copies = jnp.broadcast_to(array[None], (devices,) + array.shape)
    return lax.all_to_all(copies, axis, 0, 0, tiled=True)


def exchange(copies, axis):
    return lax.all_to_all(copies, axis, 0, 0, tiled=True)


def together(*arrays):
    return lax.optimization_barrier(arrays)


def place_in_row(index, here):
    apart = (index // 2 - here // 2 + 4) % 4
    order = jnp.where(apart == 0, 0, jnp.where(apart == 3, 1, jnp.where(apart == 1, 2, 3)))
    return order + 4 * ((index + here) % 2)


def assign_kernel(slots, cols, here, table, lists):
    devices = table.shape[1]
    me = here[0]
    filler = jnp.zeros((devices - table.shape[0], devices), jnp.float32)
    by_device = jnp.concatenate([table[...], filler], axis=0).T
    device = lax.broadcasted_iota(jnp.int32, (devices, devices), 0)
    lane = lax.broadcasted_iota(jnp.int32, (devices, devices), 1)
    same = jnp.where(device == lane, 1.0, 0.0)
    count = by_device[:, slots : slots + 1]
    load = jnp.zeros((1, devices), jnp.float32)
    moves = []
    taken = []
    listed = []
    for slot in range(slots):
        partner = by_device[:, slot : slot + 1]
        is_listed = jnp.where(count > slot, 1.0, 0.0)
        picks = jnp.where(lane.astype(jnp.float32) == partner, 1.0, 0.0)
        move = (picks - same) * is_listed
        apart = jnp.sum(move * load, axis=1, keepdims=True)
        take = jnp.where(apart <= 0, is_listed, 0.0)
        load = load + jnp.sum(same * is_listed + move * take, axis=0, keepdims=True)
        moves.append(move)
        taken.append(take)
        listed.append(is_listed)
    for slot in range(slots):
        apart = jnp.sum(moves[slot] * load, axis=1, keepdims=True)
        give = jnp.where(apart < -1, listed[slot] * (1.0 - taken[slot]), 0.0)
        back = jnp.where(apart > 1, taken[slot], 0.0)
        load = load + jnp.sum(moves[slot] * (give - back), axis=0, keepdims=True)
        taken[slot] = taken[slot] + give - back
    shared = jnp.where(jnp.max(load) <= slots, 1.0, 0.0)
    code = jnp.zeros((devices, devices), jnp.float32)
    number = device.astype(jnp.float32)
    for slot in range(slots):
        partner = by_device[:, slot : slot + 1]
        take = taken[slot] * shared
        kept = jnp.where(device == me, listed[slot] - take, 0.0)
        come = jnp.where(partner == me.astype(jnp.float32), take, 0.0)
        other = kept * partner + come * number
        cell = (kept + come) * (number * slots + (slot + 1)) * devices + other
        code = jnp.where(lane == slot, cell, code)
    lists[5 * slots] = jnp.sum(jnp.where(code > 0, 1.0, 0.0)).astype(jnp.int32)
    for slot in range(slots):
        top = jnp.max(code)
        partner = lax.rem(top.astype(jnp.int32), devices)
        code = jnp.where(code == top, 0.0, code)
        first_slot = lax.rem(partner, cols)
        second_slot = lax.div(partner, cols)
        lists[slot] = first_slot
        lists[slots + slot] = second_slot
        lists[2 * slots + slot] = place_in_row(second_slot, lax.div(me, cols))
        lists[3 * slots + 2 * slot] = lax.div(me, cols) * cols + first_slot
        lists[3 * slots + 2 * slot + 1] = second_slot * cols + lax.rem(me, cols)


def assign_tasks(self_index, table, slots, cols):
    smem = pl.BlockSpec(memory_space=pltpu.SMEM)
    return pl.pallas_call(
        functools.partial(assign_kernel, slots, cols),
        in_specs=[smem, pl.BlockSpec(memory_space=pltpu.VMEM)],
        out_specs=smem,
        out_shape=jax.ShapeDtypeStruct((6 * slots,), jnp.int32),
        compiler_params=pltpu.CompilerParams(vmem_limit_bytes=SMALL),
        name="assign_tasks",
    )(self_index.reshape(1), table)


def shards(points, feature_scale, tile_tasks, task_count, seed_ids):
    rows = points.shape[0]
    vecs = seed_ids.shape[0]
    packed = (3 * vecs // 8, 2 * vecs)
    row_devices = lax.axis_size("row")
    col_devices = lax.axis_size("col")
    all_devices = row_devices * col_devices
    self_index = lax.axis_index("row") * col_devices + lax.axis_index("col")
    weighted = (points.astype(jnp.float32) * feature_scale[None, :]).astype(jnp.bfloat16)
    row_band = lax.all_gather(points, "col", axis=0)
    scale = feature_scale[None, :]
    listed = tile_tasks.reshape(-1)
    slots = listed.shape[0]

    def shift(array, by):
        return lax.ppermute(
            array, "row", [(i, (i + by) % row_devices) for i in range(row_devices)]
        )

    local_seed = seed_ids - self_index * rows
    inside = (local_seed >= 0) & (local_seed < rows)
    picked = jnp.where(
        inside[:, None], jnp.take(weighted, jnp.clip(local_seed, 0, rows - 1), axis=0), 0
    ).astype(jnp.bfloat16)
    own_line = jnp.concatenate(
        [listed, task_count.reshape(-1), jnp.zeros((slots - 1,), jnp.int32)]
    )
    lines = jnp.where(
        (jnp.arange(weighted.shape[1]) == self_index)[None, :], own_line[:, None], 0
    ).astype(jnp.bfloat16)
    picked = jnp.concatenate([picked, lines], axis=0)
    seed_parts = spread_to(picked, "row")
    before = shift(weighted, 2)
    after = shift(weighted, -2)
    before, after, seed_parts = together(before, after, seed_parts)
    half = rows // 2
    across_low = shift(before[:half], 2)
    across_high = shift(after[half:], -2)
    seed_parts = spread_to(jnp.sum(seed_parts, axis=0), "col")
    diagonal, own_degree = form_diagonal(weighted)
    seed_sum = jnp.sum(seed_parts, axis=0)
    seeds = seed_sum[:vecs]
    table = seed_sum[vecs:, :all_devices].astype(jnp.float32)
    start, grams = call(
        start_kernel, "start", [f32(vecs, rows), f32(row_devices, *packed)]
    )(seeds, weighted)
    across_low, across_high, grams = together(across_low, across_high, grams)
    grams = exchange(grams, "row")
    across = jnp.concatenate([across_low, across_high], axis=0)
    mine = jnp.stack([weighted, before, after, across])
    mine, grams = together(mine, grams)
    other = lax.ppermute(mine, "row", [(i, i ^ 1) for i in range(row_devices)])
    grams = call(relay_kernel, "relay", f32(col_devices, *packed))(grams)
    grams = exchange(grams, "col")
    lists = assign_tasks(self_index, table, slots, col_devices)
    firsts, seconds, places, unused, unused = task_lists(slots)
    col_band, grams = together(jnp.concatenate([mine, other], axis=0), grams)
    factor, subspace, later_gram = call(
        first_factor_kernel,
        "first_factor",
        [f32(vecs, vecs), f32(vecs, rows), f32(*packed)],
    )(grams, start, diagonal, own_degree)

    tiles, lines = form_tiles(lists, slots, row_band, col_band, scale, later_gram)
    copies, inv_root = call(degree_kernel, "degree", [f32(*lines.shape), f32(1, rows)])(
        own_degree, exchange(lines, ("row", "col"))
    )
    lines = exchange(copies, ("row", "col"))
    roots = lines
    from_first = start_vectors(lists, slots, firsts, row_band, seeds, factor, scale)
    from_second = start_vectors(lists, slots, places, col_band, seeds, factor)
    spread = (subspace * inv_root).astype(jnp.bfloat16)
    for iteration in range(ITERS):
        own_part = lax.dot_general(
            spread, diagonal, (((1,), (0,)), ((), ())), preferred_element_type=jnp.float32
        )
        to_first, to_second = apply_tiles(
            lists, tiles, from_first, from_second, roots, col_devices, row_devices
        )
        second_part = lax.psum_scatter(to_second, "row", scatter_dimension=0, tiled=False)
        first_parts = exchange(to_first, "col")
        if iteration + 1 < ITERS:
            copies, spread = between(
                own_part, first_parts, second_part, inv_root, later_factor(lines, vecs)
            )
            from_second = lax.all_gather(spread, "row", axis=0)
            from_first = exchange(copies, "col")
            roots = None
    subspace, grams = call(
        last_kernel, "last", [f32(vecs, rows), f32(row_devices, *packed)]
    )(own_part, first_parts, second_part, inv_root)
    grams = exchange(grams, "row")
    grams = call(relay_kernel, "relay", f32(col_devices, *packed))(grams)
    grams = exchange(grams, "col")
    return call(
        functools.partial(final_kernel, all_devices * rows), "final", f32(vecs, rows)
    )(grams, subspace).T


def solution(mesh):
    return jax.shard_map(
        shards,
        mesh=mesh,
        in_specs=(P(("row", "col"), None), P(), P("row", "col", None), P("row", "col"), P()),
        out_specs=P(("row", "col"), None),
        check_vma=False,
    )
```

```python
import functools
import math

import jax
import jax.numpy as jnp
from jax import lax
from jax.experimental import pallas as pl
from jax.experimental.pallas import tpu as pltpu
from jax.sharding import PartitionSpec as P

ITERS = 2
LOG2E = math.log2(math.e)
VMEM = 60 * 1024 * 1024
SMALL = 24 * 1024 * 1024
HIGH = lax.Precision.HIGHEST
RIDGE = 1e-5


def for_each_task(body, lists, slots, counter, in_specs, out_specs, refs):
    live = lists[5 * slots]
    counter[0] = 0

    def one(*blocks):
        step = counter[0]
        counter[0] = step + 1

        @pl.when(step < live)
        def work():
            body(step, *blocks)

    pltpu.emit_pipeline(
        one, grid=(jnp.maximum(live, 1),), in_specs=in_specs, out_specs=out_specs
    )(*refs)


def task_call(kernel, name, operands, anywhere, out_specs, out_shape):
    places = [pltpu.SMEM] + [pl.ANY if flag else pltpu.VMEM for flag in anywhere]
    return pl.pallas_call(
        kernel,
        in_specs=[pl.BlockSpec(memory_space=place) for place in places],
        out_specs=out_specs,
        out_shape=out_shape,
        scratch_shapes=[pltpu.SMEM((1,), jnp.int32)],
        compiler_params=pltpu.CompilerParams(vmem_limit_bytes=VMEM),
        name=name,
    )(*operands)


def weigh(block, scale):
    return (block.astype(jnp.float32) * scale[...]).astype(jnp.bfloat16)


def lane_sums(values):
    part = values[:, :128]
    for start in range(128, values.shape[1], 128):
        part = part + values[:, start : start + 128]
    return jnp.sum(part.T, axis=0, keepdims=True)


def task_lists(slots):
    return 0, slots, 2 * slots, 3 * slots, 5 * slots


def live_step(step, lists, slots):
    return jnp.maximum(jnp.minimum(step, lists[5 * slots] - 1), 0)


def half_squares(rows):
    wide = rows.astype(jnp.float32)
    return wide * wide * (0.5 * LOG2E)


def tile_chunk(left, right, right_half):
    dots = lax.dot_general(
        left, right, (((1,), (1,)), ((), ())), preferred_element_type=jnp.float32
    )
    left_half = jnp.sum(half_squares(left), axis=1, keepdims=True)
    return jnp.exp2(dots * LOG2E - left_half - right_half)


def fold(block):
    return jnp.concatenate([block[i : i + 8, :] for i in range(0, block.shape[0], 8)], axis=1)


def unfold(lines):
    return jnp.concatenate([lines[:, i : i + 32] for i in range(0, lines.shape[1], 32)], axis=0)


def packed_gram(vectors):
    gram = lax.dot_general(
        vectors,
        vectors,
        (((1,), (1,)), ((), ())),
        precision=HIGH,
        preferred_element_type=jnp.float32,
    )
    half = gram.shape[0] // 2
    quarters = (gram[:half, :half], gram[half:, :half], gram[half:, half:])
    return jnp.concatenate([fold(quarter) for quarter in quarters], axis=0)


def inverse_factor(packed, ridge):
    width = packed.shape[1]
    size = width // 2
    upper, lower_left, lower = (unfold(packed[i : i + 8, :]) for i in (0, 8, 16))
    filler = jnp.zeros((size // 2, size), jnp.float32)
    state = jnp.concatenate(
        [
            jnp.concatenate([upper, lower_left.T, filler], axis=1),
            jnp.concatenate([lower_left, lower, filler], axis=1),
        ],
        axis=0,
    )
    row_id = lax.broadcasted_iota(jnp.int32, state.shape, 0)
    lane_id = lax.broadcasted_iota(jnp.int32, state.shape, 1)
    state = jnp.where(lane_id < size, state, jnp.where(lane_id - size == row_id, 1.0, 0.0))
    if ridge:
        on_diagonal = lane_id == row_id
        trace = jnp.sum(jnp.where(on_diagonal, state, 0.0))
        state = jnp.where(on_diagonal, state + trace * (RIDGE / size), state)
    done = []
    for start in range(0, size, 8):
        columns = [
            jnp.broadcast_to(state[:, start + j : start + j + 1], state.shape) for j in range(8)
        ]
        row_id = lax.broadcasted_iota(jnp.int32, state.shape, 0)
        scale = jnp.zeros((8, width), jnp.float32)
        for j in range(8):
            column = columns[j]
            pivot = column[j : j + 1, :]
            scale = jnp.where(row_id[:8] == j, lax.rsqrt(pivot), scale)
            factor = jnp.where(row_id > j, column * (1.0 / pivot), 0.0)
            state = state - factor * state[j : j + 1, :]
            for m in range(j + 1, 8):
                columns[m] = columns[m] - factor * column[m : m + 1, :]
        done.append(state[:8] * scale)
        state = state[8:]
    full = jnp.concatenate(done, axis=0)
    return pltpu.roll(full, size, 1)[:, :size]


def transform(matrix, vectors):
    return jnp.dot(matrix, vectors, precision=HIGH, preferred_element_type=jnp.float32)


def call(kernel, name, out_shape, grant=SMALL):
    return pl.pallas_call(
        kernel,
        out_shape=out_shape,
        compiler_params=pltpu.CompilerParams(vmem_limit_bytes=grant),
        name=name,
    )


def f32(*shape):
    return jax.ShapeDtypeStruct(shape, jnp.float32)


def bf16(*shape):
    return jax.ShapeDtypeStruct(shape, jnp.bfloat16)


def seed_kernel_rows(seeds, block):
    dots = lax.dot_general(
        seeds, block, (((1,), (1,)), ((), ())), preferred_element_type=jnp.float32
    )
    seed_half = jnp.sum(half_squares(seeds), axis=1, keepdims=True)
    return jnp.exp2(dots * LOG2E - seed_half - lane_sums(half_squares(block)))


def start_kernel(seeds, own, start, grams):
    value = seed_kernel_rows(seeds[...], own[...])
    start[...] = value
    grams[...] = jnp.broadcast_to(packed_gram(value)[None], grams.shape)


def first_factor_kernel(grams, start, diagonal, own_degree, factor, subspace, later_gram):
    inverse = inverse_factor(jnp.sum(grams[...], axis=0), False)
    factor[...] = inverse
    value = transform(inverse, start[...])
    subspace[...] = value
    root = lax.rsqrt(own_degree[...])
    product = jnp.dot(
        (value * root).astype(jnp.bfloat16), diagonal[...], preferred_element_type=jnp.float32
    )
    later_gram[...] = packed_gram(product * root)


def later_factor_kernel(gram_rows, factor):
    factor[...] = inverse_factor(gram_rows[:, 0, :], True)


def later_factor(lines, vecs):
    height, width = 3 * vecs // 8, 2 * vecs
    place = lines.shape[2] // width - 1
    return pl.pallas_call(
        later_factor_kernel,
        grid=(1,),
        in_specs=[pl.BlockSpec((height, 1, width), lambda s: (0, 0, place))],
        out_specs=pl.BlockSpec((vecs, vecs), lambda s: (0, 0)),
        out_shape=f32(vecs, vecs),
        compiler_params=pltpu.CompilerParams(vmem_limit_bytes=SMALL),
        name="later_factor",
    )(lines)


def degree_kernel(own_degree, parts, copies, root):
    points = root.shape[1]
    total = jnp.sum(parts[...], axis=0)
    value = lax.rsqrt(total[:, :points] + own_degree[...])
    root[...] = value
    copies[...] = jnp.broadcast_to(
        jnp.concatenate([value, total[:, points:]], axis=1)[None], copies.shape
    )


def gathered(own_part, first_parts, second_part, root):
    total = own_part[...] + second_part[...].astype(jnp.float32)
    for index in range(first_parts.shape[0]):
        total = total + first_parts[index].astype(jnp.float32)
    return total * root[...]


def between_kernel(own_part, first_parts, second_part, root, factor, copies, spread):
    value = transform(factor[...], gathered(own_part, first_parts, second_part, root))
    value = (value * root[...]).astype(jnp.bfloat16)
    spread[...] = value
    copies[...] = jnp.broadcast_to(value[None], copies.shape)


def between(own_part, first_parts, second_part, root, factor):
    copies, vecs, rows = first_parts.shape
    return call(
        between_kernel, "between", [bf16(copies, vecs, rows), bf16(vecs, rows)], VMEM
    )(own_part, first_parts, second_part, root, factor)


def last_kernel(own_part, first_parts, second_part, root, subspace, grams):
    value = gathered(own_part, first_parts, second_part, root)
    subspace[...] = value
    grams[...] = jnp.broadcast_to(packed_gram(value)[None], grams.shape)


def final_kernel(points_all, grams, subspace, embedding):
    inverse = inverse_factor(jnp.sum(grams[...], axis=0), False)
    scaled = transform(inverse, subspace[...]) * math.sqrt(points_all)
    mean = jnp.mean(scaled * scaled, axis=0, keepdims=True)
    embedding[...] = scaled * lax.rsqrt(mean + 1e-06)


def relay_kernel(grams, copies):
    copies[...] = jnp.broadcast_to(jnp.sum(grams[...], axis=0)[None], copies.shape)


def vectors_kernel(slots, lists, block, seeds, factor, *rest):
    out = rest[-1]

    @pl.when(pl.program_id(0) < lists[5 * slots])
    def work():
        rows = block[0] if len(rest) == 1 else weigh(block[0], rest[0])
        out[0] = transform(factor[...], seed_kernel_rows(seeds[...], rows))


def start_vectors(lists, slots, source, band, seeds, factor, *scale):
    unused, rows, depth = band.shape
    vecs = seeds.shape[0]
    return pl.pallas_call(
        functools.partial(vectors_kernel, slots),
        grid_spec=pltpu.PrefetchScalarGridSpec(
            num_scalar_prefetch=1,
            grid=(slots,),
            in_specs=[
                pl.BlockSpec(
                    (1, rows, depth), lambda s, t: (t[source + live_step(s, t, slots)], 0, 0)
                ),
                pl.BlockSpec((vecs, depth), lambda s, t: (0, 0)),
                pl.BlockSpec((vecs, vecs), lambda s, t: (0, 0)),
            ]
            + [pl.BlockSpec(one.shape, lambda s, t: (0, 0)) for one in scale],
            out_specs=pl.BlockSpec(
                (1, vecs, rows), lambda s, t: (live_step(s, t, slots), 0, 0)
            ),
        ),
        out_shape=f32(slots, vecs, rows),
        compiler_params=pltpu.CompilerParams(vmem_limit_bytes=VMEM),
        cost_estimate=pl.CostEstimate(
            flops=4_000_000_000, bytes_accessed=10_000_000, transcendentals=0
        ),
        name="start_vectors",
    )(lists, band, seeds, factor, *scale)


def form_kernel(chunk, slots, lists, left, right, scale, gram, tile, lines):
    step = pl.program_id(0)
    points = left.shape[1]

    @pl.when(step == 0)
    def clear():
        lines[...] = jnp.zeros_like(lines)
        for index in range(gram.shape[0]):
            lines[index, :, points:] = gram[index : index + 1, :]

    @pl.when(step < lists[5 * slots])
    def work():
        rows = left.shape[1]
        right_rows = right[0]
        right_half = lane_sums(half_squares(right_rows))
        col_total = jnp.zeros((1, rows), jnp.float32)
        row_totals = []
        for start in range(0, rows, chunk):
            left_rows = weigh(left[0, start : start + chunk, :], scale)
            value = tile_chunk(left_rows, right_rows, right_half)
            tile[0, start : start + chunk, :] = value.astype(jnp.bfloat16)
            col_total = col_total + jnp.sum(value, axis=0, keepdims=True)
            row_totals.append(lane_sums(value))
        left_owner = lists[3 * slots + 2 * step]
        right_owner = lists[3 * slots + 2 * step + 1]
        row_total = jnp.concatenate(row_totals, axis=1)
        lines[left_owner, :, :points] = lines[left_owner, :, :points] + row_total
        lines[right_owner, :, :points] = lines[right_owner, :, :points] + col_total


def form_tiles(lists, slots, row_band, col_band, scale, gram):
    col_devices, rows, depth = row_band.shape
    line = (col_devices * col_band.shape[0], 1, rows + gram.shape[1])
    firsts, unused, places, owners, live = task_lists(slots)

    return pl.pallas_call(
        functools.partial(form_kernel, min(256, rows), slots),
        grid_spec=pltpu.PrefetchScalarGridSpec(
            num_scalar_prefetch=1,
            grid=(slots,),
            in_specs=[
                pl.BlockSpec(
                    (1, rows, depth), lambda s, t: (t[firsts + live_step(s, t, slots)], 0, 0)
                ),
                pl.BlockSpec(
                    (1, rows, depth), lambda s, t: (t[places + live_step(s, t, slots)], 0, 0)
                ),
                pl.BlockSpec(scale.shape, lambda s, t: (0, 0)),
                pl.BlockSpec(gram.shape, lambda s, t: (0, 0)),
            ],
            out_specs=[
                pl.BlockSpec((1, rows, rows), lambda s, t: (live_step(s, t, slots), 0, 0)),
                pl.BlockSpec(line, lambda s, t: (0, 0, 0)),
            ],
        ),
        out_shape=[bf16(slots, rows, rows), f32(*line)],
        compiler_params=pltpu.CompilerParams(vmem_limit_bytes=VMEM),
        name="form_tiles",
    )(lists, row_band, col_band, scale, gram)


def diagonal_kernel(chunk, own, tile, degree):
    rows = own.shape[0]
    right_rows = own[...]
    right_half = lane_sums(half_squares(right_rows))
    total = jnp.zeros((1, rows), jnp.float32)
    for start in range(0, rows, chunk):
        value = tile_chunk(own[start : start + chunk, :], right_rows, right_half)
        tile[start : start + chunk, :] = value.astype(jnp.bfloat16)
        total = total + jnp.sum(value, axis=0, keepdims=True)
    degree[...] = total


def form_diagonal(own):
    rows = own.shape[0]
    return pl.pallas_call(
        functools.partial(diagonal_kernel, min(256, rows)),
        out_shape=[
            jax.ShapeDtypeStruct((rows, rows), jnp.bfloat16),
            jax.ShapeDtypeStruct((1, rows), jnp.float32),
        ],
        compiler_params=pltpu.CompilerParams(vmem_limit_bytes=SMALL),
        name="form_diagonal",
    )(own)


def apply_kernel(slots, lists, tiles, from_first, from_second, *rest):
    roots, (to_first, to_second, counter) = rest[:-3], rest[-3:]
    rows = tiles.shape[1]
    to_first[...] = jnp.zeros_like(to_first)
    to_second[...] = jnp.zeros_like(to_second)

    def body(step, tile, left, right, *task_roots):
        def scaled(vectors, which):
            if not task_roots:
                return vectors[0]
            return (vectors[0] * task_roots[which][0, :, :rows]).astype(jnp.bfloat16)

        def add(out, slot, vectors, contract):
            product = lax.dot_general(
                vectors,
                tile[0],
                (((1,), (contract,)), ((), ())),
                preferred_element_type=jnp.float32,
            )
            out[slot] = (out[slot].astype(jnp.float32) + product).astype(jnp.bfloat16)

        add(to_second, lists[slots + step], scaled(left, 0), 0)
        add(to_first, lists[step], scaled(right, 1), 1)

    def by_task(s):
        return (s, 0, 0)

    def by_first(s):
        return (lists[s], 0, 0)

    def by_second(s):
        return (lists[slots + s], 0, 0)

    def by_owner(side):
        return lambda s: (lists[3 * slots + 2 * s + side], 0, 0)

    block = (1,) + from_first.shape[1:]
    for_each_task(
        body,
        lists,
        slots,
        counter,
        [
            pl.BlockSpec((1, rows, rows), by_task),
            pl.BlockSpec(block, by_task if roots else by_first),
            pl.BlockSpec(block, by_task if roots else by_second),
        ]
        + [pl.BlockSpec((1,) + ref.shape[1:], by_owner(side)) for side, ref in enumerate(roots)],
        [],
        (tiles, from_first, from_second, *roots),
    )


def apply_tiles(lists, tiles, from_first, from_second, roots, col_devices, row_devices):
    slots, rows, unused = tiles.shape
    vecs = from_first.shape[1]
    vmem = pl.BlockSpec(memory_space=pltpu.VMEM)
    lines = () if roots is None else (roots, roots)
    return task_call(
        functools.partial(apply_kernel, slots),
        "apply_tiles",
        (lists, tiles, from_first, from_second, *lines),
        (True,) * (3 + len(lines)),
        [vmem, vmem],
        [bf16(col_devices, vecs, rows), bf16(row_devices, vecs, rows)],
    )


def spread_to(array, axis):
    devices = lax.axis_size(axis)
    copies = jnp.broadcast_to(array[None], (devices,) + array.shape)
    return lax.all_to_all(copies, axis, 0, 0, tiled=True)


def exchange(copies, axis):
    return lax.all_to_all(copies, axis, 0, 0, tiled=True)


def together(*arrays):
    return lax.optimization_barrier(arrays)


def place_in_row(index, here):
    apart = (index // 2 - here // 2 + 4) % 4
    order = jnp.where(apart == 0, 0, jnp.where(apart == 3, 1, jnp.where(apart == 1, 2, 3)))
    return order + 4 * ((index + here) % 2)


def assign_kernel(slots, cols, here, table, lists):
    devices = table.shape[1]
    me = here[0]
    filler = jnp.zeros((devices - table.shape[0], devices), jnp.float32)
    by_device = jnp.concatenate([table[...], filler], axis=0).T
    device = lax.broadcasted_iota(jnp.int32, (devices, devices), 0)
    lane = lax.broadcasted_iota(jnp.int32, (devices, devices), 1)
    same = jnp.where(device == lane, 1.0, 0.0)
    count = by_device[:, slots : slots + 1]
    load = jnp.zeros((1, devices), jnp.float32)
    moves = []
    taken = []
    listed = []
    for slot in range(slots):
        partner = by_device[:, slot : slot + 1]
        is_listed = jnp.where(count > slot, 1.0, 0.0)
        picks = jnp.where(lane.astype(jnp.float32) == partner, 1.0, 0.0)
        move = (picks - same) * is_listed
        apart = jnp.sum(move * load, axis=1, keepdims=True)
        take = jnp.where(apart <= 0, is_listed, 0.0)
        load = load + jnp.sum(same * is_listed + move * take, axis=0, keepdims=True)
        moves.append(move)
        taken.append(take)
        listed.append(is_listed)
    for slot in range(slots):
        apart = jnp.sum(moves[slot] * load, axis=1, keepdims=True)
        give = jnp.where(apart < -1, listed[slot] * (1.0 - taken[slot]), 0.0)
        back = jnp.where(apart > 1, taken[slot], 0.0)
        load = load + jnp.sum(moves[slot] * (give - back), axis=0, keepdims=True)
        taken[slot] = taken[slot] + give - back
    shared = jnp.where(jnp.max(load) <= slots, 1.0, 0.0)
    code = jnp.zeros((devices, devices), jnp.float32)
    number = device.astype(jnp.float32)
    for slot in range(slots):
        partner = by_device[:, slot : slot + 1]
        take = taken[slot] * shared
        kept = jnp.where(device == me, listed[slot] - take, 0.0)
        come = jnp.where(partner == me.astype(jnp.float32), take, 0.0)
        other = kept * partner + come * number
        cell = (kept + come) * (number * slots + (slot + 1)) * devices + other
        code = jnp.where(lane == slot, cell, code)
    lists[5 * slots] = jnp.sum(jnp.where(code > 0, 1.0, 0.0)).astype(jnp.int32)
    for slot in range(slots):
        top = jnp.max(code)
        partner = lax.rem(top.astype(jnp.int32), devices)
        code = jnp.where(code == top, 0.0, code)
        first_slot = lax.rem(partner, cols)
        second_slot = lax.div(partner, cols)
        lists[slot] = first_slot
        lists[slots + slot] = second_slot
        lists[2 * slots + slot] = place_in_row(second_slot, lax.div(me, cols))
        lists[3 * slots + 2 * slot] = lax.div(me, cols) * cols + first_slot
        lists[3 * slots + 2 * slot + 1] = second_slot * cols + lax.rem(me, cols)


def assign_tasks(self_index, table, slots, cols):
    smem = pl.BlockSpec(memory_space=pltpu.SMEM)
    return pl.pallas_call(
        functools.partial(assign_kernel, slots, cols),
        in_specs=[smem, pl.BlockSpec(memory_space=pltpu.VMEM)],
        out_specs=smem,
        out_shape=jax.ShapeDtypeStruct((6 * slots,), jnp.int32),
        compiler_params=pltpu.CompilerParams(vmem_limit_bytes=SMALL),
        name="assign_tasks",
    )(self_index.reshape(1), table)


def shards(points, feature_scale, tile_tasks, task_count, seed_ids):
    rows = points.shape[0]
    vecs = seed_ids.shape[0]
    packed = (3 * vecs // 8, 2 * vecs)
    row_devices = lax.axis_size("row")
    col_devices = lax.axis_size("col")
    all_devices = row_devices * col_devices
    self_index = lax.axis_index("row") * col_devices + lax.axis_index("col")
    weighted = (points.astype(jnp.float32) * feature_scale[None, :]).astype(jnp.bfloat16)
    row_band = lax.all_gather(points, "col", axis=0)
    scale = feature_scale[None, :]
    listed = tile_tasks.reshape(-1)
    slots = listed.shape[0]

    def shift(array, by):
        return lax.ppermute(
            array, "row", [(i, (i + by) % row_devices) for i in range(row_devices)]
        )

    local_seed = seed_ids - self_index * rows
    inside = (local_seed >= 0) & (local_seed < rows)
    picked = jnp.where(
        inside[:, None], jnp.take(weighted, jnp.clip(local_seed, 0, rows - 1), axis=0), 0
    ).astype(jnp.bfloat16)
    own_line = jnp.concatenate(
        [listed, task_count.reshape(-1), jnp.zeros((slots - 1,), jnp.int32)]
    )
    lines = jnp.where(
        (jnp.arange(weighted.shape[1]) == self_index)[None, :], own_line[:, None], 0
    ).astype(jnp.bfloat16)
    picked = jnp.concatenate([picked, lines], axis=0)
    seed_parts = spread_to(picked, "row")
    before = shift(weighted, 2)
    after = shift(weighted, -2)
    before, after, seed_parts = together(before, after, seed_parts)
    half = rows // 2
    across_low = shift(before[:half], 2)
    across_high = shift(after[half:], -2)
    seed_parts = spread_to(jnp.sum(seed_parts, axis=0), "col")
    diagonal, own_degree = form_diagonal(weighted)
    seed_sum = jnp.sum(seed_parts, axis=0)
    seeds = seed_sum[:vecs]
    table = seed_sum[vecs:, :all_devices].astype(jnp.float32)
    start, grams = call(
        start_kernel, "start", [f32(vecs, rows), f32(row_devices, *packed)]
    )(seeds, weighted)
    across_low, across_high, grams = together(across_low, across_high, grams)
    grams = exchange(grams, "row")
    across = jnp.concatenate([across_low, across_high], axis=0)
    mine = jnp.stack([weighted, before, after, across])
    mine, grams = together(mine, grams)
    other = lax.ppermute(mine, "row", [(i, i ^ 1) for i in range(row_devices)])
    grams = call(relay_kernel, "relay", f32(col_devices, *packed))(grams)
    grams = exchange(grams, "col")
    lists = assign_tasks(self_index, table, slots, col_devices)
    firsts, seconds, places, unused, unused = task_lists(slots)
    col_band, grams = together(jnp.concatenate([mine, other], axis=0), grams)
    factor, subspace, later_gram = call(
        first_factor_kernel,
        "first_factor",
        [f32(vecs, vecs), f32(vecs, rows), f32(*packed)],
    )(grams, start, diagonal, own_degree)

    tiles, lines = form_tiles(lists, slots, row_band, col_band, scale, later_gram)
    copies, inv_root = call(degree_kernel, "degree", [f32(*lines.shape), f32(1, rows)])(
        own_degree, exchange(lines, ("row", "col"))
    )
    lines = exchange(copies, ("row", "col"))
    roots = lines
    from_first = start_vectors(lists, slots, firsts, row_band, seeds, factor, scale)
    from_second = start_vectors(lists, slots, places, col_band, seeds, factor)
    spread = (subspace * inv_root).astype(jnp.bfloat16)
    for iteration in range(ITERS):
        own_part = lax.dot_general(
            spread, diagonal, (((1,), (0,)), ((), ())), preferred_element_type=jnp.float32
        )
        to_first, to_second = apply_tiles(
            lists, tiles, from_first, from_second, roots, col_devices, row_devices
        )
        second_part = lax.psum_scatter(to_second, "row", scatter_dimension=0, tiled=False)
        first_parts = exchange(to_first, "col")
        if iteration + 1 < ITERS:
            copies, spread = between(
                own_part, first_parts, second_part, inv_root, later_factor(lines, vecs)
            )
            from_second = lax.all_gather(spread, "row", axis=0)
            from_first = exchange(copies, "col")
            roots = None
    subspace, grams = call(
        last_kernel, "last", [f32(vecs, rows), f32(row_devices, *packed)]
    )(own_part, first_parts, second_part, inv_root)
    grams = exchange(grams, "row")
    grams = call(relay_kernel, "relay", f32(col_devices, *packed))(grams)
    grams = exchange(grams, "col")
    return call(
        functools.partial(final_kernel, all_devices * rows), "final", f32(vecs, rows)
    )(grams, subspace).T


def solution(mesh):
    return jax.shard_map(
        shards,
        mesh=mesh,
        in_specs=(P(("row", "col"), None), P(), P("row", "col", None), P("row", "col"), P()),
        out_specs=P(("row", "col"), None),
        check_vma=False,
    )
```

```python
import functools
import math

import jax
import jax.numpy as jnp
from jax import lax
from jax.experimental import pallas as pl
from jax.experimental.pallas import tpu as pltpu
from jax.sharding import PartitionSpec as P

ITERS = 2
LOG2E = math.log2(math.e)
VMEM = 60 * 1024 * 1024
SMALL = 24 * 1024 * 1024
HIGH = lax.Precision.HIGHEST
RIDGE = 1e-5


def weigh(block, scale):
    return (block.astype(jnp.float32) * scale[...]).astype(jnp.bfloat16)


def lane_sums(values):
    part = values[:, :128]
    for start in range(128, values.shape[1], 128):
        part = part + values[:, start : start + 128]
    return jnp.sum(part.T, axis=0, keepdims=True)


def task_lists(slots):
    return 0, slots, 2 * slots, 3 * slots, 5 * slots


def live_step(step, lists, slots):
    return jnp.maximum(jnp.minimum(step, lists[5 * slots] - 1), 0)


def half_squares(rows):
    wide = rows.astype(jnp.float32)
    return wide * wide * (0.5 * LOG2E)


def tile_chunk(left, right, right_half):
    dots = lax.dot_general(
        left, right, (((1,), (1,)), ((), ())), preferred_element_type=jnp.float32
    )
    left_half = jnp.sum(half_squares(left), axis=1, keepdims=True)
    return jnp.exp2(dots * LOG2E - left_half - right_half)


def fold(block):
    return jnp.concatenate([block[i : i + 8, :] for i in range(0, block.shape[0], 8)], axis=1)


def unfold(lines):
    return jnp.concatenate([lines[:, i : i + 32] for i in range(0, lines.shape[1], 32)], axis=0)


def packed_gram(vectors):
    gram = lax.dot_general(
        vectors,
        vectors,
        (((1,), (1,)), ((), ())),
        precision=HIGH,
        preferred_element_type=jnp.float32,
    )
    half = gram.shape[0] // 2
    quarters = (gram[:half, :half], gram[half:, :half], gram[half:, half:])
    return jnp.concatenate([fold(quarter) for quarter in quarters], axis=0)


def inverse_factor(packed, ridge):
    width = packed.shape[1]
    size = width // 2
    upper, lower_left, lower = (unfold(packed[i : i + 8, :]) for i in (0, 8, 16))
    filler = jnp.zeros((size // 2, size), jnp.float32)
    state = jnp.concatenate(
        [
            jnp.concatenate([upper, lower_left.T, filler], axis=1),
            jnp.concatenate([lower_left, lower, filler], axis=1),
        ],
        axis=0,
    )
    row_id = lax.broadcasted_iota(jnp.int32, state.shape, 0)
    lane_id = lax.broadcasted_iota(jnp.int32, state.shape, 1)
    state = jnp.where(lane_id < size, state, jnp.where(lane_id - size == row_id, 1.0, 0.0))
    if ridge:
        on_diagonal = lane_id == row_id
        trace = jnp.sum(jnp.where(on_diagonal, state, 0.0))
        state = jnp.where(on_diagonal, state + trace * (RIDGE / size), state)
    done = []
    for start in range(0, size, 8):
        columns = [
            jnp.broadcast_to(state[:, start + j : start + j + 1], state.shape) for j in range(8)
        ]
        row_id = lax.broadcasted_iota(jnp.int32, state.shape, 0)
        scale = jnp.zeros((8, width), jnp.float32)
        for j in range(8):
            column = columns[j]
            pivot = column[j : j + 1, :]
            scale = jnp.where(row_id[:8] == j, lax.rsqrt(pivot), scale)
            factor = jnp.where(row_id > j, column * (1.0 / pivot), 0.0)
            state = state - factor * state[j : j + 1, :]
            for m in range(j + 1, 8):
                columns[m] = columns[m] - factor * column[m : m + 1, :]
        done.append(state[:8] * scale)
        state = state[8:]
    full = jnp.concatenate(done, axis=0)
    return pltpu.roll(full, size, 1)[:, :size]


def transform(matrix, vectors):
    return jnp.dot(matrix, vectors, precision=HIGH, preferred_element_type=jnp.float32)


def call(kernel, name, out_shape, grant=SMALL):
    return pl.pallas_call(
        kernel,
        out_shape=out_shape,
        compiler_params=pltpu.CompilerParams(vmem_limit_bytes=grant),
        name=name,
    )


def f32(*shape):
    return jax.ShapeDtypeStruct(shape, jnp.float32)


def bf16(*shape):
    return jax.ShapeDtypeStruct(shape, jnp.bfloat16)


def seed_kernel_rows(seeds, block):
    dots = lax.dot_general(
        seeds, block, (((1,), (1,)), ((), ())), preferred_element_type=jnp.float32
    )
    seed_half = jnp.sum(half_squares(seeds), axis=1, keepdims=True)
    return jnp.exp2(dots * LOG2E - seed_half - lane_sums(half_squares(block)))


def start_kernel(seeds, own, start, grams):
    value = seed_kernel_rows(seeds[...], own[...])
    start[...] = value
    grams[...] = jnp.broadcast_to(packed_gram(value)[None], grams.shape)


def first_factor_kernel(grams, start, diagonal, own_degree, factor, subspace, later_gram):
    inverse = inverse_factor(jnp.sum(grams[...], axis=0), False)
    factor[...] = inverse
    value = transform(inverse, start[...])
    subspace[...] = value
    root = lax.rsqrt(own_degree[...])
    product = jnp.dot(
        (value * root).astype(jnp.bfloat16), diagonal[...], preferred_element_type=jnp.float32
    )
    later_gram[...] = packed_gram(product * root)


def later_factor_kernel(gram_rows, factor):
    factor[...] = inverse_factor(gram_rows[:, 0, :], True)


def later_factor(lines, vecs):
    height, width = 3 * vecs // 8, 2 * vecs
    place = lines.shape[2] // width - 1
    return pl.pallas_call(
        later_factor_kernel,
        grid=(1,),
        in_specs=[pl.BlockSpec((height, 1, width), lambda s: (0, 0, place))],
        out_specs=pl.BlockSpec((vecs, vecs), lambda s: (0, 0)),
        out_shape=f32(vecs, vecs),
        compiler_params=pltpu.CompilerParams(vmem_limit_bytes=SMALL),
        name="later_factor",
    )(lines)


def degree_kernel(own_degree, parts, copies, root):
    points = root.shape[1]
    total = jnp.sum(parts[...], axis=0)
    value = lax.rsqrt(total[:, :points] + own_degree[...])
    root[...] = value
    copies[...] = jnp.broadcast_to(
        jnp.concatenate([value, total[:, points:]], axis=1)[None], copies.shape
    )


def gathered(own_part, first_parts, second_part, root):
    total = own_part[...] + second_part[...].astype(jnp.float32)
    for index in range(first_parts.shape[0]):
        total = total + first_parts[index].astype(jnp.float32)
    return total * root[...]


def between_kernel(own_part, first_parts, second_part, root, factor, copies, spread):
    value = transform(factor[...], gathered(own_part, first_parts, second_part, root))
    value = (value * root[...]).astype(jnp.bfloat16)
    spread[...] = value
    copies[...] = jnp.broadcast_to(value[None], copies.shape)


def between(own_part, first_parts, second_part, root, factor):
    copies, vecs, rows = first_parts.shape
    return call(
        between_kernel, "between", [bf16(copies, vecs, rows), bf16(vecs, rows)], VMEM
    )(own_part, first_parts, second_part, root, factor)


def last_kernel(own_part, first_parts, second_part, root, subspace, grams):
    value = gathered(own_part, first_parts, second_part, root)
    subspace[...] = value
    grams[...] = jnp.broadcast_to(packed_gram(value)[None], grams.shape)


def final_kernel(points_all, grams, subspace, embedding):
    inverse = inverse_factor(jnp.sum(grams[...], axis=0), False)
    scaled = transform(inverse, subspace[...]) * math.sqrt(points_all)
    mean = jnp.mean(scaled * scaled, axis=0, keepdims=True)
    embedding[...] = scaled * lax.rsqrt(mean + 1e-06)


def relay_kernel(grams, copies):
    copies[...] = jnp.broadcast_to(jnp.sum(grams[...], axis=0)[None], copies.shape)


def vectors_kernel(slots, lists, block, seeds, factor, *rest):
    out = rest[-1]

    @pl.when(pl.program_id(0) < lists[5 * slots])
    def work():
        rows = block[0] if len(rest) == 1 else weigh(block[0], rest[0])
        out[0] = transform(factor[...], seed_kernel_rows(seeds[...], rows))


def start_vectors(lists, slots, source, band, seeds, factor, *scale):
    unused, rows, depth = band.shape
    vecs = seeds.shape[0]
    return pl.pallas_call(
        functools.partial(vectors_kernel, slots),
        grid_spec=pltpu.PrefetchScalarGridSpec(
            num_scalar_prefetch=1,
            grid=(slots,),
            in_specs=[
                pl.BlockSpec(
                    (1, rows, depth), lambda s, t: (t[source + live_step(s, t, slots)], 0, 0)
                ),
                pl.BlockSpec((vecs, depth), lambda s, t: (0, 0)),
                pl.BlockSpec((vecs, vecs), lambda s, t: (0, 0)),
            ]
            + [pl.BlockSpec(one.shape, lambda s, t: (0, 0)) for one in scale],
            out_specs=pl.BlockSpec(
                (1, vecs, rows), lambda s, t: (live_step(s, t, slots), 0, 0)
            ),
        ),
        out_shape=f32(slots, vecs, rows),
        compiler_params=pltpu.CompilerParams(vmem_limit_bytes=VMEM),
        cost_estimate=pl.CostEstimate(
            flops=4_000_000_000, bytes_accessed=10_000_000, transcendentals=0
        ),
        name="start_vectors",
    )(lists, band, seeds, factor, *scale)


def form_kernel(chunk, slots, lists, left, right, scale, gram, tile, lines):
    step = pl.program_id(0)
    points = left.shape[1]

    @pl.when(step == 0)
    def clear():
        lines[...] = jnp.zeros_like(lines)
        for index in range(gram.shape[0]):
            lines[index, :, points:] = gram[index : index + 1, :]

    @pl.when(step < lists[5 * slots])
    def work():
        rows = left.shape[1]
        right_rows = right[0]
        right_half = lane_sums(half_squares(right_rows))
        col_total = jnp.zeros((1, rows), jnp.float32)
        row_totals = []
        for start in range(0, rows, chunk):
            left_rows = weigh(left[0, start : start + chunk, :], scale)
            value = tile_chunk(left_rows, right_rows, right_half)
            tile[0, start : start + chunk, :] = value.astype(jnp.bfloat16)
            col_total = col_total + jnp.sum(value, axis=0, keepdims=True)
            row_totals.append(lane_sums(value))
        left_owner = lists[3 * slots + 2 * step]
        right_owner = lists[3 * slots + 2 * step + 1]
        row_total = jnp.concatenate(row_totals, axis=1)
        lines[left_owner, :, :points] = lines[left_owner, :, :points] + row_total
        lines[right_owner, :, :points] = lines[right_owner, :, :points] + col_total


def form_tiles(lists, slots, row_band, col_band, scale, gram):
    col_devices, rows, depth = row_band.shape
    line = (col_devices * col_band.shape[0], 1, rows + gram.shape[1])
    firsts, unused, places, owners, live = task_lists(slots)

    return pl.pallas_call(
        functools.partial(form_kernel, min(256, rows), slots),
        grid_spec=pltpu.PrefetchScalarGridSpec(
            num_scalar_prefetch=1,
            grid=(slots,),
            in_specs=[
                pl.BlockSpec(
                    (1, rows, depth), lambda s, t: (t[firsts + live_step(s, t, slots)], 0, 0)
                ),
                pl.BlockSpec(
                    (1, rows, depth), lambda s, t: (t[places + live_step(s, t, slots)], 0, 0)
                ),
                pl.BlockSpec(scale.shape, lambda s, t: (0, 0)),
                pl.BlockSpec(gram.shape, lambda s, t: (0, 0)),
            ],
            out_specs=[
                pl.BlockSpec((1, rows, rows), lambda s, t: (live_step(s, t, slots), 0, 0)),
                pl.BlockSpec(line, lambda s, t: (0, 0, 0)),
            ],
        ),
        out_shape=[bf16(slots, rows, rows), f32(*line)],
        compiler_params=pltpu.CompilerParams(vmem_limit_bytes=VMEM),
        name="form_tiles",
    )(lists, row_band, col_band, scale, gram)


def diagonal_kernel(chunk, own, tile, degree):
    rows = own.shape[0]
    right_rows = own[...]
    right_half = lane_sums(half_squares(right_rows))
    total = jnp.zeros((1, rows), jnp.float32)
    for start in range(0, rows, chunk):
        value = tile_chunk(own[start : start + chunk, :], right_rows, right_half)
        tile[start : start + chunk, :] = value.astype(jnp.bfloat16)
        total = total + jnp.sum(value, axis=0, keepdims=True)
    degree[...] = total


def form_diagonal(own):
    rows = own.shape[0]
    return pl.pallas_call(
        functools.partial(diagonal_kernel, min(256, rows)),
        out_shape=[
            jax.ShapeDtypeStruct((rows, rows), jnp.bfloat16),
            jax.ShapeDtypeStruct((1, rows), jnp.float32),
        ],
        compiler_params=pltpu.CompilerParams(vmem_limit_bytes=SMALL),
        name="form_diagonal",
    )(own)


def apply_kernel(slots, by_slot, lists, tiles, from_first, from_second, *rest):
    count = 5 if by_slot else 3
    lines = rest[0] if by_slot else None
    to_first, to_second = rest[-count - 3 : -count - 1]
    held, semaphores = rest[-count - 1 : -1], rest[-1]
    rows = tiles.shape[1]
    live = lists[5 * slots]

    def copies(step, side):
        first, second = lists[step], lists[slots + step]
        sources = [tiles.at[step]]
        if by_slot:
            sources += [from_first.at[step], from_second.at[step]]
            sources += [lines.at[lists[3 * slots + 2 * step + end]] for end in range(2)]
        else:
            sources += [from_first.at[first], from_second.at[second]]
        return [
            pltpu.make_async_copy(source, held[index].at[side], semaphores.at[index, side])
            for index, source in enumerate(sources)
        ]

    @pl.when(live > 0)
    def begin():
        for copy in copies(0, 0):
            copy.start()

    to_first[...] = jnp.zeros_like(to_first)
    to_second[...] = jnp.zeros_like(to_second)

    def one(step, state):
        side = lax.rem(step, 2)

        @pl.when(step + 1 < live)
        def ahead():
            for copy in copies(step + 1, 1 - side):
                copy.start()

        for copy in copies(step, side):
            copy.wait()

        def vectors(end):
            block = held[1 + end][side]
            if not by_slot:
                return block
            return (block * held[3 + end][side][:, :rows]).astype(jnp.bfloat16)

        def add(out, slot, block, contract):
            product = lax.dot_general(
                block,
                held[0][side],
                (((1,), (contract,)), ((), ())),
                preferred_element_type=jnp.float32,
            )
            out[slot] = (out[slot].astype(jnp.float32) + product).astype(jnp.bfloat16)

        add(to_second, lists[slots + step], vectors(0), 0)
        add(to_first, lists[step], vectors(1), 1)
        return state

    lax.fori_loop(0, live, one, 0)


def apply_tiles(lists, tiles, from_first, from_second, roots, col_devices, row_devices):
    slots, rows, unused = tiles.shape
    vecs = from_first.shape[1]
    by_slot = roots is not None
    operands = [tiles, from_first, from_second] + ([roots] if by_slot else [])
    held = operands + ([roots] if by_slot else [])
    return pl.pallas_call(
        functools.partial(apply_kernel, slots, by_slot),
        in_specs=[pl.BlockSpec(memory_space=pltpu.SMEM)]
        + [pl.BlockSpec(memory_space=pl.ANY)] * len(operands),
        out_specs=[pl.BlockSpec(memory_space=pltpu.VMEM)] * 2,
        out_shape=[bf16(col_devices, vecs, rows), bf16(row_devices, vecs, rows)],
        scratch_shapes=[pltpu.VMEM((2,) + one.shape[1:], one.dtype) for one in held]
        + [pltpu.SemaphoreType.DMA((len(held), 2))],
        compiler_params=pltpu.CompilerParams(vmem_limit_bytes=VMEM),
        name="apply_tiles",
    )(lists, *operands)


def spread_to(array, axis):
    devices = lax.axis_size(axis)
    copies = jnp.broadcast_to(array[None], (devices,) + array.shape)
    return lax.all_to_all(copies, axis, 0, 0, tiled=True)


def exchange(copies, axis):
    return lax.all_to_all(copies, axis, 0, 0, tiled=True)


def together(*arrays):
    return lax.optimization_barrier(arrays)


def place_in_row(index, here):
    apart = (index // 2 - here // 2 + 4) % 4
    order = jnp.where(apart == 0, 0, jnp.where(apart == 3, 1, jnp.where(apart == 1, 2, 3)))
    return order + 4 * ((index + here) % 2)


def assign_kernel(slots, cols, here, table, lists):
    devices = table.shape[1]
    me = here[0]
    filler = jnp.zeros((devices - table.shape[0], devices), jnp.float32)
    by_device = jnp.concatenate([table[...], filler], axis=0).T
    device = lax.broadcasted_iota(jnp.int32, (devices, devices), 0)
    lane = lax.broadcasted_iota(jnp.int32, (devices, devices), 1)
    same = jnp.where(device == lane, 1.0, 0.0)
    count = by_device[:, slots : slots + 1]
    load = jnp.zeros((1, devices), jnp.float32)
    moves = []
    taken = []
    listed = []
    for slot in range(slots):
        partner = by_device[:, slot : slot + 1]
        is_listed = jnp.where(count > slot, 1.0, 0.0)
        picks = jnp.where(lane.astype(jnp.float32) == partner, 1.0, 0.0)
        move = (picks - same) * is_listed
        apart = jnp.sum(move * load, axis=1, keepdims=True)
        take = jnp.where(apart <= 0, is_listed, 0.0)
        load = load + jnp.sum(same * is_listed + move * take, axis=0, keepdims=True)
        moves.append(move)
        taken.append(take)
        listed.append(is_listed)
    for slot in range(slots):
        apart = jnp.sum(moves[slot] * load, axis=1, keepdims=True)
        give = jnp.where(apart < -1, listed[slot] * (1.0 - taken[slot]), 0.0)
        back = jnp.where(apart > 1, taken[slot], 0.0)
        load = load + jnp.sum(moves[slot] * (give - back), axis=0, keepdims=True)
        taken[slot] = taken[slot] + give - back
    shared = jnp.where(jnp.max(load) <= slots, 1.0, 0.0)
    code = jnp.zeros((devices, devices), jnp.float32)
    number = device.astype(jnp.float32)
    for slot in range(slots):
        partner = by_device[:, slot : slot + 1]
        take = taken[slot] * shared
        kept = jnp.where(device == me, listed[slot] - take, 0.0)
        come = jnp.where(partner == me.astype(jnp.float32), take, 0.0)
        other = kept * partner + come * number
        cell = (kept + come) * (number * slots + (slot + 1)) * devices + other
        code = jnp.where(lane == slot, cell, code)
    lists[5 * slots] = jnp.sum(jnp.where(code > 0, 1.0, 0.0)).astype(jnp.int32)
    for slot in range(slots):
        top = jnp.max(code)
        partner = lax.rem(top.astype(jnp.int32), devices)
        code = jnp.where(code == top, 0.0, code)
        first_slot = lax.rem(partner, cols)
        second_slot = lax.div(partner, cols)
        lists[slot] = first_slot
        lists[slots + slot] = second_slot
        lists[2 * slots + slot] = place_in_row(second_slot, lax.div(me, cols))
        lists[3 * slots + 2 * slot] = lax.div(me, cols) * cols + first_slot
        lists[3 * slots + 2 * slot + 1] = second_slot * cols + lax.rem(me, cols)


def assign_tasks(self_index, table, slots, cols):
    smem = pl.BlockSpec(memory_space=pltpu.SMEM)
    return pl.pallas_call(
        functools.partial(assign_kernel, slots, cols),
        in_specs=[smem, pl.BlockSpec(memory_space=pltpu.VMEM)],
        out_specs=smem,
        out_shape=jax.ShapeDtypeStruct((6 * slots,), jnp.int32),
        compiler_params=pltpu.CompilerParams(vmem_limit_bytes=SMALL),
        name="assign_tasks",
    )(self_index.reshape(1), table)


def shards(points, feature_scale, tile_tasks, task_count, seed_ids):
    rows = points.shape[0]
    vecs = seed_ids.shape[0]
    packed = (3 * vecs // 8, 2 * vecs)
    row_devices = lax.axis_size("row")
    col_devices = lax.axis_size("col")
    all_devices = row_devices * col_devices
    self_index = lax.axis_index("row") * col_devices + lax.axis_index("col")
    weighted = (points.astype(jnp.float32) * feature_scale[None, :]).astype(jnp.bfloat16)
    row_band = lax.all_gather(points, "col", axis=0)
    scale = feature_scale[None, :]
    listed = tile_tasks.reshape(-1)
    slots = listed.shape[0]

    def shift(array, by):
        return lax.ppermute(
            array, "row", [(i, (i + by) % row_devices) for i in range(row_devices)]
        )

    local_seed = seed_ids - self_index * rows
    inside = (local_seed >= 0) & (local_seed < rows)
    picked = jnp.where(
        inside[:, None], jnp.take(weighted, jnp.clip(local_seed, 0, rows - 1), axis=0), 0
    ).astype(jnp.bfloat16)
    own_line = jnp.concatenate(
        [listed, task_count.reshape(-1), jnp.zeros((slots - 1,), jnp.int32)]
    )
    lines = jnp.where(
        (jnp.arange(weighted.shape[1]) == self_index)[None, :], own_line[:, None], 0
    ).astype(jnp.bfloat16)
    picked = jnp.concatenate([picked, lines], axis=0)
    seed_parts = spread_to(picked, "row")
    before = shift(weighted, 2)
    after = shift(weighted, -2)
    before, after, seed_parts = together(before, after, seed_parts)
    half = rows // 2
    across_low = shift(before[:half], 2)
    across_high = shift(after[half:], -2)
    seed_parts = spread_to(jnp.sum(seed_parts, axis=0), "col")
    diagonal, own_degree = form_diagonal(weighted)
    seed_sum = jnp.sum(seed_parts, axis=0)
    seeds = seed_sum[:vecs]
    table = seed_sum[vecs:, :all_devices].astype(jnp.float32)
    start, grams = call(
        start_kernel, "start", [f32(vecs, rows), f32(row_devices, *packed)]
    )(seeds, weighted)
    across_low, across_high, grams = together(across_low, across_high, grams)
    grams = exchange(grams, "row")
    across = jnp.concatenate([across_low, across_high], axis=0)
    mine = jnp.stack([weighted, before, after, across])
    mine, grams = together(mine, grams)
    other = lax.ppermute(mine, "row", [(i, i ^ 1) for i in range(row_devices)])
    grams = call(relay_kernel, "relay", f32(col_devices, *packed))(grams)
    grams = exchange(grams, "col")
    lists = assign_tasks(self_index, table, slots, col_devices)
    firsts, seconds, places, unused, unused = task_lists(slots)
    col_band, grams = together(jnp.concatenate([mine, other], axis=0), grams)
    factor, subspace, later_gram = call(
        first_factor_kernel,
        "first_factor",
        [f32(vecs, vecs), f32(vecs, rows), f32(*packed)],
    )(grams, start, diagonal, own_degree)

    tiles, lines = form_tiles(lists, slots, row_band, col_band, scale, later_gram)
    copies, inv_root = call(degree_kernel, "degree", [f32(*lines.shape), f32(1, rows)])(
        own_degree, exchange(lines, ("row", "col"))
    )
    lines = exchange(copies, ("row", "col"))
    roots = lines
    from_first = start_vectors(lists, slots, firsts, row_band, seeds, factor, scale)
    from_second = start_vectors(lists, slots, places, col_band, seeds, factor)
    spread = (subspace * inv_root).astype(jnp.bfloat16)
    for iteration in range(ITERS):
        own_part = lax.dot_general(
            spread, diagonal, (((1,), (0,)), ((), ())), preferred_element_type=jnp.float32
        )
        to_first, to_second = apply_tiles(
            lists, tiles, from_first, from_second, roots, col_devices, row_devices
        )
        second_part = lax.psum_scatter(to_second, "row", scatter_dimension=0, tiled=False)
        first_parts = exchange(to_first, "col")
        if iteration + 1 < ITERS:
            copies, spread = between(
                own_part, first_parts, second_part, inv_root, later_factor(lines, vecs)
            )
            from_second = lax.all_gather(spread, "row", axis=0)
            from_first = exchange(copies, "col")
            roots = None
    subspace, grams = call(
        last_kernel, "last", [f32(vecs, rows), f32(row_devices, *packed)]
    )(own_part, first_parts, second_part, inv_root)
    grams = exchange(grams, "row")
    grams = call(relay_kernel, "relay", f32(col_devices, *packed))(grams)
    grams = exchange(grams, "col")
    return call(
        functools.partial(final_kernel, all_devices * rows), "final", f32(vecs, rows)
    )(grams, subspace).T


def solution(mesh):
    return jax.shard_map(
        shards,
        mesh=mesh,
        in_specs=(P(("row", "col"), None), P(), P("row", "col", None), P("row", "col"), P()),
        out_specs=P(("row", "col"), None),
        check_vma=False,
    )
```

```python
import functools
import math

import jax
import jax.numpy as jnp
from jax import lax
from jax.experimental import pallas as pl
from jax.experimental.pallas import tpu as pltpu
from jax.sharding import PartitionSpec as P

ITERS = 2
LOG2E = math.log2(math.e)
VMEM = 60 * 1024 * 1024
SMALL = 24 * 1024 * 1024
HIGH = lax.Precision.HIGHEST
RIDGE = 1e-5


def weigh(block, scale):
    return (block.astype(jnp.float32) * scale[...]).astype(jnp.bfloat16)


def lane_sums(values):
    part = values[:, :128]
    for start in range(128, values.shape[1], 128):
        part = part + values[:, start : start + 128]
    return jnp.sum(part.T, axis=0, keepdims=True)


def task_lists(slots):
    return 0, slots, 2 * slots, 3 * slots, 5 * slots


def live_step(step, lists, slots):
    return jnp.maximum(jnp.minimum(step, lists[5 * slots] - 1), 0)


def half_squares(rows):
    wide = rows.astype(jnp.float32)
    return wide * wide * (0.5 * LOG2E)


def tile_chunk(left, right, right_half):
    dots = lax.dot_general(
        left, right, (((1,), (1,)), ((), ())), preferred_element_type=jnp.float32
    )
    left_half = jnp.sum(half_squares(left), axis=1, keepdims=True)
    return jnp.exp2(dots * LOG2E - left_half - right_half)


def fold(block):
    return jnp.concatenate([block[i : i + 8, :] for i in range(0, block.shape[0], 8)], axis=1)


def unfold(lines):
    return jnp.concatenate([lines[:, i : i + 32] for i in range(0, lines.shape[1], 32)], axis=0)


def packed_gram(vectors):
    gram = lax.dot_general(
        vectors,
        vectors,
        (((1,), (1,)), ((), ())),
        precision=HIGH,
        preferred_element_type=jnp.float32,
    )
    half = gram.shape[0] // 2
    quarters = (gram[:half, :half], gram[half:, :half], gram[half:, half:])
    return jnp.concatenate([fold(quarter) for quarter in quarters], axis=0)


def inverse_factor(packed, ridge):
    width = packed.shape[1]
    size = width // 2
    upper, lower_left, lower = (unfold(packed[i : i + 8, :]) for i in (0, 8, 16))
    filler = jnp.zeros((size // 2, size), jnp.float32)
    state = jnp.concatenate(
        [
            jnp.concatenate([upper, lower_left.T, filler], axis=1),
            jnp.concatenate([lower_left, lower, filler], axis=1),
        ],
        axis=0,
    )
    row_id = lax.broadcasted_iota(jnp.int32, state.shape, 0)
    lane_id = lax.broadcasted_iota(jnp.int32, state.shape, 1)
    state = jnp.where(lane_id < size, state, jnp.where(lane_id - size == row_id, 1.0, 0.0))
    if ridge:
        on_diagonal = lane_id == row_id
        trace = jnp.sum(jnp.where(on_diagonal, state, 0.0))
        state = jnp.where(on_diagonal, state + trace * (RIDGE / size), state)
    done = []
    for start in range(0, size, 8):
        columns = [
            jnp.broadcast_to(state[:, start + j : start + j + 1], state.shape) for j in range(8)
        ]
        row_id = lax.broadcasted_iota(jnp.int32, state.shape, 0)
        scale = jnp.zeros((8, width), jnp.float32)
        for j in range(8):
            column = columns[j]
            pivot = column[j : j + 1, :]
            scale = jnp.where(row_id[:8] == j, lax.rsqrt(pivot), scale)
            factor = jnp.where(row_id > j, column * (1.0 / pivot), 0.0)
            state = state - factor * state[j : j + 1, :]
            for m in range(j + 1, 8):
                columns[m] = columns[m] - factor * column[m : m + 1, :]
        done.append(state[:8] * scale)
        state = state[8:]
    full = jnp.concatenate(done, axis=0)
    return pltpu.roll(full, size, 1)[:, :size]


def transform(matrix, vectors):
    return jnp.dot(matrix, vectors, precision=HIGH, preferred_element_type=jnp.float32)


def call(kernel, name, out_shape, grant=SMALL):
    return pl.pallas_call(
        kernel,
        out_shape=out_shape,
        compiler_params=pltpu.CompilerParams(vmem_limit_bytes=grant),
        name=name,
    )


def f32(*shape):
    return jax.ShapeDtypeStruct(shape, jnp.float32)


def bf16(*shape):
    return jax.ShapeDtypeStruct(shape, jnp.bfloat16)


def seed_kernel_rows(seeds, block):
    dots = lax.dot_general(
        seeds, block, (((1,), (1,)), ((), ())), preferred_element_type=jnp.float32
    )
    seed_half = jnp.sum(half_squares(seeds), axis=1, keepdims=True)
    return jnp.exp2(dots * LOG2E - seed_half - lane_sums(half_squares(block)))


def start_kernel(seeds, own, start, grams):
    value = seed_kernel_rows(seeds[...], own[...])
    start[...] = value
    grams[...] = jnp.broadcast_to(packed_gram(value)[None], grams.shape)


def first_factor_kernel(grams, start, diagonal, own_degree, factor, subspace, later_gram):
    inverse = inverse_factor(jnp.sum(grams[...], axis=0), False)
    factor[...] = inverse
    value = transform(inverse, start[...])
    subspace[...] = value
    root = lax.rsqrt(own_degree[...])
    product = jnp.dot(
        (value * root).astype(jnp.bfloat16), diagonal[...], preferred_element_type=jnp.float32
    )
    later_gram[...] = packed_gram(product * root)


def later_factor_kernel(gram_rows, factor):
    factor[...] = inverse_factor(gram_rows[:, 0, :], True)


def later_factor(lines, vecs):
    height, width = 3 * vecs // 8, 2 * vecs
    place = lines.shape[2] // width - 1
    return pl.pallas_call(
        later_factor_kernel,
        grid=(1,),
        in_specs=[pl.BlockSpec((height, 1, width), lambda s: (0, 0, place))],
        out_specs=pl.BlockSpec((vecs, vecs), lambda s: (0, 0)),
        out_shape=f32(vecs, vecs),
        compiler_params=pltpu.CompilerParams(vmem_limit_bytes=SMALL),
        name="later_factor",
    )(lines)


def degree_kernel(own_degree, parts, copies, root):
    points = root.shape[1]
    total = jnp.sum(parts[...], axis=0)
    value = lax.rsqrt(total[:, :points] + own_degree[...])
    root[...] = value
    copies[...] = jnp.broadcast_to(
        jnp.concatenate([value, total[:, points:]], axis=1)[None], copies.shape
    )


def gathered(own_part, first_parts, second_part, root):
    total = own_part[...] + second_part[...].astype(jnp.float32)
    for index in range(first_parts.shape[0]):
        total = total + first_parts[index].astype(jnp.float32)
    return total * root[...]


def between_kernel(own_part, first_parts, second_part, root, factor, copies, spread):
    value = transform(factor[...], gathered(own_part, first_parts, second_part, root))
    value = (value * root[...]).astype(jnp.bfloat16)
    spread[...] = value
    copies[...] = jnp.broadcast_to(value[None], copies.shape)


def between(own_part, first_parts, second_part, root, factor):
    copies, vecs, rows = first_parts.shape
    return call(
        between_kernel, "between", [bf16(copies, vecs, rows), bf16(vecs, rows)], VMEM
    )(own_part, first_parts, second_part, root, factor)


def last_kernel(own_part, first_parts, second_part, root, subspace, grams):
    value = gathered(own_part, first_parts, second_part, root)
    subspace[...] = value
    grams[...] = jnp.broadcast_to(packed_gram(value)[None], grams.shape)


def final_kernel(points_all, grams, subspace, embedding):
    inverse = inverse_factor(jnp.sum(grams[...], axis=0), False)
    scaled = transform(inverse, subspace[...]) * math.sqrt(points_all)
    mean = jnp.mean(scaled * scaled, axis=0, keepdims=True)
    embedding[...] = scaled * lax.rsqrt(mean + 1e-06)


def relay_kernel(grams, copies):
    copies[...] = jnp.broadcast_to(jnp.sum(grams[...], axis=0)[None], copies.shape)


def vectors_kernel(slots, lists, block, seeds, factor, *rest):
    out = rest[-1]

    @pl.when(pl.program_id(0) < lists[5 * slots])
    def work():
        rows = block[0] if len(rest) == 1 else weigh(block[0], rest[0])
        out[0] = transform(factor[...], seed_kernel_rows(seeds[...], rows))


def start_vectors(lists, slots, source, band, seeds, factor, *scale):
    unused, rows, depth = band.shape
    vecs = seeds.shape[0]
    return pl.pallas_call(
        functools.partial(vectors_kernel, slots),
        grid_spec=pltpu.PrefetchScalarGridSpec(
            num_scalar_prefetch=1,
            grid=(slots,),
            in_specs=[
                pl.BlockSpec(
                    (1, rows, depth), lambda s, t: (t[source + live_step(s, t, slots)], 0, 0)
                ),
                pl.BlockSpec((vecs, depth), lambda s, t: (0, 0)),
                pl.BlockSpec((vecs, vecs), lambda s, t: (0, 0)),
            ]
            + [pl.BlockSpec(one.shape, lambda s, t: (0, 0)) for one in scale],
            out_specs=pl.BlockSpec(
                (1, vecs, rows), lambda s, t: (live_step(s, t, slots), 0, 0)
            ),
        ),
        out_shape=f32(slots, vecs, rows),
        compiler_params=pltpu.CompilerParams(vmem_limit_bytes=VMEM),
        cost_estimate=pl.CostEstimate(
            flops=4_000_000_000, bytes_accessed=10_000_000, transcendentals=0
        ),
        name="start_vectors",
    )(lists, band, seeds, factor, *scale)


def form_kernel(chunk, slots, lists, left, right, scale, gram, tile, lines):
    step = pl.program_id(0)
    points = left.shape[1]

    @pl.when(step == 0)
    def clear():
        lines[...] = jnp.zeros_like(lines)
        for index in range(gram.shape[0]):
            lines[index, :, points:] = gram[index : index + 1, :]

    @pl.when(step < lists[5 * slots])
    def work():
        rows = left.shape[1]
        right_rows = right[0]
        right_half = lane_sums(half_squares(right_rows))
        col_total = jnp.zeros((1, rows), jnp.float32)
        row_totals = []
        for start in range(0, rows, chunk):
            left_rows = weigh(left[0, start : start + chunk, :], scale)
            value = tile_chunk(left_rows, right_rows, right_half)
            tile[0, start : start + chunk, :] = value.astype(jnp.bfloat16)
            col_total = col_total + jnp.sum(value, axis=0, keepdims=True)
            row_totals.append(lane_sums(value))
        left_owner = lists[3 * slots + 2 * step]
        right_owner = lists[3 * slots + 2 * step + 1]
        row_total = jnp.concatenate(row_totals, axis=1)
        lines[left_owner, :, :points] = lines[left_owner, :, :points] + row_total
        lines[right_owner, :, :points] = lines[right_owner, :, :points] + col_total


def form_tiles(lists, slots, row_band, col_band, scale, gram):
    col_devices, rows, depth = row_band.shape
    line = (col_devices * col_band.shape[0], 1, rows + gram.shape[1])
    firsts, unused, places, owners, live = task_lists(slots)

    return pl.pallas_call(
        functools.partial(form_kernel, min(256, rows), slots),
        grid_spec=pltpu.PrefetchScalarGridSpec(
            num_scalar_prefetch=1,
            grid=(slots,),
            in_specs=[
                pl.BlockSpec(
                    (1, rows, depth), lambda s, t: (t[firsts + live_step(s, t, slots)], 0, 0)
                ),
                pl.BlockSpec(
                    (1, rows, depth), lambda s, t: (t[places + live_step(s, t, slots)], 0, 0)
                ),
                pl.BlockSpec(scale.shape, lambda s, t: (0, 0)),
                pl.BlockSpec(gram.shape, lambda s, t: (0, 0)),
            ],
            out_specs=[
                pl.BlockSpec((1, rows, rows), lambda s, t: (live_step(s, t, slots), 0, 0)),
                pl.BlockSpec(line, lambda s, t: (0, 0, 0)),
            ],
        ),
        out_shape=[bf16(slots, rows, rows), f32(*line)],
        compiler_params=pltpu.CompilerParams(vmem_limit_bytes=VMEM),
        name="form_tiles",
    )(lists, row_band, col_band, scale, gram)


def diagonal_kernel(chunk, own, tile, degree):
    rows = own.shape[0]
    right_rows = own[...]
    right_half = lane_sums(half_squares(right_rows))
    total = jnp.zeros((1, rows), jnp.float32)
    for start in range(0, rows, chunk):
        value = tile_chunk(own[start : start + chunk, :], right_rows, right_half)
        tile[start : start + chunk, :] = value.astype(jnp.bfloat16)
        total = total + jnp.sum(value, axis=0, keepdims=True)
    degree[...] = total


def form_diagonal(own):
    rows = own.shape[0]
    return pl.pallas_call(
        functools.partial(diagonal_kernel, min(256, rows)),
        out_shape=[
            jax.ShapeDtypeStruct((rows, rows), jnp.bfloat16),
            jax.ShapeDtypeStruct((1, rows), jnp.float32),
        ],
        compiler_params=pltpu.CompilerParams(vmem_limit_bytes=SMALL),
        name="form_diagonal",
    )(own)


def apply_kernel(slots, by_slot, lists, tiles, from_first, from_second, *rest):
    count = 5 if by_slot else 3
    lines = rest[0] if by_slot else None
    to_first, to_second = rest[-count - 3 : -count - 1]
    held, semaphores = rest[-count - 1 : -1], rest[-1]
    rows = tiles.shape[1]
    live = lists[5 * slots]
    half = rows // 2

    def copies(step, side):
        first, second = lists[step], lists[slots + step]
        sources = [tiles.at[step, pl.ds(start, half)] for start in (0, half)]
        targets = [held[0].at[side, pl.ds(start, half)] for start in (0, half)]
        targets += [one.at[side] for one in held[1:]]
        if by_slot:
            sources += [from_first.at[step], from_second.at[step]]
            sources += [lines.at[lists[3 * slots + 2 * step + end]] for end in range(2)]
        else:
            sources += [from_first.at[first], from_second.at[second]]
        return [
            pltpu.make_async_copy(source, target, semaphores.at[index, side])
            for index, (source, target) in enumerate(zip(sources, targets))
        ]

    @pl.when(live > 0)
    def begin():
        for copy in copies(0, 0):
            copy.start()

    to_first[...] = jnp.zeros_like(to_first)
    to_second[...] = jnp.zeros_like(to_second)

    def one(step, state):
        side = lax.rem(step, 2)

        @pl.when(step + 1 < live)
        def ahead():
            for copy in copies(step + 1, 1 - side):
                copy.start()

        upper, lower, *others = copies(step, side)
        for copy in (upper, *others):
            copy.wait()

        def vectors(end):
            block = held[1 + end][side]
            if not by_slot:
                return block
            return (block * held[3 + end][side][:, :rows]).astype(jnp.bfloat16)

        def product(block, tile, contract):
            return lax.dot_general(
                block, tile, (((1,), (contract,)), ((), ())), preferred_element_type=jnp.float32
            )

        def add(out, slot, value):
            out[slot] = (out[slot].astype(jnp.float32) + value).astype(jnp.bfloat16)

        left = vectors(0)
        value = product(left[:, :half], held[0][side, :half, :], 0)
        lower.wait()
        value = value + product(left[:, half:], held[0][side, half:, :], 0)
        add(to_second, lists[slots + step], value)
        add(to_first, lists[step], product(vectors(1), held[0][side], 1))
        return state

    lax.fori_loop(0, live, one, 0)


def apply_tiles(lists, tiles, from_first, from_second, roots, col_devices, row_devices):
    slots, rows, unused = tiles.shape
    vecs = from_first.shape[1]
    by_slot = roots is not None
    operands = [tiles, from_first, from_second] + ([roots] if by_slot else [])
    held = operands + ([roots] if by_slot else [])
    return pl.pallas_call(
        functools.partial(apply_kernel, slots, by_slot),
        in_specs=[pl.BlockSpec(memory_space=pltpu.SMEM)]
        + [pl.BlockSpec(memory_space=pl.ANY)] * len(operands),
        out_specs=[pl.BlockSpec(memory_space=pltpu.VMEM)] * 2,
        out_shape=[bf16(col_devices, vecs, rows), bf16(row_devices, vecs, rows)],
        scratch_shapes=[pltpu.VMEM((2,) + one.shape[1:], one.dtype) for one in held]
        + [pltpu.SemaphoreType.DMA((len(held) + 1, 2))],
        compiler_params=pltpu.CompilerParams(vmem_limit_bytes=VMEM),
        name="apply_tiles",
    )(lists, *operands)


def spread_to(array, axis):
    devices = lax.axis_size(axis)
    copies = jnp.broadcast_to(array[None], (devices,) + array.shape)
    return lax.all_to_all(copies, axis, 0, 0, tiled=True)


def exchange(copies, axis):
    return lax.all_to_all(copies, axis, 0, 0, tiled=True)


def together(*arrays):
    return lax.optimization_barrier(arrays)


def place_in_row(index, here):
    apart = (index // 2 - here // 2 + 4) % 4
    order = jnp.where(apart == 0, 0, jnp.where(apart == 3, 1, jnp.where(apart == 1, 2, 3)))
    return order + 4 * ((index + here) % 2)


def assign_kernel(slots, cols, here, table, lists):
    devices = table.shape[1]
    me = here[0]
    filler = jnp.zeros((devices - table.shape[0], devices), jnp.float32)
    by_device = jnp.concatenate([table[...], filler], axis=0).T
    device = lax.broadcasted_iota(jnp.int32, (devices, devices), 0)
    lane = lax.broadcasted_iota(jnp.int32, (devices, devices), 1)
    same = jnp.where(device == lane, 1.0, 0.0)
    count = by_device[:, slots : slots + 1]
    load = jnp.zeros((1, devices), jnp.float32)
    moves = []
    taken = []
    listed = []
    for slot in range(slots):
        partner = by_device[:, slot : slot + 1]
        is_listed = jnp.where(count > slot, 1.0, 0.0)
        picks = jnp.where(lane.astype(jnp.float32) == partner, 1.0, 0.0)
        move = (picks - same) * is_listed
        apart = jnp.sum(move * load, axis=1, keepdims=True)
        take = jnp.where(apart <= 0, is_listed, 0.0)
        load = load + jnp.sum(same * is_listed + move * take, axis=0, keepdims=True)
        moves.append(move)
        taken.append(take)
        listed.append(is_listed)
    for slot in range(slots):
        apart = jnp.sum(moves[slot] * load, axis=1, keepdims=True)
        give = jnp.where(apart < -1, listed[slot] * (1.0 - taken[slot]), 0.0)
        back = jnp.where(apart > 1, taken[slot], 0.0)
        load = load + jnp.sum(moves[slot] * (give - back), axis=0, keepdims=True)
        taken[slot] = taken[slot] + give - back
    shared = jnp.where(jnp.max(load) <= slots, 1.0, 0.0)
    code = jnp.zeros((devices, devices), jnp.float32)
    number = device.astype(jnp.float32)
    for slot in range(slots):
        partner = by_device[:, slot : slot + 1]
        take = taken[slot] * shared
        kept = jnp.where(device == me, listed[slot] - take, 0.0)
        come = jnp.where(partner == me.astype(jnp.float32), take, 0.0)
        other = kept * partner + come * number
        cell = (kept + come) * (number * slots + (slot + 1)) * devices + other
        code = jnp.where(lane == slot, cell, code)
    lists[5 * slots] = jnp.sum(jnp.where(code > 0, 1.0, 0.0)).astype(jnp.int32)
    for slot in range(slots):
        top = jnp.max(code)
        partner = lax.rem(top.astype(jnp.int32), devices)
        code = jnp.where(code == top, 0.0, code)
        first_slot = lax.rem(partner, cols)
        second_slot = lax.div(partner, cols)
        lists[slot] = first_slot
        lists[slots + slot] = second_slot
        lists[2 * slots + slot] = place_in_row(second_slot, lax.div(me, cols))
        lists[3 * slots + 2 * slot] = lax.div(me, cols) * cols + first_slot
        lists[3 * slots + 2 * slot + 1] = second_slot * cols + lax.rem(me, cols)


def assign_tasks(self_index, table, slots, cols):
    smem = pl.BlockSpec(memory_space=pltpu.SMEM)
    return pl.pallas_call(
        functools.partial(assign_kernel, slots, cols),
        in_specs=[smem, pl.BlockSpec(memory_space=pltpu.VMEM)],
        out_specs=smem,
        out_shape=jax.ShapeDtypeStruct((6 * slots,), jnp.int32),
        compiler_params=pltpu.CompilerParams(vmem_limit_bytes=SMALL),
        name="assign_tasks",
    )(self_index.reshape(1), table)


def shards(points, feature_scale, tile_tasks, task_count, seed_ids):
    rows = points.shape[0]
    vecs = seed_ids.shape[0]
    packed = (3 * vecs // 8, 2 * vecs)
    row_devices = lax.axis_size("row")
    col_devices = lax.axis_size("col")
    all_devices = row_devices * col_devices
    self_index = lax.axis_index("row") * col_devices + lax.axis_index("col")
    weighted = (points.astype(jnp.float32) * feature_scale[None, :]).astype(jnp.bfloat16)
    row_band = lax.all_gather(points, "col", axis=0)
    scale = feature_scale[None, :]
    listed = tile_tasks.reshape(-1)
    slots = listed.shape[0]

    def shift(array, by):
        return lax.ppermute(
            array, "row", [(i, (i + by) % row_devices) for i in range(row_devices)]
        )

    local_seed = seed_ids - self_index * rows
    inside = (local_seed >= 0) & (local_seed < rows)
    picked = jnp.where(
        inside[:, None], jnp.take(weighted, jnp.clip(local_seed, 0, rows - 1), axis=0), 0
    ).astype(jnp.bfloat16)
    own_line = jnp.concatenate(
        [listed, task_count.reshape(-1), jnp.zeros((slots - 1,), jnp.int32)]
    )
    lines = jnp.where(
        (jnp.arange(weighted.shape[1]) == self_index)[None, :], own_line[:, None], 0
    ).astype(jnp.bfloat16)
    picked = jnp.concatenate([picked, lines], axis=0)
    seed_parts = spread_to(picked, "row")
    before = shift(weighted, 2)
    after = shift(weighted, -2)
    before, after, seed_parts = together(before, after, seed_parts)
    half = rows // 2
    across_low = shift(before[:half], 2)
    across_high = shift(after[half:], -2)
    seed_parts = spread_to(jnp.sum(seed_parts, axis=0), "col")
    diagonal, own_degree = form_diagonal(weighted)
    seed_sum = jnp.sum(seed_parts, axis=0)
    seeds = seed_sum[:vecs]
    table = seed_sum[vecs:, :all_devices].astype(jnp.float32)
    start, grams = call(
        start_kernel, "start", [f32(vecs, rows), f32(row_devices, *packed)]
    )(seeds, weighted)
    across_low, across_high, grams = together(across_low, across_high, grams)
    grams = exchange(grams, "row")
    across = jnp.concatenate([across_low, across_high], axis=0)
    mine = jnp.stack([weighted, before, after, across])
    mine, grams = together(mine, grams)
    other = lax.ppermute(mine, "row", [(i, i ^ 1) for i in range(row_devices)])
    grams = call(relay_kernel, "relay", f32(col_devices, *packed))(grams)
    grams = exchange(grams, "col")
    lists = assign_tasks(self_index, table, slots, col_devices)
    firsts, seconds, places, unused, unused = task_lists(slots)
    col_band, grams = together(jnp.concatenate([mine, other], axis=0), grams)
    factor, subspace, later_gram = call(
        first_factor_kernel,
        "first_factor",
        [f32(vecs, vecs), f32(vecs, rows), f32(*packed)],
    )(grams, start, diagonal, own_degree)

    tiles, lines = form_tiles(lists, slots, row_band, col_band, scale, later_gram)
    copies, inv_root = call(degree_kernel, "degree", [f32(*lines.shape), f32(1, rows)])(
        own_degree, exchange(lines, ("row", "col"))
    )
    lines = exchange(copies, ("row", "col"))
    roots = lines
    from_first = start_vectors(lists, slots, firsts, row_band, seeds, factor, scale)
    from_second = start_vectors(lists, slots, places, col_band, seeds, factor)
    spread = (subspace * inv_root).astype(jnp.bfloat16)
    for iteration in range(ITERS):
        own_part = lax.dot_general(
            spread, diagonal, (((1,), (0,)), ((), ())), preferred_element_type=jnp.float32
        )
        to_first, to_second = apply_tiles(
            lists, tiles, from_first, from_second, roots, col_devices, row_devices
        )
        second_part = lax.psum_scatter(to_second, "row", scatter_dimension=0, tiled=False)
        first_parts = exchange(to_first, "col")
        if iteration + 1 < ITERS:
            copies, spread = between(
                own_part, first_parts, second_part, inv_root, later_factor(lines, vecs)
            )
            from_second = lax.all_gather(spread, "row", axis=0)
            from_first = exchange(copies, "col")
            roots = None
    subspace, grams = call(
        last_kernel, "last", [f32(vecs, rows), f32(row_devices, *packed)]
    )(own_part, first_parts, second_part, inv_root)
    grams = exchange(grams, "row")
    grams = call(relay_kernel, "relay", f32(col_devices, *packed))(grams)
    grams = exchange(grams, "col")
    return call(
        functools.partial(final_kernel, all_devices * rows), "final", f32(vecs, rows)
    )(grams, subspace).T


def solution(mesh):
    return jax.shard_map(
        shards,
        mesh=mesh,
        in_specs=(P(("row", "col"), None), P(), P("row", "col", None), P("row", "col"), P()),
        out_specs=P(("row", "col"), None),
        check_vma=False,
    )
```
